32 devices in a mesh: grp: 2 (over y), seq: 4 (over z), head: 4 (over x, core).
Axes of the slice: x: 2, y: 2, z: 4, core: 2. Of those that a mesh axis runs over, the one named last changes fastest.
Arguments:
- q_heads: bfloat16 [8, 64, 16384], P('head', None, ('grp', 'seq')), parts along dimension 2, may hold values from -12 to 12
- k_heads: bfloat16 [8, 64, 16384], P('head', None, ('grp', 'seq')), parts along dimension 2, may hold values from -10 to 10
- v_heads: bfloat16 [8, 64, 16384], P('head', None, ('grp', 'seq')), parts along dimension 2, may hold values from -10 to 10
- morton_order: int32 [8, 2048], P(('grp', 'seq')), parts along dimension 0, may hold values from 0 to 2047, each once within a row
- leaf_counts: int32 [64], P('grp'), parts along dimension 0, may hold values from 64 to 256, as said below
Outputs:
- attended: bfloat16 [8, 64, 16384], P('head', None, ('grp', 'seq')), parts along dimension 2
The draws below stay inside these ranges and needn't reach their ends.
There are 2 independent parts, one for each index of `grp`. The reference program is written for one: setup_inputs(seed, part) draws one part's arguments, and reference() takes and returns one part's arrays. A program takes and returns all parts, laid end to end along the dimension named above; each array names one. Nothing has to cross between parts.
Inputs may be any that keep to these rules, and one draw needn't show every extreme that they name: `morton_order`: each row holds every number of 0 .. 2047 once. `leaf_counts`: the valid points of a leaf are its first ones.
All inputs are finite; a program needn't handle non-finite values.
Results may differ from the reference program's by a relative error of at most 0.0021.
Values may be sent and summed in bfloat16 or wider, within the bound.
A program may use at most 64 MiB of HBM per device.

```python
import math
import jax
import jax.numpy as jnp
from jax import lax

HEADS = 8
HEAD_SIZE = 64
LEAF_POINTS = 256
TOK_DEV = 2048
TOKENS = 8192
BLOCKS = 4


def multiscale(key):
    leaves = TOKENS // LEAF_POINTS
    scale_count = leaves.bit_length()
    field = jnp.zeros((HEADS, HEAD_SIZE, TOKENS), jnp.float32)
    for level_index in range(scale_count):
        pieces = max(leaves >> level_index, 1)
        coarse = jax.random.normal(jax.random.fold_in(key, 100 + level_index), (HEADS, HEAD_SIZE, pieces), jnp.float32)
        field = field + jnp.repeat(coarse, TOKENS // pieces, axis=2)
    return field / math.sqrt(scale_count)


def draw_q_heads(key, part):
    shape = (HEADS, HEAD_SIZE, TOKENS)
    smooth = multiscale(jax.random.fold_in(key, 15))
    rough = jax.random.normal(jax.random.fold_in(key, 13), shape, jnp.float32)
    values = 1.4 * rough + 0.9 * smooth
    return jnp.clip(values, -12.0, 12.0).astype(jnp.bfloat16)


def draw_k_heads(key, part):
    shape = (HEADS, HEAD_SIZE, TOKENS)
    smooth = multiscale(jax.random.fold_in(key, 16))
    rough = jax.random.normal(jax.random.fold_in(key, 12), shape, jnp.float32)
    values = 1.4 * rough + 0.9 * smooth
    return jnp.clip(values, -10.0, 10.0).astype(jnp.bfloat16)


def draw_v_heads(key, part):
    shape = (HEADS, HEAD_SIZE, TOKENS)
    smooth = multiscale(jax.random.fold_in(key, 32))
    rough = jax.random.normal(jax.random.fold_in(key, 31), shape, jnp.float32)
    values = 1.5 * rough + 1.5 * smooth
    return jnp.clip(values, -10.0, 10.0).astype(jnp.bfloat16)


def draw_leaf_counts(key, part):
    raw_counts = jax.random.randint(jax.random.fold_in(key, 41), (TOKENS // LEAF_POINTS,), LEAF_POINTS // 4, 2 * LEAF_POINTS, jnp.int32)
    return jnp.minimum(raw_counts, LEAF_POINTS).astype(jnp.int32)


def setup_inputs(seed: int = 0, part: int = 0) -> dict:
    streams_of = jax.random.split(jax.random.key(seed), 6)
    own_keys = jax.random.split(jax.random.fold_in(streams_of[5], part), 6)
    return {
        "q_heads": draw_q_heads(jax.random.fold_in(jax.random.fold_in(streams_of[5], part), 71), part),
        "k_heads": draw_k_heads(jax.random.fold_in(jax.random.fold_in(streams_of[5], part), 71), part),
        "v_heads": draw_v_heads(jax.random.fold_in(jax.random.fold_in(streams_of[5], part), 71), part),
        "morton_order": jax.vmap(lambda own: jax.random.permutation(own, TOK_DEV))(jax.random.split(own_keys[3], BLOCKS)).reshape((BLOCKS, TOK_DEV)).astype(jnp.int32),
        "leaf_counts": draw_leaf_counts(jax.random.fold_in(jax.random.fold_in(streams_of[5], part), 71), part),
    }


NEG_FILL = -1e+30

def valid_points(leaf_counts):
    slots = jnp.arange(LEAF_POINTS, dtype=jnp.int32)
    return (slots[None, :] < leaf_counts[:, None]).astype(jnp.float32).reshape(-1)

def pooled(values, group_len):
    new_shape = values.shape[:-1] + (values.shape[-1] // group_len, group_len)
    return lax.optimization_barrier(jnp.sum(values.reshape(new_shape), axis=-1, dtype=jnp.float32))

def sibling_rows(values, block_rows):
    new_shape = values.shape[:-1] + (values.shape[-1] // (2 * block_rows), 2, block_rows)
    return jnp.flip(values.reshape(new_shape), axis=-2).reshape(values.shape)

def near_field(query_rows, key_rows, value_rows, valid):
    leaves = TOKENS // LEAF_POINTS
    scale_multiplier = 1.0 / math.sqrt(HEAD_SIZE)
    key_pad = jnp.pad(key_rows, ((0, 0), (LEAF_POINTS, LEAF_POINTS))).reshape(HEAD_SIZE, leaves + 2, LEAF_POINTS)
    value_pad = jnp.pad(value_rows, ((0, 0), (LEAF_POINTS, LEAF_POINTS))).reshape(HEAD_SIZE, leaves + 2, LEAF_POINTS)
    valid_pad = jnp.pad(valid, (LEAF_POINTS, LEAF_POINTS)).reshape(leaves + 2, LEAF_POINTS)
    key_win = jnp.concatenate([key_pad[:, offset:offset + leaves] for offset in range(3)], axis=-1)
    value_win = jnp.concatenate([value_pad[:, offset:offset + leaves] for offset in range(3)], axis=-1)
    valid_win = jnp.concatenate([valid_pad[offset:offset + leaves] for offset in range(3)], axis=-1)
    group = math.gcd(leaves, 64)
    batches = leaves // group
    query_grp = jnp.moveaxis(query_rows.reshape(HEAD_SIZE, batches, group, LEAF_POINTS), 1, 0)
    key_grp = jnp.moveaxis(key_win.reshape(HEAD_SIZE, batches, group, 3 * LEAF_POINTS), 1, 0)
    value_grp = jnp.moveaxis(value_win.reshape(HEAD_SIZE, batches, group, 3 * LEAF_POINTS), 1, 0)
    valid_grp = valid_win.reshape(batches, group, 3 * LEAF_POINTS)

    def one_batch(pieces):
        query_piece, key_piece, value_piece, mask_piece = pieces
        logit_scores = jnp.einsum('dnq,dnk->nqk', query_piece.astype(jnp.float32), key_piece.astype(jnp.float32)) * scale_multiplier
        logit_scores = jnp.where(mask_piece[:, None, :] > 0, logit_scores, NEG_FILL)
        best_score = lax.optimization_barrier(jnp.max(logit_scores, axis=-1))
        weight_probs = jnp.exp(logit_scores - best_score[..., None])
        weight_sum = lax.optimization_barrier(jnp.sum(weight_probs, axis=-1))
        probabilities = weight_probs.astype(jnp.bfloat16)
        blended_sum = jnp.einsum('nqk,dnk->dnq', probabilities.astype(jnp.float32), value_piece.astype(jnp.float32))
        return (best_score, blended_sum, weight_sum)
    best_all, mixed_all, total_all = lax.map(one_batch, (query_grp, key_grp, value_grp, valid_grp))
    mixed_all = jnp.moveaxis(mixed_all, 0, 1).reshape(HEAD_SIZE, TOKENS)
    return (best_all.reshape(-1), mixed_all, total_all.reshape(-1))

def far_field(query_rows, key_rows, value_rows, valid, level_index):
    group_len = 2 ** level_index
    scale_multiplier = 1.0 / math.sqrt(HEAD_SIZE)
    mean_query = pooled(query_rows.astype(jnp.float32), group_len) / group_len
    key_sums = pooled(key_rows.astype(jnp.float32) * valid, group_len)
    value_sums = pooled(value_rows.astype(jnp.float32) * valid, group_len)
    masses = pooled(valid, group_len)
    block_groups = TOKENS // (group_len * LEAF_POINTS)
    far_mass = sibling_rows(masses, LEAF_POINTS)
    mean_keys = sibling_rows(key_sums, LEAF_POINTS) / jnp.maximum(far_mass, 1.0)
    distant_values = sibling_rows(value_sums, LEAF_POINTS)
    mass_rows = far_mass.reshape(block_groups, LEAF_POINTS)
    logit_scores = jnp.einsum('swj,swg->wjg', mean_query.reshape(HEAD_SIZE, block_groups, LEAF_POINTS), mean_keys.reshape(HEAD_SIZE, block_groups, LEAF_POINTS), precision=lax.Precision.HIGHEST) * scale_multiplier
    logit_scores = jnp.where(mass_rows[:, None, :] > 0, logit_scores, NEG_FILL)
    best_score = lax.optimization_barrier(jnp.max(logit_scores, axis=-1))
    weight_probs = jnp.exp(logit_scores - best_score[..., None])
    weight_sum = lax.optimization_barrier(jnp.sum(weight_probs * mass_rows[:, None, :], axis=-1))
    blended_sum = jnp.einsum('rto,pro->prt', weight_probs, distant_values.reshape(HEAD_SIZE, block_groups, LEAF_POINTS), precision=lax.Precision.HIGHEST)
    return (best_score.reshape(-1), blended_sum.reshape(HEAD_SIZE, -1), weight_sum.reshape(-1))

def reference(q_heads, k_heads, v_heads, morton_order, leaf_counts):
    offsets = (jnp.arange(morton_order.shape[0], dtype=jnp.int32) * TOK_DEV)[:, None]
    gather_index = (morton_order + offsets).reshape(-1).astype(jnp.int32)
    query_all = jnp.take(q_heads, gather_index, axis=2)
    key_all = jnp.take(k_heads, gather_index, axis=2)
    value_all = jnp.take(v_heads, gather_index, axis=2)
    valid = valid_points(leaf_counts)
    depth_all = (TOKENS // LEAF_POINTS).bit_length() - 1

    def one_head(pieces):
        query_rows, key_rows, value_rows = pieces
        near_best, near_mixed, near_total = near_field(query_rows, key_rows, value_rows, valid)
        far_terms = []
        for level_index in range(1, depth_all):
            far_terms.append((2 ** level_index, far_field(query_rows, key_rows, value_rows, valid, level_index)))
        best_score = near_best
        for group_len, term in far_terms:
            best_score = jnp.maximum(best_score, jnp.repeat(term[0], group_len))
        factor = jnp.exp(near_best - best_score)
        blended_sum = near_mixed * factor[None, :]
        weight_sum = near_total * factor
        for group_len, term in far_terms:
            factor = jnp.exp(jnp.repeat(term[0], group_len) - best_score)
            blended_sum = blended_sum + jnp.repeat(term[1], group_len, axis=-1) * factor[None, :]
            weight_sum = weight_sum + jnp.repeat(term[2], group_len) * factor
        return (blended_sum / weight_sum[None, :]).astype(jnp.bfloat16)
    return lax.map(one_head, (query_all, key_all, value_all))
```

```python
import functools
import math

import jax
import jax.numpy as jnp
from jax import lax
from jax.experimental import pallas as pl
from jax.experimental.pallas import tpu as pltpu
from jax.sharding import PartitionSpec as P

LEAF = 256
LANES = 128
NEG = -1e30
BF = jnp.bfloat16
F32 = jnp.float32
I32 = jnp.int32
I16 = jnp.int16
PAD = 16
BOUND = 10.0
STEPS = 32700.0
VMEM_LIMIT = 63 * 1024 * 1024 + 512 * 1024


def dot(a, b, dims=((1,), (0,))):
    return lax.dot_general(a, b, (dims, ((), ())), preferred_element_type=F32)


def split(x):
    hi = x.astype(BF)
    return hi, (x - hi.astype(F32)).astype(BF)


def iota(shape, dim):
    return lax.broadcasted_iota(I32, shape, dim)


def fixed(x, bound):
    return jnp.floor(x * (STEPS / bound) + 0.5).astype(I32).astype(I16)


def unfixed(x, bound):
    return x.astype(I32).astype(F32) * (bound / STEPS)


def plan(tokens, seq_count):
    leaves = tokens // LEAF
    depth_local = leaves.bit_length() - 1
    depth_all = (leaves * seq_count).bit_length() - 1
    levels = list(range(1, depth_all))
    near_levels = [l for l in levels if l < depth_local]
    far_levels = [l for l in levels if l >= depth_local]
    return leaves, depth_local, near_levels, far_levels


def padded(tokens, level):
    return max(LANES, tokens >> level)


def kernel(cfg, *refs):
    heads, width, tokens, seq_count = cfg
    rows = heads * width
    leaves, depth_local, near_levels, far_levels = plan(tokens, seq_count)
    pairs = leaves // 2
    scale = math.log2(math.e) / math.sqrt(width)
    size = width + PAD
    refs = list(refs)
    take = lambda n: [refs.pop(0) for _ in range(n)]
    q_hbm, k_hbm, v_hbm, order_hbm, counts_hbm, out = take(6)
    order, counts = take(2)
    xin, ka, kb, vx, qx, xp, kv = take(7)
    w1, w3, ua, uu = take(4)
    qf, kmf, vvf, fo, fb = take(5)
    pf = take(1)[0]
    ss, sb, num, stat, zb = take(5)
    per_far = lambda: dict(zip(far_levels, take(len(far_levels))))
    kf, qr, kmr2, vvr2, for_, fbr = (per_far() for _ in range(6))
    kmp, vvp, kmr, vvr = (per_far() for _ in range(4))
    in_sem, halo_send, halo_recv = take(3)
    far_send, far_recv = per_far(), per_far()
    us = dict(zip([l for l in far_levels if (LEAF >> l) < 8], refs))

    seq = lax.axis_index("seq")
    has_left, has_right = seq > 0, seq < seq_count - 1

    loads = [
        pltpu.make_async_copy(src, xin.at[pl.ds(i * rows, rows)], in_sem.at[i])
        for i, src in enumerate((q_hbm, k_hbm, v_hbm))
    ]
    loads.append(pltpu.make_async_copy(order_hbm, order, in_sem.at[3]))
    loads.append(pltpu.make_async_copy(counts_hbm, counts, in_sem.at[4]))
    for load in loads:
        load.start()
    barrier = pltpu.get_barrier_semaphore()
    for step in range(1, seq_count):
        other = lax.rem(seq + step, seq_count)
        pl.semaphore_signal(
            barrier, inc=1, device_id={"seq": other}, device_id_type=pl.DeviceIdType.MESH
        )

    @pl.when(jnp.logical_not(has_left))
    def _():
        ka[0:LEAF, :] = jnp.zeros((LEAF, rows), BF)
        vx[:, 0:LEAF] = jnp.zeros((rows, LEAF), BF)

    @pl.when(jnp.logical_not(has_right))
    def _():
        ka[tokens + LEAF :, :] = jnp.zeros((LEAF, rows), BF)
        vx[:, tokens + LEAF :] = jnp.zeros((rows, LEAF), BF)

    def count_of(n):
        leaf = seq * leaves + n
        total = leaves * seq_count
        inside = jnp.logical_and(leaf >= 0, leaf < total)
        return jnp.where(inside, counts[jnp.clip(leaf, 0, total - 1)], 0)

    def ones_where(mask):
        return jnp.where(mask, 1.0, 0.0).astype(BF)

    t = iota((LEAF, LEAF), 0)
    c = iota((LEAF, LEAF), 1)
    for p in range(2):
        w1[p] = ones_where(
            jnp.logical_or(
                jnp.logical_and(c < LANES, (t >> 1) == c),
                jnp.logical_and(c >= LANES, (t >> 2) + 64 * p == c - LANES),
            )
        )
    uu[...] = ones_where((c >> 1) == (t & (LANES - 1)))
    for i, level in enumerate(far_levels):
        t2 = iota((2 * LEAF, LANES), 0)
        c2 = iota((2 * LEAF, LANES), 1)
        for m in range(pairs):
            w3[m, :, i * LANES : (i + 1) * LANES] = ones_where(
                ((t2 + 2 * LEAF * m) >> level) & (LANES - 1) == c2
            )
    ua_levels, ua_at, at = [l for l in near_levels + far_levels if (LEAF >> l) >= 8], {}, 0
    for level in ua_levels:
        n = LEAF >> level
        ua_at[level] = at
        if n % 16 == 0:
            ua[at : at + n, :] = ones_where((iota((n, LEAF), 1) >> level) == iota((n, LEAF), 0))
        else:
            ua[at : at + 16, :] = ones_where((iota((16, LEAF), 1) >> level) == iota((16, LEAF), 0))
        at += max(n, 16)
    for level, u in us.items():
        u[...] = ones_where((iota(u.shape, 1) >> level) == iota(u.shape, 0))

    def tail_rows(cols):
        r = iota((64, cols), 0)
        return ones_where(r == 0)

    for h in range(heads):
        off = (1 - h) * width
        qx[h, off : off + width, :] = jnp.zeros((width, tokens), BF)
        qx[h, 3 * width :, :] = tail_rows(tokens)
        for i in range(qf.shape[0]):
            qf[i, h, 3 * width :, :] = tail_rows(LEAF)
        for level in far_levels:
            qr[level][h, 3 * width :, :] = tail_rows(qr[level].shape[2])

    for load in loads:
        load.wait()

    lane_lo = iota((LEAF, LANES), 1) < width
    lane_is = iota((LEAF, LANES), 1) == width

    def key_tail(key_t, bias):
        shape = key_t.shape
        lo = iota(shape, 1) < width
        at = iota(shape, 1) == width
        rest = jnp.where(at, bias, 0.0)
        rolled = pltpu.roll(key_t, width, 1)
        return jnp.where(lo, key_t, rest), jnp.where(lo, rolled, rest), rolled

    def leaf_bias(count):
        return jnp.where(iota((LEAF, LANES), 0) < count, 0.0, NEG)

    def permute(m):
        for p in range(2):
            n = 2 * m + p
            at = pl.multiple_of(n * LEAF, LEAF)
            picks = order[0:1, pl.ds(at, LEAF)]
            spots = iota((tokens, LEAF), 0)
            hot = jnp.where(spots == picks, 1.0, 0.0).astype(BF)
            moved = dot(xin[...], hot)
            count = count_of(n)
            query, key, value = moved[:rows], moved[rows : 2 * rows], moved[2 * rows :]
            key_t = key.T
            on_row = iota((rows, LEAF), 1) < count
            on_col = iota((LEAF, rows), 0) < count
            tail0, tail1, rolled = key_tail(key_t, leaf_bias(count))
            ka[pl.ds(at + LEAF, LEAF), :] = key_t.astype(BF)
            kb[0, pl.ds(at + LEAF, LEAF), :] = tail0.astype(BF)
            kb[1, pl.ds(at + LEAF, LEAF), :] = tail1.astype(BF)
            kv[pl.ds(at, LEAF), 0:rows] = jnp.where(on_col, key_t, 0.0).astype(BF)
            kv[pl.ds(at, LEAF), rows:] = jnp.where(on_col, rolled, 0.0).astype(BF)
            vx[:, pl.ds(at + LEAF, LEAF)] = value.astype(BF)
            xp[0:rows, pl.ds(at, LEAF)] = query.astype(BF)
            xp[rows : 2 * rows, pl.ds(at, LEAF)] = jnp.where(on_row, value, 0.0).astype(BF)
            xp[2 * rows :, pl.ds(at, LEAF)] = ones_where(on_row[:PAD])
            hi, lo = split(query * scale)
            for h in range(heads):
                part = slice(h * width, (h + 1) * width)
                qx[h, part, pl.ds(at, LEAF)] = hi[part]
                qx[h, 2 * width : 3 * width, pl.ds(at, LEAF)] = lo[part]

    def put_query(ref, x, factor, where):
        hi, lo = split(x * factor)
        for h in range(heads):
            part = slice(h * width, (h + 1) * width)
            ref[h, 0:width, where] = hi[part]
            ref[h, width : 2 * width, where] = hi[part]
            ref[h, 2 * width : 3 * width, where] = lo[part]

    def put_value(ref, x, mass, where):
        hi, lo = split(x)
        for h in range(heads):
            part = slice(h * width, (h + 1) * width)
            ref[h, 0:width, where] = hi[part]
            ref[h, width:size, where] = mass.astype(BF)
            ref[h, size:, where] = lo[part]

    def put_key(ref, a, b, bias, where):
        lo_lane = iota(a.shape, 1) < width
        bias_lane = iota(a.shape, 1) == width
        a_hi, b_hi = a.astype(BF).astype(F32), b.astype(BF).astype(F32)
        rest = jnp.where(bias_lane, bias, 0.0)
        ref[0, where, 0:rows] = jnp.where(lo_lane, a_hi, b - b_hi).astype(BF)
        ref[0, where, rows:] = jnp.where(lo_lane, a_hi, rest).astype(BF)
        ref[1, where, 0:rows] = jnp.where(lo_lane, b_hi, a - a_hi).astype(BF)
        ref[1, where, rows:] = jnp.where(lo_lane, b_hi, rest).astype(BF)

    def clip_mass(count, at, g):
        return jnp.clip(count - at, 0, g).astype(F32)

    base_of, first = {}, 0
    for level in near_levels:
        base_of[level] = first
        first += leaves >> level

    def pool(m):
        start = pl.multiple_of(m * 2 * LEAF, 2 * LEAF)
        t1, kk = [], []
        for p in range(2):
            at = pl.multiple_of(start + p * LEAF, LEAF)
            t1.append(dot(xp[0 : 2 * rows, pl.ds(at, LEAF)], w1[p]))
            kk.append(dot(ua[...], kv[pl.ds(at, LEAF), :]))
        if far_levels:
            pf[m] = dot(xp[:, pl.ds(start, 2 * LEAF)], w3[m])
        n = [count_of(2 * m), count_of(2 * m + 1)]
        b1 = base_of[1] + m
        lane = iota((PAD, LANES), 1)
        for p in range(2):
            where = slice(p * LANES, (p + 1) * LANES)
            put_query(qf.at[b1], t1[p][:rows, :LANES], scale / 2, where)
            put_value(vvf.at[b1], t1[p][rows:, :LANES], clip_mass(n[p], lane << 1, 2), where)
        if 2 in near_levels:
            b2 = base_of[2] + m // 2
            x2 = t1[0][:, LANES:] + t1[1][:, LANES:]
            where = pl.ds(pl.multiple_of((m % 2) * LANES, LANES), LANES)
            mass = jnp.where(
                lane < 64, clip_mass(n[0], lane << 2, 4), clip_mass(n[1], (lane - 64) << 2, 4)
            )
            put_query(qf.at[b2], x2[:rows], scale / 4, where)
            put_value(vvf.at[b2], x2[rows:], mass, where)
        for p in range(2):
            for level in ua_levels:
                count = LEAF >> level
                x = kk[p][ua_at[level] : ua_at[level] + count]
                mass = clip_mass(n[p], iota((count, LANES), 0) << level, 1 << level)
                inverse = 1.0 / jnp.maximum(mass, 1.0)
                a = x[:, :rows] * inverse
                if level in near_levels:
                    b = x[:, rows:] * inverse
                    bias = jnp.where(mass > 0, 0.0, NEG)
                    if level == 1:
                        put_key(kmf.at[b1], a, b, bias, slice(p * count, (p + 1) * count))
                    else:
                        spot = pl.multiple_of((m % 2) * LANES + p * count, count)
                        put_key(kmf.at[b2], a, b, bias, pl.ds(spot, count))
                else:
                    spot = pl.multiple_of((2 * m + p) * count, count)
                    kf[level][pl.ds(spot, count), :] = a

    def remote(src, dst, send, recv, target):
        return pltpu.make_async_remote_copy(
            src_ref=src,
            dst_ref=dst,
            send_sem=send,
            recv_sem=recv,
            device_id={"seq": target},
            device_id_type=pl.DeviceIdType.MESH,
        )

    def halo(side):
        start, end = (LEAF, tokens + LEAF) if side == 0 else (tokens, 0)
        target = jnp.maximum(seq - 1, 0) if side == 0 else jnp.minimum(seq + 1, seq_count - 1)
        return (
            remote(
                ka.at[pl.ds(start, LEAF)],
                ka.at[pl.ds(end, LEAF)],
                halo_send.at[2 * side],
                halo_recv.at[2 * side],
                target,
            ),
            remote(
                vx.at[:, pl.ds(start, LEAF)],
                vx.at[:, pl.ds(end, LEAF)],
                halo_send.at[2 * side + 1],
                halo_recv.at[2 * side + 1],
                target,
            ),
        )

    def pair_at(i):
        return jnp.where(i == 0, 0, jnp.where(i == 1, pairs - 1, i - 1))

    permute(0)

    @pl.loop(1, pairs)
    def _(i):
        pool(pair_at(i - 1))
        permute(pair_at(i))

        @pl.when(i == 1)
        def _():
            pl.semaphore_wait(barrier, seq_count - 1)

        @pl.when(jnp.logical_and(i == 1, has_left))
        def _():
            for copy in halo(0):
                copy.start()

        @pl.when(jnp.logical_and(i == 1, has_right))
        def _():
            for copy in halo(1):
                copy.start()

    pool(pair_at(pairs - 1))

    def far_copies(level):
        bit = level - depth_local
        nb = 1 << bit
        part = tokens >> level
        slot = lax.rem(seq, nb)
        base = ((seq >> bit) ^ 1) << bit
        copies = []
        for j in range(nb):
            target = base + j
            copies.append(
                remote(
                    kmp[level],
                    kmr[level].at[pl.ds(pl.multiple_of(slot * part, part), part)],
                    far_send[level].at[2 * j],
                    far_recv[level].at[2 * slot],
                    target,
                )
            )
            copies.append(
                remote(
                    vvp[level],
                    vvr[level].at[slot],
                    far_send[level].at[2 * j + 1],
                    far_recv[level].at[2 * slot + 1],
                    target,
                )
            )
        return copies

    for i, level in enumerate(far_levels):
        part = tokens >> level
        pieces = part // LANES
        per = pairs // max(pieces, 1)
        cols = slice(i * LANES, (i + 1) * LANES)
        for j in range(max(pieces, 1)):
            x = sum(pf[j * per + e, :, cols] for e in range(per))
            where = slice(j * LANES, (j + 1) * LANES)
            put_query(qr[level], x[:rows], scale / 2**level, where)
            kept = min(LANES, part)
            where = slice(j * kept, (j + 1) * kept)
            vvp[level][0:rows, where] = fixed(x[rows : 2 * rows, :kept], BOUND * 2**level)
            vvp[level][rows:, where] = x[2 * rows :, :kept].astype(I32).astype(I16)
        if level in us:
            sums = dot(us[level][...], kv[:, 0:rows])
            valid = jnp.broadcast_to(xp[2 * rows : 2 * rows + 1, :], (LANES, tokens))
            mass = dot(us[level][...], valid, ((1,), (1,)))
            mean = sums / jnp.maximum(mass, 1.0)
        else:
            mean = kf[level][...]
        kmp[level][...] = fixed(mean, BOUND)
        for copy in far_copies(level):
            copy.start()

    def far_score(km, q, slot, h, best_ref):
        s = dot(km, q)
        keys, cols = s.shape
        ss[slot, h, 0:keys, 0:cols] = s
        best = jnp.max(s.reshape(keys // 8, 8, cols), axis=0)
        best = jnp.max(best, axis=0, keepdims=True).astype(BF).astype(F32)
        best_ref[h] = jnp.broadcast_to(best, (8, cols))

    def far_soft(vvs, slot, h, best_ref, out_ref):
        cols = best_ref.shape[2]
        best = best_ref[h]
        step, acc = 0, None
        for vv in vvs:
            keys = vv.shape[1]
            x = ss[slot, h, step : step + keys, 0:cols].reshape(keys // 8, 8, cols)
            w = jnp.exp2(x - best[None]).reshape(keys, cols)
            w_hi, w_lo = split(w)
            both = dot(vv, w_hi)
            low = jnp.concatenate([both[size:], jnp.zeros((PAD, cols), F32)], axis=0)
            term = both[:size] + low + dot(vv[:size], w_lo)
            acc = term if acc is None else acc + term
            step += keys
        out_ref[h] = acc

    def local_score(i, slot, h):
        far_score(kmf[i ^ 1, h], qf[i, h], slot, h, fb.at[i])

    def local_soft(i, slot, h):
        far_soft([vvf[i ^ 1, h]], slot, h, fb.at[i], fo.at[i])

    for h in range(heads):
        local_score(0, 0, h)

    @pl.loop(0, first // 2)
    def _(b):
        for j in range(2):
            i = 2 * b + j
            for h in range(heads):
                local_soft(i, j, h)
                local_score(jnp.minimum(i + 1, first - 1), 1 - j, h)

    @pl.when(has_right)
    def _():
        for copy in halo(0):
            copy.wait_recv()

    @pl.when(has_left)
    def _():
        for copy in halo(1):
            copy.wait_recv()

    for n, at in ((-1, 0), (leaves, tokens + LEAF)):
        tail0, tail1, _ = key_tail(ka[at : at + LEAF, :].astype(F32), leaf_bias(count_of(n)))
        kb[0, at : at + LEAF, :] = tail0.astype(BF)
        kb[1, at : at + LEAF, :] = tail1.astype(BF)

    def near_score(n, slot, h):
        at = pl.multiple_of(n * LEAF, LEAF)
        best = None
        for j in range(3):
            key_rows = pl.ds(pl.multiple_of(at + j * LEAF, LEAF), LEAF)
            left = jnp.concatenate([ka[key_rows, :], kb[h, key_rows, :]], axis=1)
            s = dot(left, qx[h, :, pl.ds(at, LEAF)])
            ss[slot, h, j * LEAF : (j + 1) * LEAF, :] = s
            top = jnp.max(s.reshape(LEAF // 8, 8, LEAF), axis=0)
            best = top if best is None else jnp.maximum(best, top)
        sb[slot, h] = jnp.broadcast_to(jnp.max(best, axis=0, keepdims=True), (8, LEAF))

    def near_soft(n, slot, h):
        at = pl.multiple_of(n * LEAF, LEAF)
        best = sb[slot, h]
        total, acc = None, None
        part = slice(h * width, (h + 1) * width)
        for j in range(3):
            x = ss[slot, h, j * LEAF : (j + 1) * LEAF, :].reshape(LEAF // 8, 8, LEAF)
            w = jnp.exp2(x - best[None])
            term = jnp.sum(w, axis=0)
            total = term if total is None else total + term
            keys = pl.ds(pl.multiple_of(at + j * LEAF, LEAF), LEAF)
            term = dot(vx[part, keys], w.reshape(LEAF, LEAF).astype(BF))
            acc = term if acc is None else acc + term
        num[part, pl.ds(at, LEAF)] = acc
        stat[2 * h : 2 * h + 1, pl.ds(at, LEAF)] = best[0:1]
        stat[2 * h + 1 : 2 * h + 2, pl.ds(at, LEAF)] = jnp.sum(total, axis=0, keepdims=True)

    for h in range(heads):
        near_score(0, 0, h)

    @pl.loop(0, leaves // 4)
    def _(i):
        for j in range(4):
            n = 4 * i + j
            for h in range(heads):
                near_soft(n, j % 2, h)
                near_score(jnp.minimum(n + 1, leaves - 1), 1 - j % 2, h)

    for slot, level in enumerate(far_levels):
        nb = 1 << (level - depth_local)
        part = tokens >> level
        for i in range(nb):
            remote(
                kmp[level], kmr[level].at[pl.ds(i * part, part)],
                far_send[level].at[2 * i], far_recv[level].at[2 * i], seq,
            ).wait_recv()
            remote(
                vvp[level], vvr[level].at[i],
                far_send[level].at[2 * i + 1], far_recv[level].at[2 * i + 1], seq,
            ).wait_recv()
        ones = jnp.ones((PAD, LANES), BF)
        masses = []
        for i in range(nb):
            mass = vvr[level][i, rows:].astype(I32).astype(F32)
            masses.append(dot(mass.astype(BF), ones, ((0,), (0,))))
            put_value(vvr2[level].at[i], unfixed(vvr[level][i, 0:rows], BOUND * 2**level), mass, slice(0, part))
        bias = jnp.where(jnp.concatenate(masses, axis=0) > 0, 0.0, NEG)
        mean = unfixed(kmr[level][...], BOUND)
        put_key(kmr2[level], mean, pltpu.roll(mean, width, 1), bias, slice(0, LEAF))
        for h in range(heads):
            far_score(kmr2[level][h], qr[level][h], slot % 2, h, fbr[level])
        for h in range(heads):
            far_soft([vvr2[level][i, h] for i in range(nb)], slot % 2, h, fbr[level], for_[level])

    def up(z):
        return dot(jnp.concatenate(split(z), axis=1), uu[...])

    def with_best(acc, best):
        return jnp.concatenate([acc[: size - 8], jnp.broadcast_to(best, (8, acc.shape[1]))], axis=0)

    def merge(acc, best, z):
        old = z[size - 8 : size - 7]
        new = jnp.maximum(best, old)
        both = acc * jnp.exp2(best - new) + z * jnp.exp2(old - new)
        return with_best(both, new)

    for h in range(heads):
        z = None
        for level in reversed(far_levels):
            acc, best = for_[level][h], fbr[level][h, 0:1]
            if z is None:
                z = with_best(acc, best)
            else:
                z = jnp.concatenate(
                    [up(z[:, j * LANES : (j + 1) * LANES]) for j in range(z.shape[1] // LANES)], axis=1
                )[:, : acc.shape[1]]
                z = merge(acc, best, z)
        if z is not None:
            for j in range(z.shape[1] // LANES):
                zb[h, j] = z[:, j * LANES : (j + 1) * LANES]
        for level in reversed(near_levels):
            for i in reversed(range(leaves >> level)):
                block = base_of[level] + i
                acc, best = fo[block, h], fb[block, h, 0:1]
                if z is None:
                    x = with_best(acc, best)
                else:
                    x = merge(acc, best, up(zb[h, i]))
                zb[h, 2 * i] = x[:, :LANES]
                zb[h, 2 * i + 1] = x[:, LANES:]
            z = True
        for n in range(leaves):
            cols = slice(n * LEAF, (n + 1) * LEAF)
            part = slice(h * width, (h + 1) * width)
            near_best, near_total = stat[2 * h : 2 * h + 1, cols], stat[2 * h + 1 : 2 * h + 2, cols]
            z = up(zb[h, n])
            old = z[size - 8 : size - 7]
            new = jnp.maximum(near_best, old)
            mine, other = jnp.exp2(near_best - new), jnp.exp2(old - new)
            inverse = 1.0 / (near_total * mine + z[width : width + 1] * other)
            out[part, cols] = (num[part, cols] * (mine * inverse) + z[:width] * (other * inverse)).astype(BF)

    @pl.when(has_left)
    def _():
        for copy in halo(0):
            copy.wait_send()

    @pl.when(has_right)
    def _():
        for copy in halo(1):
            copy.wait_send()

    for level in far_levels:
        for copy in far_copies(level):
            copy.wait_send()


def shards(q_heads, k_heads, v_heads, morton_order, leaf_counts):
    heads_real, width, tokens = q_heads.shape
    heads = heads_real + heads_real % 2
    seq_count = lax.axis_size("seq")
    rows = heads * width
    flat = []
    for x in (q_heads, k_heads, v_heads):
        if heads != heads_real:
            x = jnp.concatenate([x, jnp.zeros_like(x[:1])], axis=0)
        flat.append(x.reshape(rows, tokens))
    leaves, depth_local, near_levels, far_levels = plan(tokens, seq_count)
    size = width + PAD
    near_blocks = sum(leaves >> l for l in near_levels)
    ua_rows = sum(max(LEAF >> l, 16) for l in near_levels + far_levels if (LEAF >> l) >= 8)
    vm = pltpu.VMEM
    scratch = [
        vm(morton_order.shape, I32),
        pltpu.SMEM(leaf_counts.shape, I32),
        vm((3 * rows, tokens), BF),
        vm((tokens + 2 * LEAF, rows), BF),
        vm((heads, tokens + 2 * LEAF, LANES), BF),
        vm((rows, tokens + 2 * LEAF), BF),
        vm((heads, 4 * width, tokens), BF),
        vm((2 * rows + PAD, tokens), BF),
        vm((tokens, 2 * rows), BF),
        vm((2, LEAF, LEAF), BF),
        vm((leaves // 2, 2 * LEAF, LANES * len(far_levels)), BF),
        vm((ua_rows, LEAF), BF),
        vm((LEAF, LEAF), BF),
        vm((near_blocks, heads, 4 * width, LEAF), BF),
        vm((near_blocks, heads, LEAF, 2 * rows), BF),
        vm((near_blocks, heads, size + width, LEAF), BF),
        vm((near_blocks, heads, size, LEAF), F32),
        vm((near_blocks, heads, 8, LEAF), F32),
        vm((leaves // 2, 2 * rows + PAD, LANES * len(far_levels)), F32),
        vm((2, heads, 3 * LEAF, LEAF), F32),
        vm((2, heads, 8, LEAF), F32),
        vm((rows, tokens), F32),
        vm((2 * heads + (-2 * heads) % 8, tokens), F32),
        vm((heads, leaves, size, LANES), F32),
    ]
    scratch += [vm((tokens >> l, rows), F32) for l in far_levels]
    scratch += [vm((heads, 4 * width, padded(tokens, l)), BF) for l in far_levels]
    scratch += [vm((heads, LEAF, 2 * rows), BF) for l in far_levels]
    scratch += [vm((1 << (l - depth_local), heads, size + width, tokens >> l), BF) for l in far_levels]
    scratch += [vm((heads, size, padded(tokens, l)), F32) for l in far_levels]
    scratch += [vm((heads, 8, padded(tokens, l)), F32) for l in far_levels]
    scratch += [vm((tokens >> l, rows), I16) for l in far_levels]
    scratch += [vm((rows + PAD, tokens >> l), I16) for l in far_levels]
    scratch += [vm((LEAF, rows), I16) for l in far_levels]
    scratch += [vm((1 << (l - depth_local), rows + PAD, tokens >> l), I16) for l in far_levels]
    sem = pltpu.SemaphoreType.DMA
    scratch += [sem((5,)), sem((4,)), sem((4,))]
    scratch += [sem((2 << (l - depth_local),)) for l in far_levels] * 2
    scratch += [vm((tokens >> l, tokens), BF) for l in far_levels if (LEAF >> l) < 8]
    out = pl.pallas_call(
        functools.partial(kernel, (heads, width, tokens, seq_count)),
        out_shape=jax.ShapeDtypeStruct((rows, tokens), BF),
        in_specs=[pl.BlockSpec(memory_space=pltpu.HBM)] * 5,
        out_specs=pl.BlockSpec(memory_space=pltpu.VMEM),
        scratch_shapes=scratch,
        compiler_params=pltpu.CompilerParams(
            collective_id=0, has_side_effects=True, vmem_limit_bytes=VMEM_LIMIT
        ),
    )(*flat, morton_order, leaf_counts)
    return out.reshape(heads, width, tokens)[:heads_real]


def solution(mesh):
    placed = (
        P("head", None, ("grp", "seq")),
        P("head", None, ("grp", "seq")),
        P("head", None, ("grp", "seq")),
        P(("grp", "seq"), None),
        P("grp"),
    )
    return jax.shard_map(
        shards,
        mesh=mesh,
        in_specs=placed,
        out_specs=P("head", None, ("grp", "seq")),
        check_vma=False,
    )
```

```python
import functools
import math

import jax
import jax.numpy as jnp
from jax import lax
from jax.experimental import pallas as pl
from jax.experimental.pallas import tpu as pltpu
from jax.sharding import PartitionSpec as P

LEAF = 256
LANES = 128
NEG = -1e30
BF = jnp.bfloat16
F32 = jnp.float32
I32 = jnp.int32
I16 = jnp.int16
PAD = 16
BOUND = 10.0
STEPS = 32700.0
VMEM_LIMIT = 63488 * 1024


def dot(a, b, dims=((1,), (0,))):
    return lax.dot_general(a, b, (dims, ((), ())), preferred_element_type=F32)


def split(x):
    hi = x.astype(BF)
    return hi, (x - hi.astype(F32)).astype(BF)


def iota(shape, dim):
    return lax.broadcasted_iota(I32, shape, dim)


def fixed(x, bound):
    return jnp.floor(x * (STEPS / bound) + 0.5).astype(I32).astype(I16)


def unfixed(x, bound):
    return x.astype(I32).astype(F32) * (bound / STEPS)


def plan(tokens, seq_count):
    leaves = tokens // LEAF
    depth_local = leaves.bit_length() - 1
    depth_all = (leaves * seq_count).bit_length() - 1
    levels = list(range(1, depth_all))
    near_levels = [l for l in levels if l < depth_local]
    far_levels = [l for l in levels if l >= depth_local]
    return leaves, depth_local, near_levels, far_levels


def padded(tokens, level):
    return max(LANES, tokens >> level)


def kernel(cfg, *refs):
    heads, width, tokens, seq_count = cfg
    rows = heads * width
    leaves, depth_local, near_levels, far_levels = plan(tokens, seq_count)
    pairs = leaves // 2
    scale = math.log2(math.e) / math.sqrt(width)
    size = width + PAD
    refs = list(refs)
    take = lambda n: [refs.pop(0) for _ in range(n)]
    q_hbm, k_hbm, v_hbm, order_hbm, counts_hbm, out = take(6)
    order, counts = take(2)
    xin, ka, kb, vx, qx, xp, kv = take(7)
    w1, w3, ua, uu = take(4)
    qf, kmf, vvf, fo, fb = take(5)
    pf = take(1)[0]
    ss, sb, num, stat, zb = take(5)
    per_far = lambda: dict(zip(far_levels, take(len(far_levels))))
    kf, qr, kmr2, vvr2, for_, fbr = (per_far() for _ in range(6))
    kmp, vvp, kmr, vvr = (per_far() for _ in range(4))
    in_sem, halo_send, halo_recv = take(3)
    far_send, far_recv = per_far(), per_far()
    us = dict(zip([l for l in far_levels if (LEAF >> l) < 8], refs))

    seq = lax.axis_index("seq")
    has_left, has_right = seq > 0, seq < seq_count - 1

    loads = [
        pltpu.make_async_copy(src, xin.at[pl.ds(i * rows, rows)], in_sem.at[i])
        for i, src in enumerate((q_hbm, k_hbm, v_hbm))
    ]
    loads.append(pltpu.make_async_copy(order_hbm, order, in_sem.at[3]))
    loads.append(pltpu.make_async_copy(counts_hbm, counts, in_sem.at[4]))
    for load in loads:
        load.start()
    barrier = pltpu.get_barrier_semaphore()
    for step in range(1, seq_count):
        other = lax.rem(seq + step, seq_count)
        pl.semaphore_signal(
            barrier, inc=1, device_id={"seq": other}, device_id_type=pl.DeviceIdType.MESH
        )

    @pl.when(jnp.logical_not(has_left))
    def _():
        ka[0:LEAF, :] = jnp.zeros((LEAF, rows), BF)
        vx[:, 0:LEAF] = jnp.zeros((rows, LEAF), BF)

    @pl.when(jnp.logical_not(has_right))
    def _():
        ka[tokens + LEAF :, :] = jnp.zeros((LEAF, rows), BF)
        vx[:, tokens + LEAF :] = jnp.zeros((rows, LEAF), BF)

    def count_of(n):
        leaf = seq * leaves + n
        total = leaves * seq_count
        inside = jnp.logical_and(leaf >= 0, leaf < total)
        return jnp.where(inside, counts[jnp.clip(leaf, 0, total - 1)], 0)

    def ones_where(mask):
        return jnp.where(mask, 1.0, 0.0).astype(BF)

    t = iota((LEAF, LEAF), 0)
    c = iota((LEAF, LEAF), 1)
    for p in range(2):
        w1[p] = ones_where(
            jnp.logical_or(
                jnp.logical_and(c < LANES, (t >> 1) == c),
                jnp.logical_and(c >= LANES, (t >> 2) + 64 * p == c - LANES),
            )
        )
    uu[...] = ones_where((c >> 1) == (t & (LANES - 1)))
    for i, level in enumerate(far_levels):
        t2 = iota((2 * LEAF, LANES), 0)
        c2 = iota((2 * LEAF, LANES), 1)
        for m in range(pairs):
            w3[m, :, i * LANES : (i + 1) * LANES] = ones_where(
                ((t2 + 2 * LEAF * m) >> level) & (LANES - 1) == c2
            )
    ua_levels, ua_at, at = [l for l in near_levels + far_levels if (LEAF >> l) >= 8], {}, 0
    for level in ua_levels:
        n = LEAF >> level
        ua_at[level] = at
        if n % 16 == 0:
            ua[at : at + n, :] = ones_where((iota((n, LEAF), 1) >> level) == iota((n, LEAF), 0))
        else:
            ua[at : at + 16, :] = ones_where((iota((16, LEAF), 1) >> level) == iota((16, LEAF), 0))
        at += max(n, 16)
    for level, u in us.items():
        u[...] = ones_where((iota(u.shape, 1) >> level) == iota(u.shape, 0))

    def tail_rows(cols):
        r = iota((64, cols), 0)
        return ones_where(r == 0)

    for h in range(heads):
        off = (1 - h) * width
        qx[h, off : off + width, :] = jnp.zeros((width, tokens), BF)
        qx[h, 3 * width :, :] = tail_rows(tokens)
        for i in range(qf.shape[0]):
            qf[i, h, 3 * width :, :] = tail_rows(LEAF)
        for level in far_levels:
            qr[level][h, 3 * width :, :] = tail_rows(qr[level].shape[2])

    for load in loads:
        load.wait()

    lane_lo = iota((LEAF, LANES), 1) < width
    lane_is = iota((LEAF, LANES), 1) == width

    def key_tail(key_t, bias):
        shape = key_t.shape
        lo = iota(shape, 1) < width
        at = iota(shape, 1) == width
        rest = jnp.where(at, bias, 0.0)
        rolled = pltpu.roll(key_t, width, 1)
        return jnp.where(lo, key_t, rest), jnp.where(lo, rolled, rest), rolled

    def leaf_bias(count):
        return jnp.where(iota((LEAF, LANES), 0) < count, 0.0, NEG)

    def permute(m):
        for p in range(2):
            n = 2 * m + p
            at = pl.multiple_of(n * LEAF, LEAF)
            picks = order[0:1, pl.ds(at, LEAF)]
            spots = iota((tokens, LEAF), 0)
            hot = jnp.where(spots == picks, 1.0, 0.0).astype(BF)
            moved = dot(xin[...], hot)
            count = count_of(n)
            query, key, value = moved[:rows], moved[rows : 2 * rows], moved[2 * rows :]
            key_t = key.T
            on_row = iota((rows, LEAF), 1) < count
            on_col = iota((LEAF, rows), 0) < count
            tail0, tail1, rolled = key_tail(key_t, leaf_bias(count))
            ka[pl.ds(at + LEAF, LEAF), :] = key_t.astype(BF)
            kb[0, pl.ds(at + LEAF, LEAF), :] = tail0.astype(BF)
            kb[1, pl.ds(at + LEAF, LEAF), :] = tail1.astype(BF)
            kv[pl.ds(at, LEAF), 0:rows] = jnp.where(on_col, key_t, 0.0).astype(BF)
            kv[pl.ds(at, LEAF), rows:] = jnp.where(on_col, rolled, 0.0).astype(BF)
            vx[:, pl.ds(at + LEAF, LEAF)] = value.astype(BF)
            xp[0:rows, pl.ds(at, LEAF)] = query.astype(BF)
            xp[rows : 2 * rows, pl.ds(at, LEAF)] = jnp.where(on_row, value, 0.0).astype(BF)
            xp[2 * rows :, pl.ds(at, LEAF)] = ones_where(on_row[:PAD])
            hi, lo = split(query * scale)
            for h in range(heads):
                part = slice(h * width, (h + 1) * width)
                qx[h, part, pl.ds(at, LEAF)] = hi[part]
                qx[h, 2 * width : 3 * width, pl.ds(at, LEAF)] = lo[part]

    def put_query(ref, x, factor, where):
        hi, lo = split(x * factor)
        for h in range(heads):
            part = slice(h * width, (h + 1) * width)
            ref[h, 0:width, where] = hi[part]
            ref[h, width : 2 * width, where] = hi[part]
            ref[h, 2 * width : 3 * width, where] = lo[part]

    def put_value(ref, x, mass, where):
        hi, lo = split(x)
        for h in range(heads):
            part = slice(h * width, (h + 1) * width)
            ref[h, 0:width, where] = hi[part]
            ref[h, width:size, where] = mass.astype(BF)
            ref[h, size:, where] = lo[part]

    def put_key(ref, a, b, bias, where):
        lo_lane = iota(a.shape, 1) < width
        bias_lane = iota(a.shape, 1) == width
        a_hi, b_hi = a.astype(BF).astype(F32), b.astype(BF).astype(F32)
        rest = jnp.where(bias_lane, bias, 0.0)
        ref[0, where, 0:rows] = jnp.where(lo_lane, a_hi, b - b_hi).astype(BF)
        ref[0, where, rows:] = jnp.where(lo_lane, a_hi, rest).astype(BF)
        ref[1, where, 0:rows] = jnp.where(lo_lane, b_hi, a - a_hi).astype(BF)
        ref[1, where, rows:] = jnp.where(lo_lane, b_hi, rest).astype(BF)

    def clip_mass(count, at, g):
        return jnp.clip(count - at, 0, g).astype(F32)

    base_of, first = {}, 0
    for level in near_levels:
        base_of[level] = first
        first += leaves >> level

    def pool(m):
        start = pl.multiple_of(m * 2 * LEAF, 2 * LEAF)
        t1, kk = [], []
        for p in range(2):
            at = pl.multiple_of(start + p * LEAF, LEAF)
            t1.append(dot(xp[0 : 2 * rows, pl.ds(at, LEAF)], w1[p]))
            kk.append(dot(ua[...], kv[pl.ds(at, LEAF), :]))
        if far_levels:
            pf[m] = dot(xp[:, pl.ds(start, 2 * LEAF)], w3[m])
        n = [count_of(2 * m), count_of(2 * m + 1)]
        b1 = base_of[1] + m
        lane = iota((PAD, LANES), 1)
        for p in range(2):
            where = slice(p * LANES, (p + 1) * LANES)
            put_query(qf.at[b1], t1[p][:rows, :LANES], scale / 2, where)
            put_value(vvf.at[b1], t1[p][rows:, :LANES], clip_mass(n[p], lane << 1, 2), where)
        if 2 in near_levels:
            b2 = base_of[2] + m // 2
            x2 = t1[0][:, LANES:] + t1[1][:, LANES:]
            where = pl.ds(pl.multiple_of((m % 2) * LANES, LANES), LANES)
            mass = jnp.where(
                lane < 64, clip_mass(n[0], lane << 2, 4), clip_mass(n[1], (lane - 64) << 2, 4)
            )
            put_query(qf.at[b2], x2[:rows], scale / 4, where)
            put_value(vvf.at[b2], x2[rows:], mass, where)
        for p in range(2):
            for level in ua_levels:
                count = LEAF >> level
                x = kk[p][ua_at[level] : ua_at[level] + count]
                mass = clip_mass(n[p], iota((count, LANES), 0) << level, 1 << level)
                inverse = 1.0 / jnp.maximum(mass, 1.0)
                a = x[:, :rows] * inverse
                if level in near_levels:
                    b = x[:, rows:] * inverse
                    bias = jnp.where(mass > 0, 0.0, NEG)
                    if level == 1:
                        put_key(kmf.at[b1], a, b, bias, slice(p * count, (p + 1) * count))
                    else:
                        spot = pl.multiple_of((m % 2) * LANES + p * count, count)
                        put_key(kmf.at[b2], a, b, bias, pl.ds(spot, count))
                else:
                    spot = pl.multiple_of((2 * m + p) * count, count)
                    kf[level][pl.ds(spot, count), :] = a

    def remote(src, dst, send, recv, target):
        return pltpu.make_async_remote_copy(
            src_ref=src,
            dst_ref=dst,
            send_sem=send,
            recv_sem=recv,
            device_id={"seq": target},
            device_id_type=pl.DeviceIdType.MESH,
        )

    def halo(side):
        start, end = (LEAF, tokens + LEAF) if side == 0 else (tokens, 0)
        target = jnp.maximum(seq - 1, 0) if side == 0 else jnp.minimum(seq + 1, seq_count - 1)
        return (
            remote(
                ka.at[pl.ds(start, LEAF)],
                ka.at[pl.ds(end, LEAF)],
                halo_send.at[2 * side],
                halo_recv.at[2 * side],
                target,
            ),
            remote(
                vx.at[:, pl.ds(start, LEAF)],
                vx.at[:, pl.ds(end, LEAF)],
                halo_send.at[2 * side + 1],
                halo_recv.at[2 * side + 1],
                target,
            ),
        )

    def pair_at(i):
        return jnp.where(i == 0, 0, jnp.where(i == 1, pairs - 1, i - 1))

    permute(0)

    @pl.loop(1, pairs)
    def _(i):
        pool(pair_at(i - 1))
        permute(pair_at(i))

        @pl.when(i == 1)
        def _():
            pl.semaphore_wait(barrier, seq_count - 1)

        @pl.when(jnp.logical_and(i == 1, has_left))
        def _():
            for copy in halo(0):
                copy.start()

        @pl.when(jnp.logical_and(i == 1, has_right))
        def _():
            for copy in halo(1):
                copy.start()

    pool(pair_at(pairs - 1))

    def far_copies(level):
        bit = level - depth_local
        nb = 1 << bit
        part = tokens >> level
        slot = lax.rem(seq, nb)
        base = ((seq >> bit) ^ 1) << bit
        copies = []
        for j in range(nb):
            target = base + j
            copies.append(
                remote(
                    kmp[level],
                    kmr[level].at[pl.ds(pl.multiple_of(slot * part, part), part)],
                    far_send[level].at[2 * j],
                    far_recv[level].at[2 * slot],
                    target,
                )
            )
            copies.append(
                remote(
                    vvp[level],
                    vvr[level].at[slot],
                    far_send[level].at[2 * j + 1],
                    far_recv[level].at[2 * slot + 1],
                    target,
                )
            )
        return copies

    for i, level in enumerate(far_levels):
        part = tokens >> level
        pieces = part // LANES
        per = pairs // max(pieces, 1)
        cols = slice(i * LANES, (i + 1) * LANES)
        for j in range(max(pieces, 1)):
            x = sum(pf[j * per + e, :, cols] for e in range(per))
            where = slice(j * LANES, (j + 1) * LANES)
            put_query(qr[level], x[:rows], scale / 2**level, where)
            kept = min(LANES, part)
            where = slice(j * kept, (j + 1) * kept)
            vvp[level][0:rows, where] = fixed(x[rows : 2 * rows, :kept], BOUND * 2**level)
            vvp[level][rows:, where] = x[2 * rows :, :kept].astype(I32).astype(I16)
        if level in us:
            sums = dot(us[level][...], kv[:, 0:rows])
            valid = jnp.broadcast_to(xp[2 * rows : 2 * rows + 1, :], (LANES, tokens))
            mass = dot(us[level][...], valid, ((1,), (1,)))
            mean = sums / jnp.maximum(mass, 1.0)
        else:
            mean = kf[level][...]
        kmp[level][...] = fixed(mean, BOUND)
        for copy in far_copies(level):
            copy.start()

    def far_score(km, q, slot, h, best_ref):
        s = dot(km, q)
        keys, cols = s.shape
        ss[slot, h, 0:keys, 0:cols] = s
        best = jnp.max(s.reshape(keys // 8, 8, cols), axis=0)
        best = jnp.max(best, axis=0, keepdims=True).astype(BF).astype(F32)
        best_ref[h] = jnp.broadcast_to(best, (8, cols))

    def far_soft(vvs, slot, h, best_ref, out_ref):
        cols = best_ref.shape[2]
        best = best_ref[h]
        step, acc = 0, None
        for vv in vvs:
            keys = vv.shape[1]
            x = ss[slot, h, step : step + keys, 0:cols].reshape(keys // 8, 8, cols)
            w = jnp.exp2(x - best[None]).reshape(keys, cols)
            w_hi, w_lo = split(w)
            both = dot(vv, w_hi)
            low = jnp.concatenate([both[size:], jnp.zeros((PAD, cols), F32)], axis=0)
            term = both[:size] + low + dot(vv[:size], w_lo)
            acc = term if acc is None else acc + term
            step += keys
        out_ref[h] = acc

    def local_score(i, slot, h):
        far_score(kmf[i ^ 1, h], qf[i, h], slot, h, fb.at[i])

    def local_soft(i, slot, h):
        far_soft([vvf[i ^ 1, h]], slot, h, fb.at[i], fo.at[i])

    for h in range(heads):
        local_score(0, 0, h)

    @pl.loop(0, first // 2)
    def _(b):
        for j in range(2):
            i = 2 * b + j
            for h in range(heads):
                local_soft(i, j, h)
                local_score(jnp.minimum(i + 1, first - 1), 1 - j, h)

    @pl.when(has_right)
    def _():
        for copy in halo(0):
            copy.wait_recv()

    @pl.when(has_left)
    def _():
        for copy in halo(1):
            copy.wait_recv()

    for n, at in ((-1, 0), (leaves, tokens + LEAF)):
        tail0, tail1, _ = key_tail(ka[at : at + LEAF, :].astype(F32), leaf_bias(count_of(n)))
        kb[0, at : at + LEAF, :] = tail0.astype(BF)
        kb[1, at : at + LEAF, :] = tail1.astype(BF)

    def near_score(n, slot, h):
        at = pl.multiple_of(n * LEAF, LEAF)
        best = None
        for j in range(3):
            key_rows = pl.ds(pl.multiple_of(at + j * LEAF, LEAF), LEAF)
            left = jnp.concatenate([ka[key_rows, :], kb[h, key_rows, :]], axis=1)
            s = dot(left, qx[h, :, pl.ds(at, LEAF)])
            ss[slot, h, j * LEAF : (j + 1) * LEAF, :] = s
            top = jnp.max(s.reshape(LEAF // 8, 8, LEAF), axis=0)
            best = top if best is None else jnp.maximum(best, top)
        sb[slot, h] = jnp.broadcast_to(jnp.max(best, axis=0, keepdims=True), (8, LEAF))

    def near_soft(n, slot, h):
        at = pl.multiple_of(n * LEAF, LEAF)
        best = sb[slot, h]
        total, acc = None, None
        part = slice(h * width, (h + 1) * width)
        for j in range(3):
            x = ss[slot, h, j * LEAF : (j + 1) * LEAF, :].reshape(LEAF // 8, 8, LEAF)
            w = jnp.exp2(x - best[None])
            term = jnp.sum(w, axis=0)
            total = term if total is None else total + term
            keys = pl.ds(pl.multiple_of(at + j * LEAF, LEAF), LEAF)
            term = dot(vx[part, keys], w.reshape(LEAF, LEAF).astype(BF))
            acc = term if acc is None else acc + term
        num[part, pl.ds(at, LEAF)] = acc
        stat[2 * h : 2 * h + 1, pl.ds(at, LEAF)] = best[0:1]
        stat[2 * h + 1 : 2 * h + 2, pl.ds(at, LEAF)] = jnp.sum(total, axis=0, keepdims=True)

    for h in range(heads):
        near_score(0, 0, h)

    @pl.loop(0, leaves // 4)
    def _(i):
        for j in range(4):
            n = 4 * i + j
            for h in range(heads):
                near_soft(n, j % 2, h)
                near_score(jnp.minimum(n + 1, leaves - 1), 1 - j % 2, h)

    for slot, level in enumerate(far_levels):
        nb = 1 << (level - depth_local)
        part = tokens >> level
        for i in range(nb):
            remote(
                kmp[level], kmr[level].at[pl.ds(i * part, part)],
                far_send[level].at[2 * i], far_recv[level].at[2 * i], seq,
            ).wait_recv()
            remote(
                vvp[level], vvr[level].at[i],
                far_send[level].at[2 * i + 1], far_recv[level].at[2 * i + 1], seq,
            ).wait_recv()
        ones = jnp.ones((PAD, LANES), BF)
        masses = []
        for i in range(nb):
            mass = vvr[level][i, rows:].astype(I32).astype(F32)
            masses.append(dot(mass.astype(BF), ones, ((0,), (0,))))
            put_value(vvr2[level].at[i], unfixed(vvr[level][i, 0:rows], BOUND * 2**level), mass, slice(0, part))
        bias = jnp.where(jnp.concatenate(masses, axis=0) > 0, 0.0, NEG)
        mean = unfixed(kmr[level][...], BOUND)
        put_key(kmr2[level], mean, pltpu.roll(mean, width, 1), bias, slice(0, LEAF))
        for h in range(heads):
            far_score(kmr2[level][h], qr[level][h], slot % 2, h, fbr[level])
        for h in range(heads):
            far_soft([vvr2[level][i, h] for i in range(nb)], slot % 2, h, fbr[level], for_[level])

    def up(z):
        return dot(jnp.concatenate(split(z), axis=1), uu[...])

    def with_best(acc, best):
        return jnp.concatenate([acc[: size - 8], jnp.broadcast_to(best, (8, acc.shape[1]))], axis=0)

    def merge(acc, best, z):
        old = z[size - 8 : size - 7]
        new = jnp.maximum(best, old)
        both = acc * jnp.exp2(best - new) + z * jnp.exp2(old - new)
        return with_best(both, new)

    for h in range(heads):
        z = None
        for level in reversed(far_levels):
            acc, best = for_[level][h], fbr[level][h, 0:1]
            if z is None:
                z = with_best(acc, best)
            else:
                z = jnp.concatenate(
                    [up(z[:, j * LANES : (j + 1) * LANES]) for j in range(z.shape[1] // LANES)], axis=1
                )[:, : acc.shape[1]]
                z = merge(acc, best, z)
        if z is not None:
            for j in range(z.shape[1] // LANES):
                zb[h, j] = z[:, j * LANES : (j + 1) * LANES]
        for level in reversed(near_levels):
            for i in reversed(range(leaves >> level)):
                block = base_of[level] + i
                acc, best = fo[block, h], fb[block, h, 0:1]
                if z is None:
                    x = with_best(acc, best)
                else:
                    x = merge(acc, best, up(zb[h, i]))
                zb[h, 2 * i] = x[:, :LANES]
                zb[h, 2 * i + 1] = x[:, LANES:]
            z = True
        for n in range(leaves):
            cols = slice(n * LEAF, (n + 1) * LEAF)
            part = slice(h * width, (h + 1) * width)
            near_best, near_total = stat[2 * h : 2 * h + 1, cols], stat[2 * h + 1 : 2 * h + 2, cols]
            z = up(zb[h, n])
            old = z[size - 8 : size - 7]
            new = jnp.maximum(near_best, old)
            mine, other = jnp.exp2(near_best - new), jnp.exp2(old - new)
            inverse = 1.0 / (near_total * mine + z[width : width + 1] * other)
            out[part, cols] = (num[part, cols] * (mine * inverse) + z[:width] * (other * inverse)).astype(BF)

    @pl.when(has_left)
    def _():
        for copy in halo(0):
            copy.wait_send()

    @pl.when(has_right)
    def _():
        for copy in halo(1):
            copy.wait_send()

    for level in far_levels:
        for copy in far_copies(level):
            copy.wait_send()


def shards(q_heads, k_heads, v_heads, morton_order, leaf_counts):
    heads_real, width, tokens = q_heads.shape
    heads = heads_real + heads_real % 2
    seq_count = lax.axis_size("seq")
    rows = heads * width
    flat = []
    for x in (q_heads, k_heads, v_heads):
        if heads != heads_real:
            x = jnp.concatenate([x, jnp.zeros_like(x[:1])], axis=0)
        flat.append(x.reshape(rows, tokens))
    leaves, depth_local, near_levels, far_levels = plan(tokens, seq_count)
    size = width + PAD
    near_blocks = sum(leaves >> l for l in near_levels)
    ua_rows = sum(max(LEAF >> l, 16) for l in near_levels + far_levels if (LEAF >> l) >= 8)
    vm = pltpu.VMEM
    scratch = [
        vm(morton_order.shape, I32),
        pltpu.SMEM(leaf_counts.shape, I32),
        vm((3 * rows, tokens), BF),
        vm((tokens + 2 * LEAF, rows), BF),
        vm((heads, tokens + 2 * LEAF, LANES), BF),
        vm((rows, tokens + 2 * LEAF), BF),
        vm((heads, 4 * width, tokens), BF),
        vm((2 * rows + PAD, tokens), BF),
        vm((tokens, 2 * rows), BF),
        vm((2, LEAF, LEAF), BF),
        vm((leaves // 2, 2 * LEAF, LANES * len(far_levels)), BF),
        vm((ua_rows, LEAF), BF),
        vm((LEAF, LEAF), BF),
        vm((near_blocks, heads, 4 * width, LEAF), BF),
        vm((near_blocks, heads, LEAF, 2 * rows), BF),
        vm((near_blocks, heads, size + width, LEAF), BF),
        vm((near_blocks, heads, size, LEAF), F32),
        vm((near_blocks, heads, 8, LEAF), F32),
        vm((leaves // 2, 2 * rows + PAD, LANES * len(far_levels)), F32),
        vm((2, heads, 3 * LEAF, LEAF), F32),
        vm((2, heads, 8, LEAF), F32),
        vm((rows, tokens), F32),
        vm((2 * heads + (-2 * heads) % 8, tokens), F32),
        vm((heads, leaves, size, LANES), F32),
    ]
    scratch += [vm((tokens >> l, rows), F32) for l in far_levels]
    scratch += [vm((heads, 4 * width, padded(tokens, l)), BF) for l in far_levels]
    scratch += [vm((heads, LEAF, 2 * rows), BF) for l in far_levels]
    scratch += [vm((1 << (l - depth_local), heads, size + width, tokens >> l), BF) for l in far_levels]
    scratch += [vm((heads, size, padded(tokens, l)), F32) for l in far_levels]
    scratch += [vm((heads, 8, padded(tokens, l)), F32) for l in far_levels]
    scratch += [vm((tokens >> l, rows), I16) for l in far_levels]
    scratch += [vm((rows + PAD, tokens >> l), I16) for l in far_levels]
    scratch += [vm((LEAF, rows), I16) for l in far_levels]
    scratch += [vm((1 << (l - depth_local), rows + PAD, tokens >> l), I16) for l in far_levels]
    sem = pltpu.SemaphoreType.DMA
    scratch += [sem((5,)), sem((4,)), sem((4,))]
    scratch += [sem((2 << (l - depth_local),)) for l in far_levels] * 2
    scratch += [vm((tokens >> l, tokens), BF) for l in far_levels if (LEAF >> l) < 8]
    out = pl.pallas_call(
        functools.partial(kernel, (heads, width, tokens, seq_count)),
        out_shape=pltpu.VMEM((rows, tokens), BF),
        in_specs=[pl.BlockSpec(memory_space=pltpu.HBM)] * 5,
        out_specs=pl.BlockSpec(memory_space=pltpu.VMEM),
        scratch_shapes=scratch,
        compiler_params=pltpu.CompilerParams(
            collective_id=0, has_side_effects=True, vmem_limit_bytes=VMEM_LIMIT
        ),
    )(*flat, morton_order, leaf_counts)
    return out.reshape(heads, width, tokens)[:heads_real]


def solution(mesh):
    placed = (
        P("head", None, ("grp", "seq")),
        P("head", None, ("grp", "seq")),
        P("head", None, ("grp", "seq")),
        P(("grp", "seq"), None),
        P("grp"),
    )
    return jax.shard_map(
        shards,
        mesh=mesh,
        in_specs=placed,
        out_specs=P("head", None, ("grp", "seq")),
        check_vma=False,
    )
```

```python
import functools
import math

import jax
import jax.numpy as jnp
from jax import lax
from jax.experimental import pallas as pl
from jax.experimental.pallas import tpu as pltpu
from jax.sharding import PartitionSpec as P

LEAF = 256
LANES = 128
NEG = -1e30
BF = jnp.bfloat16
F32 = jnp.float32
I32 = jnp.int32
I16 = jnp.int16
PAD = 16
BOUND = 10.0
STEPS = 32700.0
VMEM_LIMIT = 63488 * 1024


def dot(a, b, dims=((1,), (0,))):
    return lax.dot_general(a, b, (dims, ((), ())), preferred_element_type=F32)


def split(x):
    hi = x.astype(BF)
    return hi, (x - hi.astype(F32)).astype(BF)


def iota(shape, dim):
    return lax.broadcasted_iota(I32, shape, dim)


def fixed(x, bound):
    return jnp.floor(x * (STEPS / bound) + 0.5).astype(I32).astype(I16)


def unfixed(x, bound):
    return x.astype(I32).astype(F32) * (bound / STEPS)


def plan(tokens, seq_count):
    leaves = tokens // LEAF
    depth_local = leaves.bit_length() - 1
    depth_all = (leaves * seq_count).bit_length() - 1
    levels = list(range(1, depth_all))
    near_levels = [l for l in levels if l < depth_local]
    far_levels = [l for l in levels if l >= depth_local]
    return leaves, depth_local, near_levels, far_levels


def padded(tokens, level):
    return max(LANES, tokens >> level)


def kernel(cfg, *refs):
    heads, width, tokens, seq_count = cfg
    rows = heads * width
    leaves, depth_local, near_levels, far_levels = plan(tokens, seq_count)
    pairs = leaves // 2
    scale = math.log2(math.e) / math.sqrt(width)
    size = width + PAD
    refs = list(refs)
    take = lambda n: [refs.pop(0) for _ in range(n)]
    q_hbm, k_hbm, v_hbm, order_hbm, counts_hbm, out = take(6)
    order, counts = take(2)
    xin, ka, kb, vx, qx, xp, kv = take(7)
    w1, w3, ua, uf, uu = take(5)
    qf, kmf, vvf, fo, fb = take(5)
    pf = take(1)[0]
    ss, sb, num, stat, zb = take(5)
    per_far = lambda: dict(zip(far_levels, take(len(far_levels))))
    qr, kmr2, vvr2, for_, fbr, fp, fr = (per_far() for _ in range(7))
    in_sem, halo_send, halo_recv = take(3)
    far_send, far_recv = per_far(), per_far()
    us = dict(zip([l for l in far_levels if (LEAF >> l) < 8], refs))
    pieced = [l for l in far_levels if l not in us]

    seq = lax.axis_index("seq")
    has_left, has_right = seq > 0, seq < seq_count - 1

    loads = [
        pltpu.make_async_copy(src, xin.at[pl.ds(i * rows, rows)], in_sem.at[i])
        for i, src in enumerate((q_hbm, k_hbm, v_hbm))
    ]
    loads.append(pltpu.make_async_copy(order_hbm, order, in_sem.at[3]))
    loads.append(pltpu.make_async_copy(counts_hbm, counts, in_sem.at[4]))
    for load in loads:
        load.start()
    barrier = pltpu.get_barrier_semaphore()
    for step in range(1, seq_count):
        other = lax.rem(seq + step, seq_count)
        pl.semaphore_signal(
            barrier, inc=1, device_id={"seq": other}, device_id_type=pl.DeviceIdType.MESH
        )

    @pl.when(jnp.logical_not(has_left))
    def _():
        ka[0:LEAF, :] = jnp.zeros((LEAF, rows), BF)
        vx[:, 0:LEAF] = jnp.zeros((rows, LEAF), BF)

    @pl.when(jnp.logical_not(has_right))
    def _():
        ka[tokens + LEAF :, :] = jnp.zeros((LEAF, rows), BF)
        vx[:, tokens + LEAF :] = jnp.zeros((rows, LEAF), BF)

    def count_of(n):
        leaf = seq * leaves + n
        total = leaves * seq_count
        inside = jnp.logical_and(leaf >= 0, leaf < total)
        return jnp.where(inside, counts[jnp.clip(leaf, 0, total - 1)], 0)

    def ones_where(mask):
        return jnp.where(mask, 1.0, 0.0).astype(BF)

    t = iota((LEAF, LEAF), 0)
    c = iota((LEAF, LEAF), 1)
    for p in range(2):
        w1[p] = ones_where(
            jnp.logical_or(
                jnp.logical_and(c < LANES, (t >> 1) == c),
                jnp.logical_and(c >= LANES, (t >> 2) + 64 * p == c - LANES),
            )
        )
    uu[...] = ones_where((c >> 1) == (t & (LANES - 1)))
    for i, level in enumerate(far_levels):
        t2 = iota((2 * LEAF, LANES), 0)
        c2 = iota((2 * LEAF, LANES), 1)
        for m in range(pairs):
            w3[m, :, i * LANES : (i + 1) * LANES] = ones_where(
                ((t2 + 2 * LEAF * m) >> level) & (LANES - 1) == c2
            )
    ua_at, uf_at = {}, {}
    for ref, spots, which in ((ua, ua_at, near_levels), (uf, uf_at, pieced)):
        at = 0
        for level in which:
            n = max(LEAF >> level, 16)
            spots[level] = at
            ref[at : at + n, :] = ones_where((iota((n, LEAF), 1) >> level) == iota((n, LEAF), 0))
            at += n
    for level, u in us.items():
        u[...] = ones_where((iota(u.shape, 1) >> level) == iota(u.shape, 0))

    def tail_rows(cols):
        r = iota((64, cols), 0)
        return ones_where(r == 0)

    for h in range(heads):
        off = (1 - h) * width
        qx[h, off : off + width, :] = jnp.zeros((width, tokens), BF)
        qx[h, 3 * width :, :] = tail_rows(tokens)
        for i in range(qf.shape[0]):
            qf[i, h, 3 * width :, :] = tail_rows(LEAF)
        for level in far_levels:
            qr[level][h, 3 * width :, :] = tail_rows(qr[level].shape[2])

    for load in loads:
        load.wait()

    lane_lo = iota((LEAF, LANES), 1) < width
    lane_is = iota((LEAF, LANES), 1) == width

    def key_tail(key_t, bias):
        shape = key_t.shape
        lo = iota(shape, 1) < width
        at = iota(shape, 1) == width
        rest = jnp.where(at, bias, 0.0)
        rolled = pltpu.roll(key_t, width, 1)
        return jnp.where(lo, key_t, rest), jnp.where(lo, rolled, rest), rolled

    def leaf_bias(count):
        return jnp.where(iota((LEAF, LANES), 0) < count, 0.0, NEG)

    def permute(m):
        for p in range(2):
            n = 2 * m + p
            at = pl.multiple_of(n * LEAF, LEAF)
            picks = order[0:1, pl.ds(at, LEAF)]
            spots = iota((tokens, LEAF), 0)
            hot = jnp.where(spots == picks, 1.0, 0.0).astype(BF)
            moved = dot(xin[...], hot)
            count = count_of(n)
            query, key, value = moved[:rows], moved[rows : 2 * rows], moved[2 * rows :]
            key_t = key.T
            on_row = iota((rows, LEAF), 1) < count
            on_col = iota((LEAF, rows), 0) < count
            tail0, tail1, rolled = key_tail(key_t, leaf_bias(count))
            ka[pl.ds(at + LEAF, LEAF), :] = key_t.astype(BF)
            kb[0, pl.ds(at + LEAF, LEAF), :] = tail0.astype(BF)
            kb[1, pl.ds(at + LEAF, LEAF), :] = tail1.astype(BF)
            kv[pl.ds(at, LEAF), 0:rows] = jnp.where(on_col, rolled, 0.0).astype(BF)
            kv[pl.ds(at, LEAF), rows : 2 * rows] = jnp.where(on_col, key_t, 0.0).astype(BF)
            kv[pl.ds(at, LEAF), 2 * rows :] = jnp.where(on_col, value.T, 0.0).astype(BF)
            vx[:, pl.ds(at + LEAF, LEAF)] = value.astype(BF)
            xp[0:rows, pl.ds(at, LEAF)] = query.astype(BF)
            xp[rows : 2 * rows, pl.ds(at, LEAF)] = jnp.where(on_row, value, 0.0).astype(BF)
            xp[2 * rows :, pl.ds(at, LEAF)] = ones_where(on_row[:PAD])
            hi, lo = split(query * scale)
            for h in range(heads):
                part = slice(h * width, (h + 1) * width)
                qx[h, part, pl.ds(at, LEAF)] = hi[part]
                qx[h, 2 * width : 3 * width, pl.ds(at, LEAF)] = lo[part]

    def put_query(ref, x, factor, where):
        hi, lo = split(x * factor)
        for h in range(heads):
            part = slice(h * width, (h + 1) * width)
            ref[h, 0:width, where] = hi[part]
            ref[h, width : 2 * width, where] = hi[part]
            ref[h, 2 * width : 3 * width, where] = lo[part]

    def put_value(ref, x, mass, where):
        hi, lo = split(x)
        for h in range(heads):
            part = slice(h * width, (h + 1) * width)
            ref[h, 0:width, where] = hi[part]
            ref[h, width:size, where] = mass.astype(BF)
            ref[h, size:, where] = lo[part]

    def put_key(ref, a, b, bias, where):
        lo_lane = iota(a.shape, 1) < width
        bias_lane = iota(a.shape, 1) == width
        a_hi, b_hi = a.astype(BF).astype(F32), b.astype(BF).astype(F32)
        rest = jnp.where(bias_lane, bias, 0.0)
        ref[0, where, 0:rows] = jnp.where(lo_lane, a_hi, b - b_hi).astype(BF)
        ref[0, where, rows:] = jnp.where(lo_lane, a_hi, rest).astype(BF)
        ref[1, where, 0:rows] = jnp.where(lo_lane, b_hi, a - a_hi).astype(BF)
        ref[1, where, rows:] = jnp.where(lo_lane, b_hi, rest).astype(BF)

    def clip_mass(count, at, g):
        return jnp.clip(count - at, 0, g).astype(F32)

    base_of, first = {}, 0
    for level in near_levels:
        base_of[level] = first
        first += leaves >> level

    def pool_far(m):
        if not pieced:
            return
        start = pl.multiple_of(m * 2 * LEAF, 2 * LEAF)
        kk = []
        for p in range(2):
            at = pl.multiple_of(start + p * LEAF, LEAF)
            kk.append(dot(uf[...], kv[pl.ds(at, LEAF), rows:]))
        for level in pieced:
            count = LEAF >> level
            x = jnp.concatenate([k[uf_at[level] : uf_at[level] + count] for k in kk], axis=0)
            mass = [
                clip_mass(count_of(2 * m + p), iota((count, LANES), 0) << level, 1 << level)
                for p in range(2)
            ]
            mean = x[:, :rows] / jnp.maximum(jnp.concatenate(mass, axis=0), 1.0)
            fp[level][m, :, 0:rows] = fixed(mean, BOUND)
            fp[level][m, :, rows:] = fixed(x[:, rows:], BOUND * 2**level)

    def pool_near(m):
        start = pl.multiple_of(m * 2 * LEAF, 2 * LEAF)
        t1, kk = [], []
        for p in range(2):
            at = pl.multiple_of(start + p * LEAF, LEAF)
            t1.append(dot(xp[0 : 2 * rows, pl.ds(at, LEAF)], w1[p]))
            kk.append(dot(ua[...], kv[pl.ds(at, LEAF), 0 : 2 * rows]))
        if far_levels:
            pf[m] = dot(xp[0:rows, pl.ds(start, 2 * LEAF)], w3[m])
        n = [count_of(2 * m), count_of(2 * m + 1)]
        b1 = base_of[1] + m
        lane = iota((PAD, LANES), 1)
        for p in range(2):
            where = slice(p * LANES, (p + 1) * LANES)
            put_query(qf.at[b1], t1[p][:rows, :LANES], scale / 2, where)
            put_value(vvf.at[b1], t1[p][rows:, :LANES], clip_mass(n[p], lane << 1, 2), where)
        if 2 in near_levels:
            b2 = base_of[2] + m // 2
            x2 = t1[0][:, LANES:] + t1[1][:, LANES:]
            where = pl.ds(pl.multiple_of((m % 2) * LANES, LANES), LANES)
            mass = jnp.where(
                lane < 64, clip_mass(n[0], lane << 2, 4), clip_mass(n[1], (lane - 64) << 2, 4)
            )
            put_query(qf.at[b2], x2[:rows], scale / 4, where)
            put_value(vvf.at[b2], x2[rows:], mass, where)
        for p in range(2):
            for level in near_levels:
                count = LEAF >> level
                x = kk[p][ua_at[level] : ua_at[level] + count]
                mass = clip_mass(n[p], iota((count, LANES), 0) << level, 1 << level)
                inverse = 1.0 / jnp.maximum(mass, 1.0)
                b, a = x[:, :rows] * inverse, x[:, rows:] * inverse
                bias = jnp.where(mass > 0, 0.0, NEG)
                if level == 1:
                    put_key(kmf.at[b1], a, b, bias, slice(p * count, (p + 1) * count))
                else:
                    spot = pl.multiple_of((m % 2) * LANES + p * count, count)
                    put_key(kmf.at[b2], a, b, bias, pl.ds(spot, count))

    def remote(src, dst, send, recv, target):
        return pltpu.make_async_remote_copy(
            src_ref=src,
            dst_ref=dst,
            send_sem=send,
            recv_sem=recv,
            device_id={"seq": target},
            device_id_type=pl.DeviceIdType.MESH,
        )

    def halo(side):
        start, end = (LEAF, tokens + LEAF) if side == 0 else (tokens, 0)
        target = jnp.maximum(seq - 1, 0) if side == 0 else jnp.minimum(seq + 1, seq_count - 1)
        return (
            remote(
                ka.at[pl.ds(start, LEAF)],
                ka.at[pl.ds(end, LEAF)],
                halo_send.at[2 * side],
                halo_recv.at[2 * side],
                target,
            ),
            remote(
                vx.at[:, pl.ds(start, LEAF)],
                vx.at[:, pl.ds(end, LEAF)],
                halo_send.at[2 * side + 1],
                halo_recv.at[2 * side + 1],
                target,
            ),
        )

    def pair_at(i):
        return jnp.where(i == 0, 0, jnp.where(i == 1, pairs - 1, i - 1))

    def far_copies(level, piece):
        bit = level - depth_local
        nb = 1 << bit
        pieces = fp[level].shape[0]
        slot = lax.rem(seq, nb)
        base = ((seq >> bit) ^ 1) << bit
        return [
            remote(
                fp[level].at[piece],
                fr[level].at[slot, piece],
                far_send[level].at[j * pieces + piece],
                far_recv[level].at[slot * pieces + piece],
                base + j,
            )
            for j in range(nb)
        ]

    permute(0)

    @pl.loop(1, pairs)
    def _(i):
        pool_far(pair_at(i - 1))
        permute(pair_at(i))

        @pl.when(i == 1)
        def _():
            pl.semaphore_wait(barrier, seq_count - 1)

        @pl.when(jnp.logical_and(i == 1, has_left))
        def _():
            for copy in halo(0):
                copy.start()

        @pl.when(jnp.logical_and(i == 1, has_right))
        def _():
            for copy in halo(1):
                copy.start()

        for level in reversed(pieced):
            for copy in far_copies(level, pair_at(i - 1)):
                copy.start()

    pool_far(pair_at(pairs - 1))
    for level in reversed(pieced):
        for copy in far_copies(level, pair_at(pairs - 1)):
            copy.start()
    for level in us:
        sums = dot(us[level][...], kv[:, rows:])
        valid = jnp.broadcast_to(xp[2 * rows : 2 * rows + 1, :], (LANES, tokens))
        mass = dot(us[level][...], valid, ((1,), (1,)))
        fp[level][0, :, 0:rows] = fixed(sums[:, :rows] / jnp.maximum(mass, 1.0), BOUND)
        fp[level][0, :, rows:] = fixed(sums[:, rows:], BOUND * 2**level)
        for copy in far_copies(level, 0):
            copy.start()

    @pl.loop(0, pairs)
    def _(m):
        pool_near(m)

    for i, level in enumerate(far_levels):
        pieces = max((tokens >> level) // LANES, 1)
        per = pairs // pieces
        cols = slice(i * LANES, (i + 1) * LANES)
        for j in range(pieces):
            x = sum(pf[j * per + e, :, cols] for e in range(per))
            put_query(qr[level], x, scale / 2**level, slice(j * LANES, (j + 1) * LANES))

    def far_score(km, q, slot, h, best_ref):
        s = dot(km, q)
        keys, cols = s.shape
        ss[slot, h, 0:keys, 0:cols] = s
        best = jnp.max(s.reshape(keys // 8, 8, cols), axis=0)
        best = jnp.max(best, axis=0, keepdims=True).astype(BF).astype(F32)
        best_ref[h] = jnp.broadcast_to(best, (8, cols))

    def far_soft(vvs, slot, h, best_ref, out_ref):
        cols = best_ref.shape[2]
        best = best_ref[h]
        step, acc = 0, None
        for vv in vvs:
            keys = vv.shape[1]
            x = ss[slot, h, step : step + keys, 0:cols].reshape(keys // 8, 8, cols)
            w = jnp.exp2(x - best[None]).reshape(keys, cols)
            w_hi, w_lo = split(w)
            both = dot(vv, w_hi)
            low = jnp.concatenate([both[size:], jnp.zeros((PAD, cols), F32)], axis=0)
            term = both[:size] + low + dot(vv[:size], w_lo)
            acc = term if acc is None else acc + term
            step += keys
        out_ref[h] = acc

    def local_score(i, slot, h):
        far_score(kmf[i ^ 1, h], qf[i, h], slot, h, fb.at[i])

    def local_soft(i, slot, h):
        far_soft([vvf[i ^ 1, h]], slot, h, fb.at[i], fo.at[i])

    for h in range(heads):
        local_score(0, 0, h)

    @pl.loop(0, first // 2)
    def _(b):
        for j in range(2):
            i = 2 * b + j
            for h in range(heads):
                local_soft(i, j, h)
                local_score(jnp.minimum(i + 1, first - 1), 1 - j, h)

    @pl.when(has_right)
    def _():
        for copy in halo(0):
            copy.wait_recv()

    @pl.when(has_left)
    def _():
        for copy in halo(1):
            copy.wait_recv()

    for n, at in ((-1, 0), (leaves, tokens + LEAF)):
        tail0, tail1, _ = key_tail(ka[at : at + LEAF, :].astype(F32), leaf_bias(count_of(n)))
        kb[0, at : at + LEAF, :] = tail0.astype(BF)
        kb[1, at : at + LEAF, :] = tail1.astype(BF)

    def near_score(n, slot, h):
        at = pl.multiple_of(n * LEAF, LEAF)
        best = None
        for j in range(3):
            key_rows = pl.ds(pl.multiple_of(at + j * LEAF, LEAF), LEAF)
            left = jnp.concatenate([ka[key_rows, :], kb[h, key_rows, :]], axis=1)
            s = dot(left, qx[h, :, pl.ds(at, LEAF)])
            ss[slot, h, j * LEAF : (j + 1) * LEAF, :] = s
            top = jnp.max(s.reshape(LEAF // 8, 8, LEAF), axis=0)
            best = top if best is None else jnp.maximum(best, top)
        sb[slot, h] = jnp.broadcast_to(jnp.max(best, axis=0, keepdims=True), (8, LEAF))

    def near_soft(n, slot, h):
        at = pl.multiple_of(n * LEAF, LEAF)
        best = sb[slot, h]
        total, acc = None, None
        part = slice(h * width, (h + 1) * width)
        for j in range(3):
            x = ss[slot, h, j * LEAF : (j + 1) * LEAF, :].reshape(LEAF // 8, 8, LEAF)
            w = jnp.exp2(x - best[None])
            term = jnp.sum(w, axis=0)
            total = term if total is None else total + term
            keys = pl.ds(pl.multiple_of(at + j * LEAF, LEAF), LEAF)
            term = dot(vx[part, keys], w.reshape(LEAF, LEAF).astype(BF))
            acc = term if acc is None else acc + term
        num[part, pl.ds(at, LEAF)] = acc
        stat[2 * h : 2 * h + 1, pl.ds(at, LEAF)] = best[0:1]
        stat[2 * h + 1 : 2 * h + 2, pl.ds(at, LEAF)] = jnp.sum(total, axis=0, keepdims=True)

    for h in range(heads):
        near_score(0, 0, h)

    @pl.loop(0, leaves // 4)
    def _(i):
        for j in range(4):
            n = 4 * i + j
            for h in range(heads):
                near_soft(n, j % 2, h)
                near_score(jnp.minimum(n + 1, leaves - 1), 1 - j % 2, h)

    for slot, level in enumerate(reversed(far_levels)):
        bit = level - depth_local
        nb = 1 << bit
        part = tokens >> level
        pieces = fp[level].shape[0]
        base = ((seq >> bit) ^ 1) << bit
        lane = iota((PAD, LEAF), 1)
        count = jnp.zeros((PAD, LEAF), I32)
        for leaf in range(leaves * nb):
            count = jnp.where((lane << level) >> 8 == leaf, counts[base * leaves + leaf], count)
        mass = clip_mass(count, (lane << level) & (LEAF - 1), 1 << level)
        mass_col = dot(mass.astype(BF), jnp.ones((PAD, LANES), BF), ((0,), (0,)))
        bias = jnp.where(mass_col > 0, 0.0, NEG)
        for i in range(nb):
            for piece in range(pieces):
                remote(
                    fp[level].at[piece], fr[level].at[i, piece],
                    far_send[level].at[i * pieces + piece], far_recv[level].at[i * pieces + piece], seq,
                ).wait_recv()
        got = jnp.concatenate(
            [fr[level][i, piece].astype(I32).astype(F32) for i in range(nb) for piece in range(pieces)],
            axis=0,
        )
        mean = got[:, :rows] * (BOUND / STEPS)
        put_key(kmr2[level], mean, pltpu.roll(mean, width, 1), bias, slice(0, LEAF))
        put_value(vvr2[level], got[:, rows:].T * (BOUND * 2**level / STEPS), mass, slice(0, LEAF))
        for h in range(heads):
            far_score(kmr2[level][h], qr[level][h], slot % 2, h, fbr[level])
        for h in range(heads):
            far_soft([vvr2[level][h]], slot % 2, h, fbr[level], for_[level])

    def up(z):
        return dot(jnp.concatenate(split(z), axis=1), uu[...])

    def with_best(acc, best):
        return jnp.concatenate([acc[: size - 8], jnp.broadcast_to(best, (8, acc.shape[1]))], axis=0)

    def merge(acc, best, z):
        old = z[size - 8 : size - 7]
        new = jnp.maximum(best, old)
        both = acc * jnp.exp2(best - new) + z * jnp.exp2(old - new)
        return with_best(both, new)

    for h in range(heads):
        z = None
        for level in reversed(far_levels):
            acc, best = for_[level][h], fbr[level][h, 0:1]
            if z is None:
                z = with_best(acc, best)
            else:
                z = jnp.concatenate(
                    [up(z[:, j * LANES : (j + 1) * LANES]) for j in range(z.shape[1] // LANES)], axis=1
                )[:, : acc.shape[1]]
                z = merge(acc, best, z)
        if z is not None:
            for j in range(z.shape[1] // LANES):
                zb[h, j] = z[:, j * LANES : (j + 1) * LANES]
        for level in reversed(near_levels):
            for i in reversed(range(leaves >> level)):
                block = base_of[level] + i
                acc, best = fo[block, h], fb[block, h, 0:1]
                if z is None:
                    x = with_best(acc, best)
                else:
                    x = merge(acc, best, up(zb[h, i]))
                zb[h, 2 * i] = x[:, :LANES]
                zb[h, 2 * i + 1] = x[:, LANES:]
            z = True
        for n in range(leaves):
            cols = slice(n * LEAF, (n + 1) * LEAF)
            part = slice(h * width, (h + 1) * width)
            near_best, near_total = stat[2 * h : 2 * h + 1, cols], stat[2 * h + 1 : 2 * h + 2, cols]
            z = up(zb[h, n])
            old = z[size - 8 : size - 7]
            new = jnp.maximum(near_best, old)
            mine, other = jnp.exp2(near_best - new), jnp.exp2(old - new)
            inverse = 1.0 / (near_total * mine + z[width : width + 1] * other)
            out[part, cols] = (num[part, cols] * (mine * inverse) + z[:width] * (other * inverse)).astype(BF)

    @pl.when(has_left)
    def _():
        for copy in halo(0):
            copy.wait_send()

    @pl.when(has_right)
    def _():
        for copy in halo(1):
            copy.wait_send()

    for level in far_levels:
        for piece in range(fp[level].shape[0]):
            for copy in far_copies(level, piece):
                copy.wait_send()


def shards(q_heads, k_heads, v_heads, morton_order, leaf_counts):
    heads_real, width, tokens = q_heads.shape
    heads = heads_real + heads_real % 2
    seq_count = lax.axis_size("seq")
    rows = heads * width
    flat = []
    for x in (q_heads, k_heads, v_heads):
        if heads != heads_real:
            x = jnp.concatenate([x, jnp.zeros_like(x[:1])], axis=0)
        flat.append(x.reshape(rows, tokens))
    leaves, depth_local, near_levels, far_levels = plan(tokens, seq_count)
    size = width + PAD
    near_blocks = sum(leaves >> l for l in near_levels)
    pieced = [l for l in far_levels if (LEAF >> l) >= 8]
    unit_rows = lambda which: max(sum(max(LEAF >> l, 16) for l in which), 16)
    pieces = lambda l: leaves // 2 if l in pieced else 1
    vm = pltpu.VMEM
    scratch = [
        vm(morton_order.shape, I32),
        pltpu.SMEM(leaf_counts.shape, I32),
        vm((3 * rows, tokens), BF),
        vm((tokens + 2 * LEAF, rows), BF),
        vm((heads, tokens + 2 * LEAF, LANES), BF),
        vm((rows, tokens + 2 * LEAF), BF),
        vm((heads, 4 * width, tokens), BF),
        vm((2 * rows + PAD, tokens), BF),
        vm((tokens, 3 * rows), BF),
        vm((2, LEAF, LEAF), BF),
        vm((leaves // 2, 2 * LEAF, LANES * len(far_levels)), BF),
        vm((unit_rows(near_levels), LEAF), BF),
        vm((unit_rows(pieced), LEAF), BF),
        vm((LEAF, LEAF), BF),
        vm((near_blocks, heads, 4 * width, LEAF), BF),
        vm((near_blocks, heads, LEAF, 2 * rows), BF),
        vm((near_blocks, heads, size + width, LEAF), BF),
        vm((near_blocks, heads, size, LEAF), F32),
        vm((near_blocks, heads, 8, LEAF), F32),
        vm((leaves // 2, rows, LANES * len(far_levels)), F32),
        vm((2, heads, 3 * LEAF, LEAF), F32),
        vm((2, heads, 8, LEAF), F32),
        vm((rows, tokens), F32),
        vm((2 * heads + (-2 * heads) % 8, tokens), F32),
        vm((heads, leaves, size, LANES), F32),
    ]
    scratch += [vm((heads, 4 * width, padded(tokens, l)), BF) for l in far_levels]
    scratch += [vm((heads, LEAF, 2 * rows), BF) for l in far_levels]
    scratch += [vm((heads, size + width, LEAF), BF) for l in far_levels]
    scratch += [vm((heads, size, padded(tokens, l)), F32) for l in far_levels]
    scratch += [vm((heads, 8, padded(tokens, l)), F32) for l in far_levels]
    sent = lambda l: (pieces(l), (tokens >> l) // pieces(l), 2 * rows)
    scratch += [vm(sent(l), I16) for l in far_levels]
    scratch += [vm((1 << (l - depth_local), *sent(l)), I16) for l in far_levels]
    sem = pltpu.SemaphoreType.DMA
    scratch += [sem((5,)), sem((4,)), sem((4,))]
    scratch += [sem((pieces(l) << (l - depth_local),)) for l in far_levels] * 2
    scratch += [vm((tokens >> l, tokens), BF) for l in far_levels if (LEAF >> l) < 8]
    out = pl.pallas_call(
        functools.partial(kernel, (heads, width, tokens, seq_count)),
        out_shape=pltpu.VMEM((rows, tokens), BF),
        in_specs=[pl.BlockSpec(memory_space=pltpu.HBM)] * 5,
        out_specs=pl.BlockSpec(memory_space=pltpu.VMEM),
        scratch_shapes=scratch,
        compiler_params=pltpu.CompilerParams(
            collective_id=0, has_side_effects=True, vmem_limit_bytes=VMEM_LIMIT
        ),
    )(*flat, morton_order, leaf_counts)
    return out.reshape(heads, width, tokens)[:heads_real]


def solution(mesh):
    placed = (
        P("head", None, ("grp", "seq")),
        P("head", None, ("grp", "seq")),
        P("head", None, ("grp", "seq")),
        P(("grp", "seq"), None),
        P("grp"),
    )
    return jax.shard_map(
        shards,
        mesh=mesh,
        in_specs=placed,
        out_specs=P("head", None, ("grp", "seq")),
        check_vma=False,
    )
```

```python
import functools
import math

import jax
import jax.numpy as jnp
from jax import lax
from jax.experimental import pallas as pl
from jax.experimental.pallas import tpu as pltpu
from jax.sharding import PartitionSpec as P

LEAF = 256
LANES = 128
NEG = -1e30
BF = jnp.bfloat16
F32 = jnp.float32
I32 = jnp.int32
I16 = jnp.int16
PAD = 16
BOUND = 10.0
STEPS = 32700.0
VMEM_LIMIT = 63488 * 1024


def dot(a, b, dims=((1,), (0,))):
    return lax.dot_general(a, b, (dims, ((), ())), preferred_element_type=F32)


def split(x):
    hi = x.astype(BF)
    return hi, (x - hi.astype(F32)).astype(BF)


def iota(shape, dim):
    return lax.broadcasted_iota(I32, shape, dim)


def fixed(x, bound):
    return jnp.floor(x * (STEPS / bound) + 0.5).astype(I32).astype(I16)


def unfixed(x, bound):
    return x.astype(I32).astype(F32) * (bound / STEPS)


def plan(tokens, seq_count):
    leaves = tokens // LEAF
    depth_local = leaves.bit_length() - 1
    depth_all = (leaves * seq_count).bit_length() - 1
    levels = list(range(1, depth_all))
    near_levels = [l for l in levels if l < depth_local]
    far_levels = [l for l in levels if l >= depth_local]
    return leaves, depth_local, near_levels, far_levels


def padded(tokens, level):
    return max(LANES, tokens >> level)


def kernel(cfg, *refs):
    heads, width, tokens, seq_count = cfg
    rows = heads * width
    leaves, depth_local, near_levels, far_levels = plan(tokens, seq_count)
    pairs = leaves // 2
    scale = math.log2(math.e) / math.sqrt(width)
    size = width + PAD
    refs = list(refs)
    take = lambda n: [refs.pop(0) for _ in range(n)]
    q_hbm, k_hbm, v_hbm, order_hbm, counts_hbm, out = take(6)
    order, counts = take(2)
    xin, ka, kb, vx, qx, xp, kv = take(7)
    w1, w3, ua, uf, uu = take(5)
    qf, kmf, vvf, fo, fb = take(5)
    pf = take(1)[0]
    ss, sb, num, stat, zb = take(5)
    per_far = lambda: dict(zip(far_levels, take(len(far_levels))))
    qr, kmr2, vvr2, for_, fbr, fp, fr = (per_far() for _ in range(7))
    in_sem, halo_send, halo_recv = take(3)
    far_send, far_recv = per_far(), per_far()
    us = dict(zip([l for l in far_levels if (LEAF >> l) < 8], refs))
    pieced = [l for l in far_levels if l not in us]

    seq = lax.axis_index("seq")
    has_left, has_right = seq > 0, seq < seq_count - 1

    loads = [
        pltpu.make_async_copy(src, xin.at[pl.ds(i * rows, rows)], in_sem.at[i])
        for i, src in enumerate((q_hbm, k_hbm, v_hbm))
    ]
    loads.append(pltpu.make_async_copy(order_hbm, order, in_sem.at[3]))
    loads.append(pltpu.make_async_copy(counts_hbm, counts, in_sem.at[4]))
    for load in loads:
        load.start()
    barrier = pltpu.get_barrier_semaphore()
    for step in range(1, seq_count):
        other = lax.rem(seq + step, seq_count)
        pl.semaphore_signal(
            barrier, inc=1, device_id={"seq": other}, device_id_type=pl.DeviceIdType.MESH
        )

    @pl.when(jnp.logical_not(has_left))
    def _():
        ka[0:LEAF, :] = jnp.zeros((LEAF, rows), BF)
        vx[:, 0:LEAF] = jnp.zeros((rows, LEAF), BF)

    @pl.when(jnp.logical_not(has_right))
    def _():
        ka[tokens + LEAF :, :] = jnp.zeros((LEAF, rows), BF)
        vx[:, tokens + LEAF :] = jnp.zeros((rows, LEAF), BF)

    def count_of(n):
        leaf = seq * leaves + n
        total = leaves * seq_count
        inside = jnp.logical_and(leaf >= 0, leaf < total)
        return jnp.where(inside, counts[jnp.clip(leaf, 0, total - 1)], 0)

    def ones_where(mask):
        return jnp.where(mask, 1.0, 0.0).astype(BF)

    t = iota((LEAF, LEAF), 0)
    c = iota((LEAF, LEAF), 1)
    for p in range(2):
        w1[p] = ones_where(
            jnp.logical_or(
                jnp.logical_and(c < LANES, (t >> 1) == c),
                jnp.logical_and(c >= LANES, (t >> 2) + 64 * p == c - LANES),
            )
        )
    uu[...] = ones_where((c >> 1) == (t & (LANES - 1)))
    for i, level in enumerate(far_levels):
        t2 = iota((2 * LEAF, LANES), 0)
        c2 = iota((2 * LEAF, LANES), 1)
        for m in range(pairs):
            w3[m, :, i * LANES : (i + 1) * LANES] = ones_where(
                ((t2 + 2 * LEAF * m) >> level) & (LANES - 1) == c2
            )
    ua_at, uf_at = {}, {}
    for ref, spots, which in ((ua, ua_at, near_levels), (uf, uf_at, pieced)):
        at = 0
        for level in which:
            n = max(LEAF >> level, 16)
            spots[level] = at
            ref[at : at + n, :] = ones_where((iota((n, LEAF), 1) >> level) == iota((n, LEAF), 0))
            at += n
    for level, u in us.items():
        u[...] = ones_where((iota(u.shape, 1) >> level) == iota(u.shape, 0))

    def tail_rows(cols):
        r = iota((64, cols), 0)
        return ones_where(r == 0)

    for h in range(heads):
        off = (1 - h) * width
        qx[h, off : off + width, :] = jnp.zeros((width, tokens), BF)
        qx[h, 3 * width :, :] = tail_rows(tokens)
        for i in range(qf.shape[0]):
            qf[i, h, 3 * width :, :] = tail_rows(LEAF)
        for level in far_levels:
            qr[level][h, 3 * width :, :] = tail_rows(qr[level].shape[2])

    for load in loads:
        load.wait()

    lane_lo = iota((LEAF, LANES), 1) < width
    lane_is = iota((LEAF, LANES), 1) == width

    def key_tail(key_t, bias):
        shape = key_t.shape
        lo = iota(shape, 1) < width
        at = iota(shape, 1) == width
        rest = jnp.where(at, bias, 0.0)
        rolled = pltpu.roll(key_t, width, 1)
        return jnp.where(lo, key_t, rest), jnp.where(lo, rolled, rest), rolled

    def leaf_bias(count):
        return jnp.where(iota((LEAF, LANES), 0) < count, 0.0, NEG)

    def permute(m):
        for p in range(2):
            n = 2 * m + p
            at = pl.multiple_of(n * LEAF, LEAF)
            picks = order[0:1, pl.ds(at, LEAF)]
            spots = iota((tokens, LEAF), 0)
            hot = jnp.where(spots == picks, 1.0, 0.0).astype(BF)
            moved = dot(xin[...], hot)
            count = count_of(n)
            query, key, value = moved[:rows], moved[rows : 2 * rows], moved[2 * rows :]
            key_t = key.T
            on_row = iota((rows, LEAF), 1) < count
            on_col = iota((LEAF, rows), 0) < count
            tail0, tail1, rolled = key_tail(key_t, leaf_bias(count))
            ka[pl.ds(at + LEAF, LEAF), :] = key_t.astype(BF)
            kb[0, pl.ds(at + LEAF, LEAF), :] = tail0.astype(BF)
            kb[1, pl.ds(at + LEAF, LEAF), :] = tail1.astype(BF)
            kv[pl.ds(at, LEAF), 0:rows] = jnp.where(on_col, rolled, 0.0).astype(BF)
            kv[pl.ds(at, LEAF), rows : 2 * rows] = jnp.where(on_col, key_t, 0.0).astype(BF)
            kv[pl.ds(at, LEAF), 2 * rows :] = jnp.where(on_col, value.T, 0.0).astype(BF)
            vx[:, pl.ds(at + LEAF, LEAF)] = value.astype(BF)
            xp[0:rows, pl.ds(at, LEAF)] = query.astype(BF)
            xp[rows : 2 * rows, pl.ds(at, LEAF)] = jnp.where(on_row, value, 0.0).astype(BF)
            xp[2 * rows :, pl.ds(at, LEAF)] = ones_where(on_row[:PAD])
            hi, lo = split(query * scale)
            for h in range(heads):
                part = slice(h * width, (h + 1) * width)
                qx[h, part, pl.ds(at, LEAF)] = hi[part]
                qx[h, 2 * width : 3 * width, pl.ds(at, LEAF)] = lo[part]

    def put_query(ref, x, factor, where):
        hi, lo = split(x * factor)
        for h in range(heads):
            part = slice(h * width, (h + 1) * width)
            ref[h, 0:width, where] = hi[part]
            ref[h, width : 2 * width, where] = hi[part]
            ref[h, 2 * width : 3 * width, where] = lo[part]

    def put_value(ref, x, mass, where):
        hi, lo = split(x)
        for h in range(heads):
            part = slice(h * width, (h + 1) * width)
            ref[h, 0:width, where] = hi[part]
            ref[h, width:size, where] = mass.astype(BF)
            ref[h, size:, where] = lo[part]

    def put_key(ref, a, b, bias, where):
        lo_lane = iota(a.shape, 1) < width
        bias_lane = iota(a.shape, 1) == width
        a_hi, b_hi = a.astype(BF).astype(F32), b.astype(BF).astype(F32)
        rest = jnp.where(bias_lane, bias, 0.0)
        ref[0, where, 0:rows] = jnp.where(lo_lane, a_hi, b - b_hi).astype(BF)
        ref[0, where, rows:] = jnp.where(lo_lane, a_hi, rest).astype(BF)
        ref[1, where, 0:rows] = jnp.where(lo_lane, b_hi, a - a_hi).astype(BF)
        ref[1, where, rows:] = jnp.where(lo_lane, b_hi, rest).astype(BF)

    def clip_mass(count, at, g):
        return jnp.clip(count - at, 0, g).astype(F32)

    base_of, first = {}, 0
    for level in near_levels:
        base_of[level] = first
        first += leaves >> level

    def pool_far(m):
        if not pieced:
            return
        start = pl.multiple_of(m * 2 * LEAF, 2 * LEAF)
        kk = []
        for p in range(2):
            at = pl.multiple_of(start + p * LEAF, LEAF)
            kk.append(dot(uf[...], kv[pl.ds(at, LEAF), rows:]))
        for level in pieced:
            count = LEAF >> level
            x = jnp.concatenate([k[uf_at[level] : uf_at[level] + count] for k in kk], axis=0)
            mass = [
                clip_mass(count_of(2 * m + p), iota((count, LANES), 0) << level, 1 << level)
                for p in range(2)
            ]
            mean = x[:, :rows] / jnp.maximum(jnp.concatenate(mass, axis=0), 1.0)
            fp[level][m, :, 0:rows] = fixed(mean, BOUND)
            fp[level][m, :, rows:] = fixed(x[:, rows:], BOUND * 2**level)

    def pool_near(m):
        start = pl.multiple_of(m * 2 * LEAF, 2 * LEAF)
        t1, kk = [], []
        for p in range(2):
            at = pl.multiple_of(start + p * LEAF, LEAF)
            t1.append(dot(xp[0 : 2 * rows, pl.ds(at, LEAF)], w1[p]))
            kk.append(dot(ua[...], kv[pl.ds(at, LEAF), 0 : 2 * rows]))
        if far_levels:
            pf[m] = dot(xp[0:rows, pl.ds(start, 2 * LEAF)], w3[m])
        n = [count_of(2 * m), count_of(2 * m + 1)]
        b1 = base_of[1] + m
        lane = iota((PAD, LANES), 1)
        for p in range(2):
            where = slice(p * LANES, (p + 1) * LANES)
            put_query(qf.at[b1], t1[p][:rows, :LANES], scale / 2, where)
            put_value(vvf.at[b1], t1[p][rows:, :LANES], clip_mass(n[p], lane << 1, 2), where)
        if 2 in near_levels:
            b2 = base_of[2] + m // 2
            x2 = t1[0][:, LANES:] + t1[1][:, LANES:]
            where = pl.ds(pl.multiple_of((m % 2) * LANES, LANES), LANES)
            mass = jnp.where(
                lane < 64, clip_mass(n[0], lane << 2, 4), clip_mass(n[1], (lane - 64) << 2, 4)
            )
            put_query(qf.at[b2], x2[:rows], scale / 4, where)
            put_value(vvf.at[b2], x2[rows:], mass, where)
        for p in range(2):
            for level in near_levels:
                count = LEAF >> level
                x = kk[p][ua_at[level] : ua_at[level] + count]
                mass = clip_mass(n[p], iota((count, LANES), 0) << level, 1 << level)
                inverse = 1.0 / jnp.maximum(mass, 1.0)
                b, a = x[:, :rows] * inverse, x[:, rows:] * inverse
                bias = jnp.where(mass > 0, 0.0, NEG)
                if level == 1:
                    put_key(kmf.at[b1], a, b, bias, slice(p * count, (p + 1) * count))
                else:
                    spot = pl.multiple_of((m % 2) * LANES + p * count, count)
                    put_key(kmf.at[b2], a, b, bias, pl.ds(spot, count))

    def remote(src, dst, send, recv, target):
        return pltpu.make_async_remote_copy(
            src_ref=src,
            dst_ref=dst,
            send_sem=send,
            recv_sem=recv,
            device_id={"seq": target},
            device_id_type=pl.DeviceIdType.MESH,
        )

    def halo(side):
        start, end = (LEAF, tokens + LEAF) if side == 0 else (tokens, 0)
        target = jnp.maximum(seq - 1, 0) if side == 0 else jnp.minimum(seq + 1, seq_count - 1)
        return (
            remote(
                ka.at[pl.ds(start, LEAF)],
                ka.at[pl.ds(end, LEAF)],
                halo_send.at[2 * side],
                halo_recv.at[2 * side],
                target,
            ),
            remote(
                vx.at[:, pl.ds(start, LEAF)],
                vx.at[:, pl.ds(end, LEAF)],
                halo_send.at[2 * side + 1],
                halo_recv.at[2 * side + 1],
                target,
            ),
        )

    def pair_at(i):
        return jnp.where(i == 0, 0, jnp.where(i == 1, pairs - 1, i - 1))

    def far_copies(level, piece):
        bit = level - depth_local
        nb = 1 << bit
        pieces = fp[level].shape[0]
        slot = lax.rem(seq, nb)
        base = ((seq >> bit) ^ 1) << bit
        return [
            remote(
                fp[level].at[piece],
                fr[level].at[slot, piece],
                far_send[level].at[j * pieces + piece],
                far_recv[level].at[slot * pieces + piece],
                base + j,
            )
            for j in range(nb)
        ]

    permute(0)

    @pl.loop(1, pairs)
    def _(i):
        pool_far(pair_at(i - 1))
        permute(pair_at(i))

        @pl.when(i == 1)
        def _():
            pl.semaphore_wait(barrier, seq_count - 1)

        @pl.when(jnp.logical_and(i == 1, has_left))
        def _():
            for copy in halo(0):
                copy.start()

        @pl.when(jnp.logical_and(i == 1, has_right))
        def _():
            for copy in halo(1):
                copy.start()

        for level in reversed(pieced):
            for copy in far_copies(level, pair_at(i - 1)):
                copy.start()

    pool_far(pair_at(pairs - 1))
    for level in reversed(pieced):
        for copy in far_copies(level, pair_at(pairs - 1)):
            copy.start()
    for level in us:
        sums = dot(us[level][...], kv[:, rows:])
        valid = jnp.broadcast_to(xp[2 * rows : 2 * rows + 1, :], (LANES, tokens))
        mass = dot(us[level][...], valid, ((1,), (1,)))
        fp[level][0, :, 0:rows] = fixed(sums[:, :rows] / jnp.maximum(mass, 1.0), BOUND)
        fp[level][0, :, rows:] = fixed(sums[:, rows:], BOUND * 2**level)
        for copy in far_copies(level, 0):
            copy.start()

    @pl.loop(0, pairs, unroll=2)
    def _(m):
        pool_near(m)

    for i, level in enumerate(far_levels):
        pieces = max((tokens >> level) // LANES, 1)
        per = pairs // pieces
        cols = slice(i * LANES, (i + 1) * LANES)
        for j in range(pieces):
            x = sum(pf[j * per + e, :, cols] for e in range(per))
            put_query(qr[level], x, scale / 2**level, slice(j * LANES, (j + 1) * LANES))

    def far_score(km, q, slot, h, best_ref):
        s = dot(km, q)
        keys, cols = s.shape
        ss[slot, h, 0:keys, 0:cols] = s
        best = jnp.max(s.reshape(keys // 8, 8, cols), axis=0)
        best = jnp.max(best, axis=0, keepdims=True).astype(BF).astype(F32)
        best_ref[h] = jnp.broadcast_to(best, (8, cols))

    def far_soft(vvs, slot, h, best_ref, out_ref):
        cols = best_ref.shape[2]
        best = best_ref[h]
        step, acc = 0, None
        for vv in vvs:
            keys = vv.shape[1]
            x = ss[slot, h, step : step + keys, 0:cols].reshape(keys // 8, 8, cols)
            w = jnp.exp2(x - best[None]).reshape(keys, cols)
            w_hi, w_lo = split(w)
            both = dot(vv, w_hi)
            low = jnp.concatenate([both[size:], jnp.zeros((PAD, cols), F32)], axis=0)
            term = both[:size] + low + dot(vv[:size], w_lo)
            acc = term if acc is None else acc + term
            step += keys
        out_ref[h] = acc

    def local_score(i, slot, h):
        far_score(kmf[i ^ 1, h], qf[i, h], slot, h, fb.at[i])

    def local_soft(i, slot, h):
        far_soft([vvf[i ^ 1, h]], slot, h, fb.at[i], fo.at[i])

    for h in range(heads):
        local_score(0, 0, h)

    @pl.loop(0, first // 2)
    def _(b):
        for j in range(2):
            i = 2 * b + j
            for h in range(heads):
                local_soft(i, j, h)
                local_score(jnp.minimum(i + 1, first - 1), 1 - j, h)

    @pl.when(has_right)
    def _():
        for copy in halo(0):
            copy.wait_recv()

    @pl.when(has_left)
    def _():
        for copy in halo(1):
            copy.wait_recv()

    for n, at in ((-1, 0), (leaves, tokens + LEAF)):
        tail0, tail1, _ = key_tail(ka[at : at + LEAF, :].astype(F32), leaf_bias(count_of(n)))
        kb[0, at : at + LEAF, :] = tail0.astype(BF)
        kb[1, at : at + LEAF, :] = tail1.astype(BF)

    def near_score(n, slot, h):
        at = pl.multiple_of(n * LEAF, LEAF)
        best = None
        for j in range(3):
            key_rows = pl.ds(pl.multiple_of(at + j * LEAF, LEAF), LEAF)
            left = jnp.concatenate([ka[key_rows, :], kb[h, key_rows, :]], axis=1)
            s = dot(left, qx[h, :, pl.ds(at, LEAF)])
            ss[slot, h, j * LEAF : (j + 1) * LEAF, :] = s
            top = jnp.max(s.reshape(LEAF // 8, 8, LEAF), axis=0)
            best = top if best is None else jnp.maximum(best, top)
        sb[slot, h] = jnp.broadcast_to(jnp.max(best, axis=0, keepdims=True), (8, LEAF))

    def near_soft(n, slot, h):
        at = pl.multiple_of(n * LEAF, LEAF)
        best = sb[slot, h]
        total, acc = None, None
        part = slice(h * width, (h + 1) * width)
        for j in range(3):
            x = ss[slot, h, j * LEAF : (j + 1) * LEAF, :].reshape(LEAF // 8, 8, LEAF)
            w = jnp.exp2(x - best[None])
            term = jnp.sum(w, axis=0)
            total = term if total is None else total + term
            keys = pl.ds(pl.multiple_of(at + j * LEAF, LEAF), LEAF)
            term = dot(vx[part, keys], w.reshape(LEAF, LEAF).astype(BF))
            acc = term if acc is None else acc + term
        num[part, pl.ds(at, LEAF)] = acc
        stat[2 * h : 2 * h + 1, pl.ds(at, LEAF)] = best[0:1]
        stat[2 * h + 1 : 2 * h + 2, pl.ds(at, LEAF)] = jnp.sum(total, axis=0, keepdims=True)

    for h in range(heads):
        near_score(0, 0, h)

    @pl.loop(0, leaves // 4)
    def _(i):
        for j in range(4):
            n = 4 * i + j
            for h in range(heads):
                near_soft(n, j % 2, h)
                near_score(jnp.minimum(n + 1, leaves - 1), 1 - j % 2, h)

    for level in reversed(far_levels):
        pieces = fp[level].shape[0]
        for i in range(1 << (level - depth_local)):
            for piece in range(pieces):
                remote(
                    fp[level].at[piece], fr[level].at[i, piece],
                    far_send[level].at[i * pieces + piece], far_recv[level].at[i * pieces + piece], seq,
                ).wait_recv()

    def unpack(level):
        bit = level - depth_local
        nb = 1 << bit
        base = ((seq >> bit) ^ 1) << bit
        lane = iota((PAD, LEAF), 1)
        count = jnp.zeros((PAD, LEAF), I32)
        for leaf in range(leaves * nb):
            count = jnp.where((lane << level) >> 8 == leaf, counts[base * leaves + leaf], count)
        mass = clip_mass(count, (lane << level) & (LEAF - 1), 1 << level)
        mass_col = dot(mass.astype(BF), jnp.ones((PAD, LANES), BF), ((0,), (0,)))
        bias = jnp.where(mass_col > 0, 0.0, NEG)
        got = jnp.concatenate(
            [
                fr[level][i, piece].astype(I32).astype(F32)
                for i in range(nb)
                for piece in range(fp[level].shape[0])
            ],
            axis=0,
        )
        mean = got[:, :rows] * (BOUND / STEPS)
        put_key(kmr2[level], mean, pltpu.roll(mean, width, 1), bias, slice(0, LEAF))
        put_value(vvr2[level], got[:, rows:].T * (BOUND * 2**level / STEPS), mass, slice(0, LEAF))

    for first_level in range(0, len(far_levels), 2):
        group = list(reversed(far_levels))[first_level : first_level + 2]
        for level in group:
            unpack(level)
        for slot, level in enumerate(group):
            for h in range(heads):
                far_score(kmr2[level][h], qr[level][h], slot, h, fbr[level])
        for slot, level in enumerate(group):
            for h in range(heads):
                far_soft([vvr2[level][h]], slot, h, fbr[level], for_[level])

    def up(z):
        return dot(jnp.concatenate(split(z), axis=1), uu[...])

    def with_best(acc, best):
        return jnp.concatenate([acc[: size - 8], jnp.broadcast_to(best, (8, acc.shape[1]))], axis=0)

    def merge(acc, best, z):
        old = z[size - 8 : size - 7]
        new = jnp.maximum(best, old)
        both = acc * jnp.exp2(best - new) + z * jnp.exp2(old - new)
        return with_best(both, new)

    def tiles(z):
        return [z[:, j * LANES : (j + 1) * LANES] for j in range(z.shape[1] // LANES)]

    zs = [None] * heads
    for level in reversed(far_levels):
        for h in range(heads):
            acc, best = for_[level][h], fbr[level][h, 0:1]
            if zs[h] is None:
                zs[h] = with_best(acc, best)
            else:
                z = jnp.concatenate([up(x) for x in tiles(zs[h])], axis=1)
                zs[h] = merge(acc, best, z[:, : acc.shape[1]])
    zs = [None if z is None else tiles(z) for z in zs]
    for level in reversed(near_levels):
        new = [[] for _ in range(heads)]
        for i in range(leaves >> level):
            for h in range(heads):
                block = base_of[level] + i
                acc, best = fo[block, h], fb[block, h, 0:1]
                x = with_best(acc, best) if zs[h] is None else merge(acc, best, up(zs[h][i]))
                for j, part in enumerate(tiles(x)):
                    zb[level % 2, h, 2 * i + j] = part
                    new[h].append(zb.at[level % 2, h, 2 * i + j])
        zs = [[ref[...] for ref in refs_h] for refs_h in new]
    for n in range(leaves):
        for h in range(heads):
            cols = slice(n * LEAF, (n + 1) * LEAF)
            part = slice(h * width, (h + 1) * width)
            near_best, near_total = stat[2 * h : 2 * h + 1, cols], stat[2 * h + 1 : 2 * h + 2, cols]
            z = up(zs[h][n])
            old = z[size - 8 : size - 7]
            new_best = jnp.maximum(near_best, old)
            mine, other = jnp.exp2(near_best - new_best), jnp.exp2(old - new_best)
            inverse = 1.0 / (near_total * mine + z[width : width + 1] * other)
            out[part, cols] = (num[part, cols] * (mine * inverse) + z[:width] * (other * inverse)).astype(BF)

    @pl.when(has_left)
    def _():
        for copy in halo(0):
            copy.wait_send()

    @pl.when(has_right)
    def _():
        for copy in halo(1):
            copy.wait_send()

    for level in far_levels:
        for piece in range(fp[level].shape[0]):
            for copy in far_copies(level, piece):
                copy.wait_send()


def shards(q_heads, k_heads, v_heads, morton_order, leaf_counts):
    heads_real, width, tokens = q_heads.shape
    heads = heads_real + heads_real % 2
    seq_count = lax.axis_size("seq")
    rows = heads * width
    flat = []
    for x in (q_heads, k_heads, v_heads):
        if heads != heads_real:
            x = jnp.concatenate([x, jnp.zeros_like(x[:1])], axis=0)
        flat.append(x.reshape(rows, tokens))
    leaves, depth_local, near_levels, far_levels = plan(tokens, seq_count)
    size = width + PAD
    near_blocks = sum(leaves >> l for l in near_levels)
    pieced = [l for l in far_levels if (LEAF >> l) >= 8]
    unit_rows = lambda which: max(sum(max(LEAF >> l, 16) for l in which), 16)
    pieces = lambda l: leaves // 2 if l in pieced else 1
    vm = pltpu.VMEM
    scratch = [
        vm(morton_order.shape, I32),
        pltpu.SMEM(leaf_counts.shape, I32),
        vm((3 * rows, tokens), BF),
        vm((tokens + 2 * LEAF, rows), BF),
        vm((heads, tokens + 2 * LEAF, LANES), BF),
        vm((rows, tokens + 2 * LEAF), BF),
        vm((heads, 4 * width, tokens), BF),
        vm((2 * rows + PAD, tokens), BF),
        vm((tokens, 3 * rows), BF),
        vm((2, LEAF, LEAF), BF),
        vm((leaves // 2, 2 * LEAF, LANES * len(far_levels)), BF),
        vm((unit_rows(near_levels), LEAF), BF),
        vm((unit_rows(pieced), LEAF), BF),
        vm((LEAF, LEAF), BF),
        vm((near_blocks, heads, 4 * width, LEAF), BF),
        vm((near_blocks, heads, LEAF, 2 * rows), BF),
        vm((near_blocks, heads, size + width, LEAF), BF),
        vm((near_blocks, heads, size, LEAF), F32),
        vm((near_blocks, heads, 8, LEAF), F32),
        vm((leaves // 2, rows, LANES * len(far_levels)), F32),
        vm((2, heads, 3 * LEAF, LEAF), F32),
        vm((2, heads, 8, LEAF), F32),
        vm((rows, tokens), F32),
        vm((2 * heads + (-2 * heads) % 8, tokens), F32),
        vm((2, heads, leaves, size, LANES), F32),
    ]
    scratch += [vm((heads, 4 * width, padded(tokens, l)), BF) for l in far_levels]
    scratch += [vm((heads, LEAF, 2 * rows), BF) for l in far_levels]
    scratch += [vm((heads, size + width, LEAF), BF) for l in far_levels]
    scratch += [vm((heads, size, padded(tokens, l)), F32) for l in far_levels]
    scratch += [vm((heads, 8, padded(tokens, l)), F32) for l in far_levels]
    sent = lambda l: (pieces(l), (tokens >> l) // pieces(l), 2 * rows)
    scratch += [vm(sent(l), I16) for l in far_levels]
    scratch += [vm((1 << (l - depth_local), *sent(l)), I16) for l in far_levels]
    sem = pltpu.SemaphoreType.DMA
    scratch += [sem((5,)), sem((4,)), sem((4,))]
    scratch += [sem((pieces(l) << (l - depth_local),)) for l in far_levels] * 2
    scratch += [vm((tokens >> l, tokens), BF) for l in far_levels if (LEAF >> l) < 8]
    out = pl.pallas_call(
        functools.partial(kernel, (heads, width, tokens, seq_count)),
        out_shape=pltpu.VMEM((rows, tokens), BF),
        in_specs=[pl.BlockSpec(memory_space=pltpu.HBM)] * 5,
        out_specs=pl.BlockSpec(memory_space=pltpu.VMEM),
        scratch_shapes=scratch,
        compiler_params=pltpu.CompilerParams(
            collective_id=0, has_side_effects=True, vmem_limit_bytes=VMEM_LIMIT
        ),
    )(*flat, morton_order, leaf_counts)
    return out.reshape(heads, width, tokens)[:heads_real]


def solution(mesh):
    placed = (
        P("head", None, ("grp", "seq")),
        P("head", None, ("grp", "seq")),
        P("head", None, ("grp", "seq")),
        P(("grp", "seq"), None),
        P("grp"),
    )
    return jax.shard_map(
        shards,
        mesh=mesh,
        in_specs=placed,
        out_specs=P("head", None, ("grp", "seq")),
        check_vma=False,
    )
```

```python
import functools
import math

import jax
import jax.numpy as jnp
from jax import lax
from jax.experimental import pallas as pl
from jax.experimental.pallas import tpu as pltpu
from jax.sharding import PartitionSpec as P

LEAF = 256
LANES = 128
NEG = -1e30
BF = jnp.bfloat16
F32 = jnp.float32
I32 = jnp.int32
I16 = jnp.int16
PAD = 16
BOUND = 10.0
STEPS = 32700.0
VMEM_LIMIT = 63488 * 1024


def dot(a, b, dims=((1,), (0,))):
    return lax.dot_general(a, b, (dims, ((), ())), preferred_element_type=F32)


def split(x):
    hi = x.astype(BF)
    return hi, (x - hi.astype(F32)).astype(BF)


def iota(shape, dim):
    return lax.broadcasted_iota(I32, shape, dim)


def fixed(x, bound):
    return jnp.floor(x * (STEPS / bound) + 0.5).astype(I32).astype(I16)


def unfixed(x, bound):
    return x.astype(I32).astype(F32) * (bound / STEPS)


def plan(tokens, seq_count):
    leaves = tokens // LEAF
    depth_local = leaves.bit_length() - 1
    depth_all = (leaves * seq_count).bit_length() - 1
    levels = list(range(1, depth_all))
    near_levels = [l for l in levels if l < depth_local]
    far_levels = [l for l in levels if l >= depth_local]
    return leaves, depth_local, near_levels, far_levels


def padded(tokens, level):
    return max(LANES, tokens >> level)


def kernel(cfg, *refs):
    heads, width, tokens, seq_count = cfg
    rows = heads * width
    leaves, depth_local, near_levels, far_levels = plan(tokens, seq_count)
    pairs = leaves // 2
    scale = math.log2(math.e) / math.sqrt(width)
    size = width + PAD
    refs = list(refs)
    take = lambda n: [refs.pop(0) for _ in range(n)]
    q_hbm, k_hbm, v_hbm, order_hbm, counts_hbm, out = take(6)
    order, counts = take(2)
    xin, ka, kb, vx, qx, xp, kv = take(7)
    w1, w3, ua, uf, uu = take(5)
    qf, kmf, vvf, fo, fb = take(5)
    pf = take(1)[0]
    ss, sb, num, stat, zb = take(5)
    per_far = lambda: dict(zip(far_levels, take(len(far_levels))))
    qr, kmr2, vvr2, for_, fbr, fp, fr = (per_far() for _ in range(7))
    in_sem, halo_send, halo_recv = take(3)
    far_send, far_recv = per_far(), per_far()
    us = dict(zip([l for l in far_levels if (LEAF >> l) < 8], refs))
    pieced = [l for l in far_levels if l not in us]

    seq = lax.axis_index("seq")
    has_left, has_right = seq > 0, seq < seq_count - 1

    loads = [
        pltpu.make_async_copy(src, xin.at[pl.ds(i * rows, rows)], in_sem.at[i])
        for i, src in enumerate((q_hbm, k_hbm, v_hbm))
    ]
    loads.append(pltpu.make_async_copy(order_hbm, order, in_sem.at[3]))
    loads.append(pltpu.make_async_copy(counts_hbm, counts, in_sem.at[4]))
    for load in loads:
        load.start()
    barrier = pltpu.get_barrier_semaphore()
    for step in range(1, seq_count):
        other = lax.rem(seq + step, seq_count)
        pl.semaphore_signal(
            barrier, inc=1, device_id={"seq": other}, device_id_type=pl.DeviceIdType.MESH
        )

    @pl.when(jnp.logical_not(has_left))
    def _():
        ka[0:LEAF, :] = jnp.zeros((LEAF, rows), BF)
        vx[:, 0:LEAF] = jnp.zeros((rows, LEAF), BF)

    @pl.when(jnp.logical_not(has_right))
    def _():
        ka[tokens + LEAF :, :] = jnp.zeros((LEAF, rows), BF)
        vx[:, tokens + LEAF :] = jnp.zeros((rows, LEAF), BF)

    def count_of(n):
        leaf = seq * leaves + n
        total = leaves * seq_count
        inside = jnp.logical_and(leaf >= 0, leaf < total)
        return jnp.where(inside, counts[jnp.clip(leaf, 0, total - 1)], 0)

    def ones_where(mask):
        return jnp.where(mask, 1.0, 0.0).astype(BF)

    t = iota((LEAF, LEAF), 0)
    c = iota((LEAF, LEAF), 1)
    for p in range(2):
        w1[p] = ones_where(
            jnp.logical_or(
                jnp.logical_and(c < LANES, (t >> 1) == c),
                jnp.logical_and(c >= LANES, (t >> 2) + 64 * p == c - LANES),
            )
        )
    uu[...] = ones_where((c >> 1) == (t & (LANES - 1)))
    for i, level in enumerate(far_levels):
        t2 = iota((2 * LEAF, LANES), 0)
        c2 = iota((2 * LEAF, LANES), 1)
        for m in range(pairs):
            w3[m, :, i * LANES : (i + 1) * LANES] = ones_where(
                ((t2 + 2 * LEAF * m) >> level) & (LANES - 1) == c2
            )
    ua_at, uf_at = {}, {}
    for ref, spots, which in ((ua, ua_at, near_levels), (uf, uf_at, pieced)):
        at = 0
        for level in which:
            n = max(LEAF >> level, 16)
            spots[level] = at
            ref[at : at + n, :] = ones_where((iota((n, LEAF), 1) >> level) == iota((n, LEAF), 0))
            at += n
    for level, u in us.items():
        u[...] = ones_where((iota(u.shape, 1) >> level) == iota(u.shape, 0))

    def tail_rows(cols):
        r = iota((64, cols), 0)
        return ones_where(r == 0)

    for h in range(heads):
        off = (1 - h) * width
        qx[h, off : off + width, :] = jnp.zeros((width, tokens), BF)
        qx[h, 3 * width :, :] = tail_rows(tokens)
        for i in range(qf.shape[0]):
            qf[i, h, 3 * width :, :] = tail_rows(LEAF)
        for level in far_levels:
            qr[level][h, 3 * width :, :] = tail_rows(qr[level].shape[2])

    for load in loads:
        load.wait()

    lane_lo = iota((LEAF, LANES), 1) < width
    lane_is = iota((LEAF, LANES), 1) == width

    def key_tail(key_t, bias):
        shape = key_t.shape
        lo = iota(shape, 1) < width
        at = iota(shape, 1) == width
        rest = jnp.where(at, bias, 0.0)
        rolled = pltpu.roll(key_t, width, 1)
        return jnp.where(lo, key_t, rest), jnp.where(lo, rolled, rest), rolled

    def leaf_bias(count):
        return jnp.where(iota((LEAF, LANES), 0) < count, 0.0, NEG)

    def permute(group):
        for n in group:
            at = n * LEAF
            picks = order[0:1, pl.ds(at, LEAF)]
            spots = iota((tokens, LEAF), 0)
            hot = jnp.where(spots == picks, 1.0, 0.0).astype(BF)
            moved = dot(xin[...], hot)
            count = count_of(n)
            query, key, value = moved[:rows], moved[rows : 2 * rows], moved[2 * rows :]
            key_t = key.T
            on_row = iota((rows, LEAF), 1) < count
            on_col = iota((LEAF, rows), 0) < count
            tail0, tail1, rolled = key_tail(key_t, leaf_bias(count))
            ka[pl.ds(at + LEAF, LEAF), :] = key_t.astype(BF)
            kb[0, pl.ds(at + LEAF, LEAF), :] = tail0.astype(BF)
            kb[1, pl.ds(at + LEAF, LEAF), :] = tail1.astype(BF)
            kv[pl.ds(at, LEAF), 0:rows] = jnp.where(on_col, rolled, 0.0).astype(BF)
            kv[pl.ds(at, LEAF), rows : 2 * rows] = jnp.where(on_col, key_t, 0.0).astype(BF)
            kv[pl.ds(at, LEAF), 2 * rows :] = jnp.where(on_col, value.T, 0.0).astype(BF)
            vx[:, pl.ds(at + LEAF, LEAF)] = value.astype(BF)
            xp[0:rows, pl.ds(at, LEAF)] = query.astype(BF)
            xp[rows : 2 * rows, pl.ds(at, LEAF)] = jnp.where(on_row, value, 0.0).astype(BF)
            xp[2 * rows :, pl.ds(at, LEAF)] = ones_where(on_row[:PAD])
            hi, lo = split(query * scale)
            for h in range(heads):
                part = slice(h * width, (h + 1) * width)
                qx[h, part, pl.ds(at, LEAF)] = hi[part]
                qx[h, 2 * width : 3 * width, pl.ds(at, LEAF)] = lo[part]

    def put_query(ref, x, factor, where):
        hi, lo = split(x * factor)
        for h in range(heads):
            part = slice(h * width, (h + 1) * width)
            ref[h, 0:width, where] = hi[part]
            ref[h, width : 2 * width, where] = hi[part]
            ref[h, 2 * width : 3 * width, where] = lo[part]

    def put_value(ref, x, mass, where):
        hi, lo = split(x)
        for h in range(heads):
            part = slice(h * width, (h + 1) * width)
            ref[h, 0:width, where] = hi[part]
            ref[h, width:size, where] = mass.astype(BF)
            ref[h, size:, where] = lo[part]

    def put_key(ref, a, b, bias, where):
        lo_lane = iota(a.shape, 1) < width
        bias_lane = iota(a.shape, 1) == width
        a_hi, b_hi = a.astype(BF).astype(F32), b.astype(BF).astype(F32)
        rest = jnp.where(bias_lane, bias, 0.0)
        ref[0, where, 0:rows] = jnp.where(lo_lane, a_hi, b - b_hi).astype(BF)
        ref[0, where, rows:] = jnp.where(lo_lane, a_hi, rest).astype(BF)
        ref[1, where, 0:rows] = jnp.where(lo_lane, b_hi, a - a_hi).astype(BF)
        ref[1, where, rows:] = jnp.where(lo_lane, b_hi, rest).astype(BF)

    def clip_mass(count, at, g):
        return jnp.clip(count - at, 0, g).astype(F32)

    base_of, first = {}, 0
    for level in near_levels:
        base_of[level] = first
        first += leaves >> level

    def pool_far(m):
        if not pieced:
            return
        start = m * 2 * LEAF
        kk = []
        for p in range(2):
            at = start + p * LEAF
            kk.append(dot(uf[...], kv[pl.ds(at, LEAF), rows:]))
        for level in pieced:
            count = LEAF >> level
            x = jnp.concatenate([k[uf_at[level] : uf_at[level] + count] for k in kk], axis=0)
            mass = [
                clip_mass(count_of(2 * m + p), iota((count, LANES), 0) << level, 1 << level)
                for p in range(2)
            ]
            mean = x[:, :rows] / jnp.maximum(jnp.concatenate(mass, axis=0), 1.0)
            fp[level][m, :, 0:rows] = fixed(mean, BOUND)
            fp[level][m, :, rows:] = fixed(x[:, rows:], BOUND * 2**level)

    def pool_near(m):
        start = m * 2 * LEAF
        t1, kk = [], []
        for p in range(2):
            at = start + p * LEAF
            t1.append(dot(xp[0 : 2 * rows, pl.ds(at, LEAF)], w1[p]))
            kk.append(dot(ua[...], kv[pl.ds(at, LEAF), 0 : 2 * rows]))
        if far_levels:
            pf[m] = dot(xp[0:rows, pl.ds(start, 2 * LEAF)], w3[m])
        n = [count_of(2 * m), count_of(2 * m + 1)]
        b1 = base_of[1] + m
        lane = iota((PAD, LANES), 1)
        for p in range(2):
            where = slice(p * LANES, (p + 1) * LANES)
            put_query(qf.at[b1], t1[p][:rows, :LANES], scale / 2, where)
            put_value(vvf.at[b1], t1[p][rows:, :LANES], clip_mass(n[p], lane << 1, 2), where)
        if 2 in near_levels:
            b2 = base_of[2] + m // 2
            x2 = t1[0][:, LANES:] + t1[1][:, LANES:]
            where = pl.ds((m % 2) * LANES, LANES)
            mass = jnp.where(
                lane < 64, clip_mass(n[0], lane << 2, 4), clip_mass(n[1], (lane - 64) << 2, 4)
            )
            put_query(qf.at[b2], x2[:rows], scale / 4, where)
            put_value(vvf.at[b2], x2[rows:], mass, where)
        for p in range(2):
            for level in near_levels:
                count = LEAF >> level
                x = kk[p][ua_at[level] : ua_at[level] + count]
                mass = clip_mass(n[p], iota((count, LANES), 0) << level, 1 << level)
                inverse = 1.0 / jnp.maximum(mass, 1.0)
                b, a = x[:, :rows] * inverse, x[:, rows:] * inverse
                bias = jnp.where(mass > 0, 0.0, NEG)
                if level == 1:
                    put_key(kmf.at[b1], a, b, bias, slice(p * count, (p + 1) * count))
                else:
                    spot = (m % 2) * LANES + p * count
                    put_key(kmf.at[b2], a, b, bias, pl.ds(spot, count))

    def remote(src, dst, send, recv, target):
        return pltpu.make_async_remote_copy(
            src_ref=src,
            dst_ref=dst,
            send_sem=send,
            recv_sem=recv,
            device_id={"seq": target},
            device_id_type=pl.DeviceIdType.MESH,
        )

    def halo(side):
        start, end = (LEAF, tokens + LEAF) if side == 0 else (tokens, 0)
        target = jnp.maximum(seq - 1, 0) if side == 0 else jnp.minimum(seq + 1, seq_count - 1)
        return (
            remote(
                ka.at[pl.ds(start, LEAF)],
                ka.at[pl.ds(end, LEAF)],
                halo_send.at[2 * side],
                halo_recv.at[2 * side],
                target,
            ),
            remote(
                vx.at[:, pl.ds(start, LEAF)],
                vx.at[:, pl.ds(end, LEAF)],
                halo_send.at[2 * side + 1],
                halo_recv.at[2 * side + 1],
                target,
            ),
        )

    def far_copies(level, piece):
        bit = level - depth_local
        nb = 1 << bit
        pieces = fp[level].shape[0]
        slot = lax.rem(seq, nb)
        base = ((seq >> bit) ^ 1) << bit
        return [
            remote(
                fp[level].at[piece],
                fr[level].at[slot, piece],
                far_send[level].at[j * pieces + piece],
                far_recv[level].at[slot * pieces + piece],
                base + j,
            )
            for j in range(nb)
        ]

    def send_far(m):
        for level in reversed(pieced):
            for copy in far_copies(level, m):
                copy.start()

    groups = [(0, leaves - 1), (1, leaves - 2)] + [(2 * m, 2 * m + 1) for m in range(1, pairs - 1)]
    ready = [[], []] + [[0, pairs - 1]] + [[m] for m in range(1, pairs - 1)]
    for step, group in enumerate(groups):
        for m in ready[step]:
            pool_far(m)
        permute(group)
        if step == 0:
            pl.semaphore_wait(barrier, seq_count - 1)

            @pl.when(has_left)
            def _():
                for copy in halo(0):
                    copy.start()

            @pl.when(has_right)
            def _():
                for copy in halo(1):
                    copy.start()

        for m in ready[step]:
            send_far(m)
    for m in ready[len(groups)]:
        pool_far(m)
    pool_near(0)
    for m in ready[len(groups)]:
        send_far(m)
    for level in us:
        sums = dot(us[level][...], kv[:, rows:])
        valid = jnp.broadcast_to(xp[2 * rows : 2 * rows + 1, :], (LANES, tokens))
        mass = dot(us[level][...], valid, ((1,), (1,)))
        fp[level][0, :, 0:rows] = fixed(sums[:, :rows] / jnp.maximum(mass, 1.0), BOUND)
        fp[level][0, :, rows:] = fixed(sums[:, rows:], BOUND * 2**level)
        for copy in far_copies(level, 0):
            copy.start()

    for m in range(1, pairs):
        pool_near(m)

    for i, level in enumerate(far_levels):
        pieces = max((tokens >> level) // LANES, 1)
        per = pairs // pieces
        cols = slice(i * LANES, (i + 1) * LANES)
        for j in range(pieces):
            x = sum(pf[j * per + e, :, cols] for e in range(per))
            put_query(qr[level], x, scale / 2**level, slice(j * LANES, (j + 1) * LANES))

    def far_score(km, q, slot, h, best_ref):
        s = dot(km, q)
        keys, cols = s.shape
        ss[slot, h, 0:keys, 0:cols] = s
        best = jnp.max(s.reshape(keys // 8, 8, cols), axis=0)
        best = jnp.max(best, axis=0, keepdims=True).astype(BF).astype(F32)
        best_ref[h] = jnp.broadcast_to(best, (8, cols))

    def far_soft(vvs, slot, h, best_ref, out_ref):
        cols = best_ref.shape[2]
        best = best_ref[h]
        step, acc = 0, None
        for vv in vvs:
            keys = vv.shape[1]
            x = ss[slot, h, step : step + keys, 0:cols].reshape(keys // 8, 8, cols)
            w = jnp.exp2(x - best[None]).reshape(keys, cols)
            w_hi, w_lo = split(w)
            both = dot(vv, w_hi)
            low = jnp.concatenate([both[size:], jnp.zeros((PAD, cols), F32)], axis=0)
            term = both[:size] + low + dot(vv[:size], w_lo)
            acc = term if acc is None else acc + term
            step += keys
        out_ref[h] = acc

    def local_score(i, slot, h):
        far_score(kmf[i ^ 1, h], qf[i, h], slot, h, fb.at[i])

    def local_soft(i, slot, h):
        far_soft([vvf[i ^ 1, h]], slot, h, fb.at[i], fo.at[i])

    def near_score(n, slot, h):
        at = pl.multiple_of(n * LEAF, LEAF)
        best = None
        for j in range(3):
            key_rows = pl.ds(pl.multiple_of(at + j * LEAF, LEAF), LEAF)
            left = jnp.concatenate([ka[key_rows, :], kb[h, key_rows, :]], axis=1)
            s = dot(left, qx[h, :, pl.ds(at, LEAF)])
            ss[slot, h, j * LEAF : (j + 1) * LEAF, :] = s
            top = jnp.max(s.reshape(LEAF // 8, 8, LEAF), axis=0)
            best = top if best is None else jnp.maximum(best, top)
        sb[slot, h] = jnp.broadcast_to(jnp.max(best, axis=0, keepdims=True), (8, LEAF))

    def near_soft(n, slot, h):
        at = pl.multiple_of(n * LEAF, LEAF)
        best = sb[slot, h]
        total, acc = None, None
        part = slice(h * width, (h + 1) * width)
        for j in range(3):
            x = ss[slot, h, j * LEAF : (j + 1) * LEAF, :].reshape(LEAF // 8, 8, LEAF)
            w = jnp.exp2(x - best[None])
            term = jnp.sum(w, axis=0)
            total = term if total is None else total + term
            keys = pl.ds(pl.multiple_of(at + j * LEAF, LEAF), LEAF)
            term = dot(vx[part, keys], w.reshape(LEAF, LEAF).astype(BF))
            acc = term if acc is None else acc + term
        num[part, pl.ds(at, LEAF)] = acc
        stat[2 * h : 2 * h + 1, pl.ds(at, LEAF)] = best[0:1]
        stat[2 * h + 1 : 2 * h + 2, pl.ds(at, LEAF)] = jnp.sum(total, axis=0, keepdims=True)

    def leaf_at(k):
        return jnp.where(k < leaves - 2, k + 1, jnp.where(k == leaves - 2, 0, leaves - 1))

    for h in range(heads):
        local_score(0, 0, h)
    for i in range(first):
        for h in range(heads):
            local_soft(i, i % 2, h)
            if i + 1 < first:
                local_score(i + 1, 1 - i % 2, h)
            else:
                near_score(leaf_at(0), 1 - i % 2, h)
    turn = first % 2

    @pl.loop(0, leaves // 4)
    def _(i):
        @pl.when(jnp.logical_and(i == 1, has_right))
        def _():
            for copy in halo(0):
                copy.wait_recv()

        @pl.when(jnp.logical_and(i == 1, has_left))
        def _():
            for copy in halo(1):
                copy.wait_recv()

        @pl.when(i == 1)
        def _():
            for n, at in ((-1, 0), (leaves, tokens + LEAF)):
                tail0, tail1, _ = key_tail(ka[at : at + LEAF, :].astype(F32), leaf_bias(count_of(n)))
                kb[0, at : at + LEAF, :] = tail0.astype(BF)
                kb[1, at : at + LEAF, :] = tail1.astype(BF)

        for j in range(4):
            k = 4 * i + j
            slot = (turn + j) % 2
            for h in range(heads):
                near_soft(leaf_at(k), slot, h)
                near_score(leaf_at(jnp.minimum(k + 1, leaves - 1)), 1 - slot, h)

    for level in reversed(far_levels):
        pieces = fp[level].shape[0]
        for i in range(1 << (level - depth_local)):
            for piece in range(pieces):
                remote(
                    fp[level].at[piece], fr[level].at[i, piece],
                    far_send[level].at[i * pieces + piece], far_recv[level].at[i * pieces + piece], seq,
                ).wait_recv()

    def unpack(level):
        bit = level - depth_local
        nb = 1 << bit
        base = ((seq >> bit) ^ 1) << bit
        lane = iota((PAD, LEAF), 1)
        count = jnp.zeros((PAD, LEAF), I32)
        for leaf in range(leaves * nb):
            count = jnp.where((lane << level) >> 8 == leaf, counts[base * leaves + leaf], count)
        mass = clip_mass(count, (lane << level) & (LEAF - 1), 1 << level)
        mass_col = dot(mass.astype(BF), jnp.ones((PAD, LANES), BF), ((0,), (0,)))
        bias = jnp.where(mass_col > 0, 0.0, NEG)
        got = jnp.concatenate(
            [
                fr[level][i, piece].astype(I32).astype(F32)
                for i in range(nb)
                for piece in range(fp[level].shape[0])
            ],
            axis=0,
        )
        mean = got[:, :rows] * (BOUND / STEPS)
        put_key(kmr2[level], mean, pltpu.roll(mean, width, 1), bias, slice(0, LEAF))
        put_value(vvr2[level], got[:, rows:].T * (BOUND * 2**level / STEPS), mass, slice(0, LEAF))

    for first_level in range(0, len(far_levels), 2):
        group = list(reversed(far_levels))[first_level : first_level + 2]
        for level in group:
            unpack(level)
        for slot, level in enumerate(group):
            for h in range(heads):
                far_score(kmr2[level][h], qr[level][h], slot, h, fbr[level])
        for slot, level in enumerate(group):
            for h in range(heads):
                far_soft([vvr2[level][h]], slot, h, fbr[level], for_[level])

    def up(z):
        return dot(jnp.concatenate(split(z), axis=1), uu[...])

    def with_best(acc, best):
        return jnp.concatenate([acc[: size - 8], jnp.broadcast_to(best, (8, acc.shape[1]))], axis=0)

    def merge(acc, best, z):
        old = z[size - 8 : size - 7]
        new = jnp.maximum(best, old)
        both = acc * jnp.exp2(best - new) + z * jnp.exp2(old - new)
        return with_best(both, new)

    def tiles(z):
        return [z[:, j * LANES : (j + 1) * LANES] for j in range(z.shape[1] // LANES)]

    zs = [None] * heads
    for level in reversed(far_levels):
        for h in range(heads):
            acc, best = for_[level][h], fbr[level][h, 0:1]
            if zs[h] is None:
                zs[h] = with_best(acc, best)
            else:
                z = jnp.concatenate([up(x) for x in tiles(zs[h])], axis=1)
                zs[h] = merge(acc, best, z[:, : acc.shape[1]])
    zs = [None if z is None else tiles(z) for z in zs]
    for level in reversed(near_levels):
        new = [[] for _ in range(heads)]
        for i in range(leaves >> level):
            for h in range(heads):
                block = base_of[level] + i
                acc, best = fo[block, h], fb[block, h, 0:1]
                x = with_best(acc, best) if zs[h] is None else merge(acc, best, up(zs[h][i]))
                for j, part in enumerate(tiles(x)):
                    zb[level % 2, h, 2 * i + j] = part
                    new[h].append(zb.at[level % 2, h, 2 * i + j])
        zs = [[ref[...] for ref in refs_h] for refs_h in new]
    for n in range(leaves):
        for h in range(heads):
            cols = slice(n * LEAF, (n + 1) * LEAF)
            part = slice(h * width, (h + 1) * width)
            near_best, near_total = stat[2 * h : 2 * h + 1, cols], stat[2 * h + 1 : 2 * h + 2, cols]
            z = up(zs[h][n])
            old = z[size - 8 : size - 7]
            new_best = jnp.maximum(near_best, old)
            mine, other = jnp.exp2(near_best - new_best), jnp.exp2(old - new_best)
            inverse = 1.0 / (near_total * mine + z[width : width + 1] * other)
            out[part, cols] = (num[part, cols] * (mine * inverse) + z[:width] * (other * inverse)).astype(BF)

    @pl.when(has_left)
    def _():
        for copy in halo(0):
            copy.wait_send()

    @pl.when(has_right)
    def _():
        for copy in halo(1):
            copy.wait_send()

    for level in far_levels:
        for piece in range(fp[level].shape[0]):
            for copy in far_copies(level, piece):
                copy.wait_send()


def shards(q_heads, k_heads, v_heads, morton_order, leaf_counts):
    heads_real, width, tokens = q_heads.shape
    heads = heads_real + heads_real % 2
    seq_count = lax.axis_size("seq")
    rows = heads * width
    flat = []
    for x in (q_heads, k_heads, v_heads):
        if heads != heads_real:
            x = jnp.concatenate([x, jnp.zeros_like(x[:1])], axis=0)
        flat.append(x.reshape(rows, tokens))
    leaves, depth_local, near_levels, far_levels = plan(tokens, seq_count)
    size = width + PAD
    near_blocks = sum(leaves >> l for l in near_levels)
    pieced = [l for l in far_levels if (LEAF >> l) >= 8]
    unit_rows = lambda which: max(sum(max(LEAF >> l, 16) for l in which), 16)
    pieces = lambda l: leaves // 2 if l in pieced else 1
    vm = pltpu.VMEM
    scratch = [
        vm(morton_order.shape, I32),
        pltpu.SMEM(leaf_counts.shape, I32),
        vm((3 * rows, tokens), BF),
        vm((tokens + 2 * LEAF, rows), BF),
        vm((heads, tokens + 2 * LEAF, LANES), BF),
        vm((rows, tokens + 2 * LEAF), BF),
        vm((heads, 4 * width, tokens), BF),
        vm((2 * rows + PAD, tokens), BF),
        vm((tokens, 3 * rows), BF),
        vm((2, LEAF, LEAF), BF),
        vm((leaves // 2, 2 * LEAF, LANES * len(far_levels)), BF),
        vm((unit_rows(near_levels), LEAF), BF),
        vm((unit_rows(pieced), LEAF), BF),
        vm((LEAF, LEAF), BF),
        vm((near_blocks, heads, 4 * width, LEAF), BF),
        vm((near_blocks, heads, LEAF, 2 * rows), BF),
        vm((near_blocks, heads, size + width, LEAF), BF),
        vm((near_blocks, heads, size, LEAF), F32),
        vm((near_blocks, heads, 8, LEAF), F32),
        vm((leaves // 2, rows, LANES * len(far_levels)), F32),
        vm((2, heads, 3 * LEAF, LEAF), F32),
        vm((2, heads, 8, LEAF), F32),
        vm((rows, tokens), F32),
        vm((2 * heads + (-2 * heads) % 8, tokens), F32),
        vm((2, heads, leaves, size, LANES), F32),
    ]
    scratch += [vm((heads, 4 * width, padded(tokens, l)), BF) for l in far_levels]
    scratch += [vm((heads, LEAF, 2 * rows), BF) for l in far_levels]
    scratch += [vm((heads, size + width, LEAF), BF) for l in far_levels]
    scratch += [vm((heads, size, padded(tokens, l)), F32) for l in far_levels]
    scratch += [vm((heads, 8, padded(tokens, l)), F32) for l in far_levels]
    sent = lambda l: (pieces(l), (tokens >> l) // pieces(l), 2 * rows)
    scratch += [vm(sent(l), I16) for l in far_levels]
    scratch += [vm((1 << (l - depth_local), *sent(l)), I16) for l in far_levels]
    sem = pltpu.SemaphoreType.DMA
    scratch += [sem((5,)), sem((4,)), sem((4,))]
    scratch += [sem((pieces(l) << (l - depth_local),)) for l in far_levels] * 2
    scratch += [vm((tokens >> l, tokens), BF) for l in far_levels if (LEAF >> l) < 8]
    out = pl.pallas_call(
        functools.partial(kernel, (heads, width, tokens, seq_count)),
        out_shape=pltpu.VMEM((rows, tokens), BF),
        in_specs=[pl.BlockSpec(memory_space=pltpu.HBM)] * 5,
        out_specs=pl.BlockSpec(memory_space=pltpu.VMEM),
        scratch_shapes=scratch,
        compiler_params=pltpu.CompilerParams(
            collective_id=0, has_side_effects=True, vmem_limit_bytes=VMEM_LIMIT
        ),
    )(*flat, morton_order, leaf_counts)
    return out.reshape(heads, width, tokens)[:heads_real]


def solution(mesh):
    placed = (
        P("head", None, ("grp", "seq")),
        P("head", None, ("grp", "seq")),
        P("head", None, ("grp", "seq")),
        P(("grp", "seq"), None),
        P("grp"),
    )
    return jax.shard_map(
        shards,
        mesh=mesh,
        in_specs=placed,
        out_specs=P("head", None, ("grp", "seq")),
        check_vma=False,
    )
```

```python
import functools
import math

import jax
import jax.numpy as jnp
from jax import lax
from jax.experimental import pallas as pl
from jax.experimental.pallas import tpu as pltpu
from jax.sharding import PartitionSpec as P

LEAF = 256
LANES = 128
NEG = -1e30
BF = jnp.bfloat16
F32 = jnp.float32
I32 = jnp.int32
I16 = jnp.int16
PAD = 16
BOUND = 10.0
STEPS = 32700.0
VMEM_LIMIT = 63488 * 1024


def dot(a, b, dims=((1,), (0,))):
    return lax.dot_general(a, b, (dims, ((), ())), preferred_element_type=F32)


def split(x):
    hi = x.astype(BF)
    return hi, (x - hi.astype(F32)).astype(BF)


def iota(shape, dim):
    return lax.broadcasted_iota(I32, shape, dim)


def fixed(x, bound):
    return jnp.floor(x * (STEPS / bound) + 0.5).astype(I32).astype(I16)


def unfixed(x, bound):
    return x.astype(I32).astype(F32) * (bound / STEPS)


def plan(tokens, seq_count):
    leaves = tokens // LEAF
    depth_local = leaves.bit_length() - 1
    depth_all = (leaves * seq_count).bit_length() - 1
    levels = list(range(1, depth_all))
    near_levels = [l for l in levels if l < depth_local]
    far_levels = [l for l in levels if l >= depth_local]
    return leaves, depth_local, near_levels, far_levels


def padded(tokens, level):
    return max(LANES, tokens >> level)


def kernel(cfg, *refs):
    heads, width, tokens, seq_count = cfg
    rows = heads * width
    leaves, depth_local, near_levels, far_levels = plan(tokens, seq_count)
    pairs = leaves // 2
    scale = math.log2(math.e) / math.sqrt(width)
    size = width + PAD
    refs = list(refs)
    take = lambda n: [refs.pop(0) for _ in range(n)]
    q_hbm, k_hbm, v_hbm, order_hbm, counts_hbm, out = take(6)
    order, counts = take(2)
    xin, ka, kb, vx, qx, xp, kv = take(7)
    w1, w3, ua, uf, uu = take(5)
    qf, kmf, vvf, fo, fb = take(5)
    pf = take(1)[0]
    ss, sb, num, stat, zb = take(5)
    per_far = lambda: dict(zip(far_levels, take(len(far_levels))))
    qr, kmr2, vvr2, for_, fbr, fp, fr = (per_far() for _ in range(7))
    in_sem, halo_send, halo_recv = take(3)
    far_send, far_recv = per_far(), per_far()
    us = dict(zip([l for l in far_levels if (LEAF >> l) < 8], refs))
    pieced = [l for l in far_levels if l not in us]

    seq = lax.axis_index("seq")
    has_left, has_right = seq > 0, seq < seq_count - 1

    loads = [
        pltpu.make_async_copy(src, xin.at[pl.ds(i * rows, rows)], in_sem.at[i])
        for i, src in enumerate((q_hbm, k_hbm, v_hbm))
    ]
    loads.append(pltpu.make_async_copy(order_hbm, order, in_sem.at[3]))
    loads.append(pltpu.make_async_copy(counts_hbm, counts, in_sem.at[4]))
    for load in loads:
        load.start()
    barrier = pltpu.get_barrier_semaphore()
    for step in range(1, seq_count):
        other = lax.rem(seq + step, seq_count)
        pl.semaphore_signal(
            barrier, inc=1, device_id={"seq": other}, device_id_type=pl.DeviceIdType.MESH
        )

    @pl.when(jnp.logical_not(has_left))
    def _():
        ka[0:LEAF, :] = jnp.zeros((LEAF, rows), BF)
        vx[:, 0:LEAF] = jnp.zeros((rows, LEAF), BF)

    @pl.when(jnp.logical_not(has_right))
    def _():
        ka[tokens + LEAF :, :] = jnp.zeros((LEAF, rows), BF)
        vx[:, tokens + LEAF :] = jnp.zeros((rows, LEAF), BF)

    def count_of(n):
        leaf = seq * leaves + n
        total = leaves * seq_count
        inside = jnp.logical_and(leaf >= 0, leaf < total)
        return jnp.where(inside, counts[jnp.clip(leaf, 0, total - 1)], 0)

    def ones_where(mask):
        return jnp.where(mask, 1.0, 0.0).astype(BF)

    ua_at, uf_at = {}, {}

    def constants():
        t = iota((LEAF, LEAF), 0)
        c = iota((LEAF, LEAF), 1)
        for p in range(2):
            w1[p] = ones_where(
                jnp.logical_or(
                    jnp.logical_and(c < LANES, (t >> 1) == c),
                    jnp.logical_and(c >= LANES, (t >> 2) + 64 * p == c - LANES),
                )
            )
        uu[...] = ones_where((c >> 1) == (t & (LANES - 1)))
        for i, level in enumerate(far_levels):
            t2 = iota((2 * LEAF, LANES), 0)
            c2 = iota((2 * LEAF, LANES), 1)
            for m in range(pairs):
                w3[m, :, i * LANES : (i + 1) * LANES] = ones_where(
                    ((t2 + 2 * LEAF * m) >> level) & (LANES - 1) == c2
                )
        for ref, spots, which in ((ua, ua_at, near_levels), (uf, uf_at, pieced)):
            at = 0
            for level in which:
                n = max(LEAF >> level, 16)
                spots[level] = at
                ref[at : at + n, :] = ones_where((iota((n, LEAF), 1) >> level) == iota((n, LEAF), 0))
                at += n
        for level, u in us.items():
            u[...] = ones_where((iota(u.shape, 1) >> level) == iota(u.shape, 0))

        def tail_rows(cols):
            r = iota((64, cols), 0)
            return ones_where(r == 0)

        for h in range(heads):
            off = (1 - h) * width
            qx[h, off : off + width, :] = jnp.zeros((width, tokens), BF)
            qx[h, 3 * width :, :] = tail_rows(tokens)
            for i in range(qf.shape[0]):
                qf[i, h, 3 * width :, :] = tail_rows(LEAF)
            for level in far_levels:
                qr[level][h, 3 * width :, :] = tail_rows(qr[level].shape[2])

    constants()
    for load in loads[1:]:
        load.wait()

    lane_lo = iota((LEAF, LANES), 1) < width
    lane_is = iota((LEAF, LANES), 1) == width

    def key_tail(key_t, bias):
        shape = key_t.shape
        lo = iota(shape, 1) < width
        at = iota(shape, 1) == width
        rest = jnp.where(at, bias, 0.0)
        rolled = pltpu.roll(key_t, width, 1)
        return jnp.where(lo, key_t, rest), jnp.where(lo, rolled, rest), rolled

    def leaf_bias(count):
        return jnp.where(iota((LEAF, LANES), 0) < count, 0.0, NEG)

    def put_keys(n, key, value):
        at = n * LEAF
        count = count_of(n)
        key_t = key.T
        on_row = iota((rows, LEAF), 1) < count
        on_col = iota((LEAF, rows), 0) < count
        tail0, tail1, rolled = key_tail(key_t, leaf_bias(count))
        ka[at + LEAF : at + 2 * LEAF, :] = key_t.astype(BF)
        kb[0, at + LEAF : at + 2 * LEAF, :] = tail0.astype(BF)
        kb[1, at + LEAF : at + 2 * LEAF, :] = tail1.astype(BF)
        kv[at : at + LEAF, 0:rows] = jnp.where(on_col, rolled, 0.0).astype(BF)
        kv[at : at + LEAF, rows : 2 * rows] = jnp.where(on_col, key_t, 0.0).astype(BF)
        kv[at : at + LEAF, 2 * rows :] = jnp.where(on_col, value.T, 0.0).astype(BF)
        vx[:, at + LEAF : at + 2 * LEAF] = value.astype(BF)
        xp[rows : 2 * rows, at : at + LEAF] = jnp.where(on_row, value, 0.0).astype(BF)
        xp[2 * rows :, at : at + LEAF] = ones_where(on_row[:PAD])

    def put_queries(n, query):
        cols = slice(n * LEAF, (n + 1) * LEAF)
        xp[0:rows, cols] = query.astype(BF)
        hi, lo = split(query * scale)
        for h in range(heads):
            part = slice(h * width, (h + 1) * width)
            qx[h, part, cols] = hi[part]
            qx[h, 2 * width : 3 * width, cols] = lo[part]

    def permute(group, start=0, stop=3):
        for n in group:
            picks = order[0:1, n * LEAF : (n + 1) * LEAF]
            hot = jnp.where(iota((tokens, LEAF), 0) == picks, 1.0, 0.0).astype(BF)
            moved = dot(xin[start * rows : stop * rows], hot)
            if start == 0:
                put_queries(n, moved[:rows])
            if stop == 3:
                put_keys(n, moved[(1 - start) * rows : (2 - start) * rows], moved[(2 - start) * rows :])

    def put_query(ref, x, factor, where):
        hi, lo = split(x * factor)
        for h in range(heads):
            part = slice(h * width, (h + 1) * width)
            ref[h, 0:width, where] = hi[part]
            ref[h, width : 2 * width, where] = hi[part]
            ref[h, 2 * width : 3 * width, where] = lo[part]

    def put_value(ref, x, mass, where):
        hi, lo = split(x)
        for h in range(heads):
            part = slice(h * width, (h + 1) * width)
            ref[h, 0:width, where] = hi[part]
            ref[h, width:size, where] = mass.astype(BF)
            ref[h, size:, where] = lo[part]

    def put_key(ref, a, b, bias, where):
        lo_lane = iota(a.shape, 1) < width
        bias_lane = iota(a.shape, 1) == width
        a_hi, b_hi = a.astype(BF).astype(F32), b.astype(BF).astype(F32)
        rest = jnp.where(bias_lane, bias, 0.0)
        ref[0, where, 0:rows] = jnp.where(lo_lane, a_hi, b - b_hi).astype(BF)
        ref[0, where, rows:] = jnp.where(lo_lane, a_hi, rest).astype(BF)
        ref[1, where, 0:rows] = jnp.where(lo_lane, b_hi, a - a_hi).astype(BF)
        ref[1, where, rows:] = jnp.where(lo_lane, b_hi, rest).astype(BF)

    def clip_mass(count, at, g):
        return jnp.clip(count - at, 0, g).astype(F32)

    base_of, first = {}, 0
    for level in near_levels:
        base_of[level] = first
        first += leaves >> level

    def pool_far(m):
        if not pieced:
            return
        start = m * 2 * LEAF
        kk = []
        for p in range(2):
            at = start + p * LEAF
            kk.append(dot(uf[...], kv[pl.ds(at, LEAF), rows:]))
        for level in pieced:
            count = LEAF >> level
            x = jnp.concatenate([k[uf_at[level] : uf_at[level] + count] for k in kk], axis=0)
            mass = [
                clip_mass(count_of(2 * m + p), iota((count, LANES), 0) << level, 1 << level)
                for p in range(2)
            ]
            mean = x[:, :rows] / jnp.maximum(jnp.concatenate(mass, axis=0), 1.0)
            fp[level][m, :, 0:rows] = fixed(mean, BOUND)
            fp[level][m, :, rows:] = fixed(x[:, rows:], BOUND * 2**level)

    def pool_near(m):
        start = m * 2 * LEAF
        t1, kk = [], []
        for p in range(2):
            at = start + p * LEAF
            t1.append(dot(xp[0 : 2 * rows, pl.ds(at, LEAF)], w1[p]))
            kk.append(dot(ua[...], kv[pl.ds(at, LEAF), 0 : 2 * rows]))
        if far_levels:
            pf[m] = dot(xp[0:rows, pl.ds(start, 2 * LEAF)], w3[m])
        n = [count_of(2 * m), count_of(2 * m + 1)]
        b1 = base_of[1] + m
        lane = iota((PAD, LANES), 1)
        for p in range(2):
            where = slice(p * LANES, (p + 1) * LANES)
            put_query(qf.at[b1], t1[p][:rows, :LANES], scale / 2, where)
            put_value(vvf.at[b1], t1[p][rows:, :LANES], clip_mass(n[p], lane << 1, 2), where)
        if 2 in near_levels:
            b2 = base_of[2] + m // 2
            x2 = t1[0][:, LANES:] + t1[1][:, LANES:]
            where = pl.ds((m % 2) * LANES, LANES)
            mass = jnp.where(
                lane < 64, clip_mass(n[0], lane << 2, 4), clip_mass(n[1], (lane - 64) << 2, 4)
            )
            put_query(qf.at[b2], x2[:rows], scale / 4, where)
            put_value(vvf.at[b2], x2[rows:], mass, where)
        for p in range(2):
            for level in near_levels:
                count = LEAF >> level
                x = kk[p][ua_at[level] : ua_at[level] + count]
                mass = clip_mass(n[p], iota((count, LANES), 0) << level, 1 << level)
                inverse = 1.0 / jnp.maximum(mass, 1.0)
                b, a = x[:, :rows] * inverse, x[:, rows:] * inverse
                bias = jnp.where(mass > 0, 0.0, NEG)
                if level == 1:
                    put_key(kmf.at[b1], a, b, bias, slice(p * count, (p + 1) * count))
                else:
                    spot = (m % 2) * LANES + p * count
                    put_key(kmf.at[b2], a, b, bias, pl.ds(spot, count))

    def remote(src, dst, send, recv, target):
        return pltpu.make_async_remote_copy(
            src_ref=src,
            dst_ref=dst,
            send_sem=send,
            recv_sem=recv,
            device_id={"seq": target},
            device_id_type=pl.DeviceIdType.MESH,
        )

    def halo(side):
        start, end = (LEAF, tokens + LEAF) if side == 0 else (tokens, 0)
        target = jnp.maximum(seq - 1, 0) if side == 0 else jnp.minimum(seq + 1, seq_count - 1)
        return (
            remote(
                ka.at[pl.ds(start, LEAF)],
                ka.at[pl.ds(end, LEAF)],
                halo_send.at[2 * side],
                halo_recv.at[2 * side],
                target,
            ),
            remote(
                vx.at[:, pl.ds(start, LEAF)],
                vx.at[:, pl.ds(end, LEAF)],
                halo_send.at[2 * side + 1],
                halo_recv.at[2 * side + 1],
                target,
            ),
        )

    def far_copies(level, piece):
        bit = level - depth_local
        nb = 1 << bit
        pieces = fp[level].shape[0]
        slot = lax.rem(seq, nb)
        base = ((seq >> bit) ^ 1) << bit
        return [
            remote(
                fp[level].at[piece],
                fr[level].at[slot, piece],
                far_send[level].at[j * pieces + piece],
                far_recv[level].at[slot * pieces + piece],
                base + j,
            )
            for j in range(nb)
        ]

    def send_far(m):
        for level in reversed(pieced):
            for copy in far_copies(level, m):
                copy.start()

    groups = [(0, leaves - 1), (1, leaves - 2)] + [(2 * m, 2 * m + 1) for m in range(1, pairs - 1)]
    ready = [[], []] + [[0, pairs - 1]] + [[m] for m in range(1, pairs - 1)]
    for step, group in enumerate(groups):
        for m in ready[step]:
            pool_far(m)
        if step:
            permute(group)
        else:
            permute(group, start=1)
            pl.semaphore_wait(barrier, seq_count - 1)

            @pl.when(has_left)
            def _():
                for copy in halo(0):
                    copy.start()

            @pl.when(has_right)
            def _():
                for copy in halo(1):
                    copy.start()

            loads[0].wait()

        for m in ready[step]:
            send_far(m)
    for m in ready[len(groups)]:
        pool_far(m)
    if pairs > 2:
        pool_near(1)
    for m in ready[len(groups)]:
        send_far(m)
    for level in us:
        sums = dot(us[level][...], kv[:, rows:])
        valid = jnp.broadcast_to(xp[2 * rows : 2 * rows + 1, :], (LANES, tokens))
        mass = dot(us[level][...], valid, ((1,), (1,)))
        fp[level][0, :, 0:rows] = fixed(sums[:, :rows] / jnp.maximum(mass, 1.0), BOUND)
        fp[level][0, :, rows:] = fixed(sums[:, rows:], BOUND * 2**level)
        for copy in far_copies(level, 0):
            copy.start()

    for m in range(2, pairs - 1):
        pool_near(m)
    permute(groups[0], stop=1)
    for m in (0, pairs - 1):
        pool_near(m)

    for i, level in enumerate(far_levels):
        pieces = max((tokens >> level) // LANES, 1)
        per = pairs // pieces
        cols = slice(i * LANES, (i + 1) * LANES)
        for j in range(pieces):
            x = sum(pf[j * per + e, :, cols] for e in range(per))
            put_query(qr[level], x, scale / 2**level, slice(j * LANES, (j + 1) * LANES))

    def far_score(km, q, slot, h, best_ref):
        s = dot(km, q)
        keys, cols = s.shape
        ss[slot, h, 0:keys, 0:cols] = s
        best = jnp.max(s.reshape(keys // 8, 8, cols), axis=0)
        best = jnp.max(best, axis=0, keepdims=True).astype(BF).astype(F32)
        best_ref[h] = jnp.broadcast_to(best, (8, cols))

    def far_soft(vvs, slot, h, best_ref, out_ref):
        cols = best_ref.shape[2]
        best = best_ref[h]
        step, acc = 0, None
        for vv in vvs:
            keys = vv.shape[1]
            x = ss[slot, h, step : step + keys, 0:cols].reshape(keys // 8, 8, cols)
            w = jnp.exp2(x - best[None]).reshape(keys, cols)
            w_hi, w_lo = split(w)
            both = dot(vv, w_hi)
            low = jnp.concatenate([both[size:], jnp.zeros((PAD, cols), F32)], axis=0)
            term = both[:size] + low + dot(vv[:size], w_lo)
            acc = term if acc is None else acc + term
            step += keys
        out_ref[h] = acc

    def local_score(i, slot, h):
        far_score(kmf[i ^ 1, h], qf[i, h], slot, h, fb.at[i])

    def local_soft(i, slot, h):
        far_soft([vvf[i ^ 1, h]], slot, h, fb.at[i], fo.at[i])

    def near_score(n, slot, h):
        at = pl.multiple_of(n * LEAF, LEAF)
        best = None
        for j in range(3):
            key_rows = pl.ds(pl.multiple_of(at + j * LEAF, LEAF), LEAF)
            left = jnp.concatenate([ka[key_rows, :], kb[h, key_rows, :]], axis=1)
            s = dot(left, qx[h, :, pl.ds(at, LEAF)])
            ss[slot, h, j * LEAF : (j + 1) * LEAF, :] = s
            top = jnp.max(s.reshape(LEAF // 8, 8, LEAF), axis=0)
            best = top if best is None else jnp.maximum(best, top)
        sb[slot, h] = jnp.broadcast_to(jnp.max(best, axis=0, keepdims=True), (8, LEAF))

    def near_soft(n, slot, h):
        at = pl.multiple_of(n * LEAF, LEAF)
        best = sb[slot, h]
        total, acc = None, None
        part = slice(h * width, (h + 1) * width)
        for j in range(3):
            x = ss[slot, h, j * LEAF : (j + 1) * LEAF, :].reshape(LEAF // 8, 8, LEAF)
            w = jnp.exp2(x - best[None])
            term = jnp.sum(w, axis=0)
            total = term if total is None else total + term
            keys = pl.ds(pl.multiple_of(at + j * LEAF, LEAF), LEAF)
            term = dot(vx[part, keys], w.reshape(LEAF, LEAF).astype(BF))
            acc = term if acc is None else acc + term
        num[part, pl.ds(at, LEAF)] = acc
        stat[2 * h : 2 * h + 1, pl.ds(at, LEAF)] = best[0:1]
        stat[2 * h + 1 : 2 * h + 2, pl.ds(at, LEAF)] = jnp.sum(total, axis=0, keepdims=True)

    def leaf_at(k):
        return jnp.where(k < leaves - 2, k + 1, jnp.where(k == leaves - 2, 0, leaves - 1))

    for h in range(heads):
        local_score(0, 0, h)
    for i in range(first):
        for h in range(heads):
            local_soft(i, i % 2, h)
            if i + 1 < first:
                local_score(i + 1, 1 - i % 2, h)
            else:
                near_score(leaf_at(0), 1 - i % 2, h)
    turn = first % 2

    @pl.loop(0, leaves // 4)
    def _(i):
        @pl.when(jnp.logical_and(i == 1, has_right))
        def _():
            for copy in halo(0):
                copy.wait_recv()

        @pl.when(jnp.logical_and(i == 1, has_left))
        def _():
            for copy in halo(1):
                copy.wait_recv()

        @pl.when(i == 1)
        def _():
            for n, at in ((-1, 0), (leaves, tokens + LEAF)):
                tail0, tail1, _ = key_tail(ka[at : at + LEAF, :].astype(F32), leaf_bias(count_of(n)))
                kb[0, at : at + LEAF, :] = tail0.astype(BF)
                kb[1, at : at + LEAF, :] = tail1.astype(BF)

        for j in range(4):
            k = 4 * i + j
            slot = (turn + j) % 2
            for h in range(heads):
                near_soft(leaf_at(k), slot, h)
                near_score(leaf_at(jnp.minimum(k + 1, leaves - 1)), 1 - slot, h)

    for level in reversed(far_levels):
        pieces = fp[level].shape[0]
        for i in range(1 << (level - depth_local)):
            for piece in range(pieces):
                remote(
                    fp[level].at[piece], fr[level].at[i, piece],
                    far_send[level].at[i * pieces + piece], far_recv[level].at[i * pieces + piece], seq,
                ).wait_recv()

    def unpack(level):
        bit = level - depth_local
        nb = 1 << bit
        base = ((seq >> bit) ^ 1) << bit
        lane = iota((PAD, LEAF), 1)
        count = jnp.zeros((PAD, LEAF), I32)
        for leaf in range(leaves * nb):
            count = jnp.where((lane << level) >> 8 == leaf, counts[base * leaves + leaf], count)
        mass = clip_mass(count, (lane << level) & (LEAF - 1), 1 << level)
        mass_col = dot(mass.astype(BF), jnp.ones((PAD, LANES), BF), ((0,), (0,)))
        bias = jnp.where(mass_col > 0, 0.0, NEG)
        got = jnp.concatenate(
            [
                fr[level][i, piece].astype(I32).astype(F32)
                for i in range(nb)
                for piece in range(fp[level].shape[0])
            ],
            axis=0,
        )
        mean = got[:, :rows] * (BOUND / STEPS)
        put_key(kmr2[level], mean, pltpu.roll(mean, width, 1), bias, slice(0, LEAF))
        put_value(vvr2[level], got[:, rows:].T * (BOUND * 2**level / STEPS), mass, slice(0, LEAF))

    for first_level in range(0, len(far_levels), 2):
        group = list(reversed(far_levels))[first_level : first_level + 2]
        for level in group:
            unpack(level)
        for slot, level in enumerate(group):
            for h in range(heads):
                far_score(kmr2[level][h], qr[level][h], slot, h, fbr[level])
        for slot, level in enumerate(group):
            for h in range(heads):
                far_soft([vvr2[level][h]], slot, h, fbr[level], for_[level])

    def up(z):
        return dot(jnp.concatenate(split(z), axis=1), uu[...])

    def with_best(acc, best):
        return jnp.concatenate([acc[: size - 8], jnp.broadcast_to(best, (8, acc.shape[1]))], axis=0)

    def merge(acc, best, z):
        old = z[size - 8 : size - 7]
        new = jnp.maximum(best, old)
        both = acc * jnp.exp2(best - new) + z * jnp.exp2(old - new)
        return with_best(both, new)

    def tiles(z):
        return [z[:, j * LANES : (j + 1) * LANES] for j in range(z.shape[1] // LANES)]

    zs = [None] * heads
    for level in reversed(far_levels):
        for h in range(heads):
            acc, best = for_[level][h], fbr[level][h, 0:1]
            if zs[h] is None:
                zs[h] = with_best(acc, best)
            else:
                z = jnp.concatenate([up(x) for x in tiles(zs[h])], axis=1)
                zs[h] = merge(acc, best, z[:, : acc.shape[1]])
    zs = [None if z is None else tiles(z) for z in zs]
    for level in reversed(near_levels):
        new = [[] for _ in range(heads)]
        for i in range(leaves >> level):
            for h in range(heads):
                block = base_of[level] + i
                acc, best = fo[block, h], fb[block, h, 0:1]
                x = with_best(acc, best) if zs[h] is None else merge(acc, best, up(zs[h][i]))
                for j, part in enumerate(tiles(x)):
                    zb[level % 2, h, 2 * i + j] = part
                    new[h].append(zb.at[level % 2, h, 2 * i + j])
        zs = [[ref[...] for ref in refs_h] for refs_h in new]
    for n in range(leaves):
        for h in range(heads):
            cols = slice(n * LEAF, (n + 1) * LEAF)
            part = slice(h * width, (h + 1) * width)
            near_best, near_total = stat[2 * h : 2 * h + 1, cols], stat[2 * h + 1 : 2 * h + 2, cols]
            z = up(zs[h][n])
            old = z[size - 8 : size - 7]
            new_best = jnp.maximum(near_best, old)
            mine, other = jnp.exp2(near_best - new_best), jnp.exp2(old - new_best)
            inverse = 1.0 / (near_total * mine + z[width : width + 1] * other)
            out[part, cols] = (num[part, cols] * (mine * inverse) + z[:width] * (other * inverse)).astype(BF)

    @pl.when(has_left)
    def _():
        for copy in halo(0):
            copy.wait_send()

    @pl.when(has_right)
    def _():
        for copy in halo(1):
            copy.wait_send()

    for level in far_levels:
        for piece in range(fp[level].shape[0]):
            for copy in far_copies(level, piece):
                copy.wait_send()


def shards(q_heads, k_heads, v_heads, morton_order, leaf_counts):
    heads_real, width, tokens = q_heads.shape
    heads = heads_real + heads_real % 2
    seq_count = lax.axis_size("seq")
    rows = heads * width
    flat = []
    for x in (q_heads, k_heads, v_heads):
        if heads != heads_real:
            x = jnp.concatenate([x, jnp.zeros_like(x[:1])], axis=0)
        flat.append(x.reshape(rows, tokens))
    leaves, depth_local, near_levels, far_levels = plan(tokens, seq_count)
    size = width + PAD
    near_blocks = sum(leaves >> l for l in near_levels)
    pieced = [l for l in far_levels if (LEAF >> l) >= 8]
    unit_rows = lambda which: max(sum(max(LEAF >> l, 16) for l in which), 16)
    pieces = lambda l: leaves // 2 if l in pieced else 1
    vm = pltpu.VMEM
    scratch = [
        vm(morton_order.shape, I32),
        pltpu.SMEM(leaf_counts.shape, I32),
        vm((3 * rows, tokens), BF),
        vm((tokens + 2 * LEAF, rows), BF),
        vm((heads, tokens + 2 * LEAF, LANES), BF),
        vm((rows, tokens + 2 * LEAF), BF),
        vm((heads, 4 * width, tokens), BF),
        vm((2 * rows + PAD, tokens), BF),
        vm((tokens, 3 * rows), BF),
        vm((2, LEAF, LEAF), BF),
        vm((leaves // 2, 2 * LEAF, LANES * len(far_levels)), BF),
        vm((unit_rows(near_levels), LEAF), BF),
        vm((unit_rows(pieced), LEAF), BF),
        vm((LEAF, LEAF), BF),
        vm((near_blocks, heads, 4 * width, LEAF), BF),
        vm((near_blocks, heads, LEAF, 2 * rows), BF),
        vm((near_blocks, heads, size + width, LEAF), BF),
        vm((near_blocks, heads, size, LEAF), F32),
        vm((near_blocks, heads, 8, LEAF), F32),
        vm((leaves // 2, rows, LANES * len(far_levels)), F32),
        vm((2, heads, 3 * LEAF, LEAF), F32),
        vm((2, heads, 8, LEAF), F32),
        vm((rows, tokens), F32),
        vm((2 * heads + (-2 * heads) % 8, tokens), F32),
        vm((2, heads, leaves, size, LANES), F32),
    ]
    scratch += [vm((heads, 4 * width, padded(tokens, l)), BF) for l in far_levels]
    scratch += [vm((heads, LEAF, 2 * rows), BF) for l in far_levels]
    scratch += [vm((heads, size + width, LEAF), BF) for l in far_levels]
    scratch += [vm((heads, size, padded(tokens, l)), F32) for l in far_levels]
    scratch += [vm((heads, 8, padded(tokens, l)), F32) for l in far_levels]
    sent = lambda l: (pieces(l), (tokens >> l) // pieces(l), 2 * rows)
    scratch += [vm(sent(l), I16) for l in far_levels]
    scratch += [vm((1 << (l - depth_local), *sent(l)), I16) for l in far_levels]
    sem = pltpu.SemaphoreType.DMA
    scratch += [sem((5,)), sem((4,)), sem((4,))]
    scratch += [sem((pieces(l) << (l - depth_local),)) for l in far_levels] * 2
    scratch += [vm((tokens >> l, tokens), BF) for l in far_levels if (LEAF >> l) < 8]
    out = pl.pallas_call(
        functools.partial(kernel, (heads, width, tokens, seq_count)),
        out_shape=pltpu.VMEM((rows, tokens), BF),
        in_specs=[pl.BlockSpec(memory_space=pltpu.HBM)] * 5,
        out_specs=pl.BlockSpec(memory_space=pltpu.VMEM),
        scratch_shapes=scratch,
        compiler_params=pltpu.CompilerParams(
            collective_id=0, has_side_effects=True, vmem_limit_bytes=VMEM_LIMIT
        ),
    )(*flat, morton_order, leaf_counts)
    return out.reshape(heads, width, tokens)[:heads_real]


def solution(mesh):
    placed = (
        P("head", None, ("grp", "seq")),
        P("head", None, ("grp", "seq")),
        P("head", None, ("grp", "seq")),
        P(("grp", "seq"), None),
        P("grp"),
    )
    return jax.shard_map(
        shards,
        mesh=mesh,
        in_specs=placed,
        out_specs=P("head", None, ("grp", "seq")),
        check_vma=False,
    )
```

```python
import functools
import math

import jax
import jax.numpy as jnp
from jax import lax
from jax.experimental import pallas as pl
from jax.experimental.pallas import tpu as pltpu
from jax.sharding import PartitionSpec as P

LEAF = 256
LANES = 128
NEG = -1e30
BF = jnp.bfloat16
F32 = jnp.float32
I32 = jnp.int32
I16 = jnp.int16
PAD = 16
BOUND = 10.0
STEPS = 32700.0
VMEM_LIMIT = 63488 * 1024


def dot(a, b, dims=((1,), (0,))):
    return lax.dot_general(a, b, (dims, ((), ())), preferred_element_type=F32)


def split(x):
    hi = x.astype(BF)
    return hi, (x - hi.astype(F32)).astype(BF)


def iota(shape, dim):
    return lax.broadcasted_iota(I32, shape, dim)


def fixed(x, bound):
    return jnp.floor(x * (STEPS / bound) + 0.5).astype(I32).astype(I16)


def unfixed(x, bound):
    return x.astype(I32).astype(F32) * (bound / STEPS)


def plan(tokens, seq_count):
    leaves = tokens // LEAF
    depth_local = leaves.bit_length() - 1
    depth_all = (leaves * seq_count).bit_length() - 1
    levels = list(range(1, depth_all))
    near_levels = [l for l in levels if l < depth_local]
    far_levels = [l for l in levels if l >= depth_local]
    return leaves, depth_local, near_levels, far_levels


def padded(tokens, level):
    return max(LANES, tokens >> level)


def kernel(cfg, *refs):
    heads, width, tokens, seq_count = cfg
    rows = heads * width
    leaves, depth_local, near_levels, far_levels = plan(tokens, seq_count)
    pairs = leaves // 2
    scale = math.log2(math.e) / math.sqrt(width)
    size = width + PAD
    refs = list(refs)
    take = lambda n: [refs.pop(0) for _ in range(n)]
    q_hbm, k_hbm, v_hbm, order_hbm, counts_hbm, out = take(6)
    order, counts = take(2)
    xin, ka, kb, vx, qx, xp, kv = take(7)
    w1, w3, ua, uf, uu = take(5)
    qf, kmf, vvf, fo, fb = take(5)
    pf = take(1)[0]
    ss, sb, num, stat, zb = take(5)
    per_far = lambda: dict(zip(far_levels, take(len(far_levels))))
    qr, kmr2, vvr2, for_, fbr, fp, fr = (per_far() for _ in range(7))
    in_sem, halo_send, halo_recv = take(3)
    far_send, far_recv = per_far(), per_far()
    us = dict(zip([l for l in far_levels if (LEAF >> l) < 8], refs))
    pieced = [l for l in far_levels if l not in us]

    seq = lax.axis_index("seq")
    has_left, has_right = seq > 0, seq < seq_count - 1

    loads = [
        pltpu.make_async_copy(src, xin.at[pl.ds(i * rows, rows)], in_sem.at[i])
        for i, src in enumerate((q_hbm, k_hbm, v_hbm))
    ]
    loads.append(pltpu.make_async_copy(order_hbm, order, in_sem.at[3]))
    loads.append(pltpu.make_async_copy(counts_hbm, counts, in_sem.at[4]))
    for load in loads:
        load.start()
    barrier = pltpu.get_barrier_semaphore()
    for step in range(1, seq_count):
        other = lax.rem(seq + step, seq_count)
        pl.semaphore_signal(
            barrier, inc=1, device_id={"seq": other}, device_id_type=pl.DeviceIdType.MESH
        )

    @pl.when(jnp.logical_not(has_left))
    def _():
        ka[0:LEAF, :] = jnp.zeros((LEAF, rows), BF)
        vx[:, 0:LEAF] = jnp.zeros((rows, LEAF), BF)

    @pl.when(jnp.logical_not(has_right))
    def _():
        ka[tokens + LEAF :, :] = jnp.zeros((LEAF, rows), BF)
        vx[:, tokens + LEAF :] = jnp.zeros((rows, LEAF), BF)

    def count_of(n):
        leaf = seq * leaves + n
        total = leaves * seq_count
        inside = jnp.logical_and(leaf >= 0, leaf < total)
        return jnp.where(inside, counts[jnp.clip(leaf, 0, total - 1)], 0)

    def ones_where(mask):
        return jnp.where(mask, 1.0, 0.0).astype(BF)

    ua_at, uf_at = {}, {}

    def constants():
        t = iota((LEAF, LEAF), 0)
        c = iota((LEAF, LEAF), 1)
        for p in range(2):
            w1[p] = ones_where(
                jnp.logical_or(
                    jnp.logical_and(c < LANES, (t >> 1) == c),
                    jnp.logical_and(c >= LANES, (t >> 2) + 64 * p == c - LANES),
                )
            )
        uu[...] = ones_where((c >> 1) == (t & (LANES - 1)))
        for i, level in enumerate(far_levels):
            t2 = iota((2 * LEAF, LANES), 0)
            c2 = iota((2 * LEAF, LANES), 1)
            for m in range(pairs):
                w3[m, :, i * LANES : (i + 1) * LANES] = ones_where(
                    ((t2 + 2 * LEAF * m) >> level) & (LANES - 1) == c2
                )
        for ref, spots, which in ((ua, ua_at, near_levels), (uf, uf_at, pieced)):
            at = 0
            for level in which:
                n = max(LEAF >> level, 16)
                spots[level] = at
                ref[at : at + n, :] = ones_where((iota((n, LEAF), 1) >> level) == iota((n, LEAF), 0))
                at += n
        for level, u in us.items():
            u[...] = ones_where((iota(u.shape, 1) >> level) == iota(u.shape, 0))

        def tail_rows(cols):
            r = iota((64, cols), 0)
            return ones_where(r == 0)

        for h in range(heads):
            off = (1 - h) * width
            qx[h, off : off + width, :] = jnp.zeros((width, tokens), BF)
            qx[h, 3 * width :, :] = tail_rows(tokens)
            for i in range(qf.shape[0]):
                qf[i, h, 3 * width :, :] = tail_rows(LEAF)
            for level in far_levels:
                qr[level][h, 3 * width :, :] = tail_rows(qr[level].shape[2])

    constants()
    for load in loads[1:]:
        load.wait()

    lane_lo = iota((LEAF, LANES), 1) < width
    lane_is = iota((LEAF, LANES), 1) == width

    def key_tail(key_t, bias):
        shape = key_t.shape
        lo = iota(shape, 1) < width
        at = iota(shape, 1) == width
        rest = jnp.where(at, bias, 0.0)
        rolled = pltpu.roll(key_t, width, 1)
        return jnp.where(lo, key_t, rest), jnp.where(lo, rolled, rest), rolled

    def leaf_bias(count):
        return jnp.where(iota((LEAF, LANES), 0) < count, 0.0, NEG)

    def put_keys(n, key, value):
        at = n * LEAF
        count = count_of(n)
        key_t = key.T
        on_row = iota((rows, LEAF), 1) < count
        on_col = iota((LEAF, rows), 0) < count
        tail0, tail1, rolled = key_tail(key_t, leaf_bias(count))
        ka[at + LEAF : at + 2 * LEAF, :] = key_t.astype(BF)
        kb[0, at + LEAF : at + 2 * LEAF, :] = tail0.astype(BF)
        kb[1, at + LEAF : at + 2 * LEAF, :] = tail1.astype(BF)
        kv[at : at + LEAF, 0:rows] = jnp.where(on_col, rolled, 0.0).astype(BF)
        kv[at : at + LEAF, rows : 2 * rows] = jnp.where(on_col, key_t, 0.0).astype(BF)
        kv[at : at + LEAF, 2 * rows :] = jnp.where(on_col, value.T, 0.0).astype(BF)
        vx[:, at + LEAF : at + 2 * LEAF] = value.astype(BF)
        xp[rows : 2 * rows, at : at + LEAF] = jnp.where(on_row, value, 0.0).astype(BF)
        xp[2 * rows :, at : at + LEAF] = ones_where(on_row[:PAD])

    def put_queries(n, query):
        cols = slice(n * LEAF, (n + 1) * LEAF)
        xp[0:rows, cols] = query.astype(BF)
        hi, lo = split(query * scale)
        for h in range(heads):
            part = slice(h * width, (h + 1) * width)
            qx[h, part, cols] = hi[part]
            qx[h, 2 * width : 3 * width, cols] = lo[part]

    def permute(group, start=0, stop=3):
        for n in group:
            picks = order[0:1, n * LEAF : (n + 1) * LEAF]
            hot = jnp.where(iota((tokens, LEAF), 0) == picks, 1.0, 0.0).astype(BF)
            moved = dot(xin[start * rows : stop * rows], hot)
            if start == 0:
                put_queries(n, moved[:rows])
            if stop == 3:
                put_keys(n, moved[(1 - start) * rows : (2 - start) * rows], moved[(2 - start) * rows :])

    def put_query(ref, x, factor, where):
        hi, lo = split(x * factor)
        for h in range(heads):
            part = slice(h * width, (h + 1) * width)
            ref[h, 0:width, where] = hi[part]
            ref[h, width : 2 * width, where] = hi[part]
            ref[h, 2 * width : 3 * width, where] = lo[part]

    def put_value(ref, x, mass, where):
        hi, lo = split(x)
        for h in range(heads):
            part = slice(h * width, (h + 1) * width)
            ref[h, 0:width, where] = hi[part]
            ref[h, width:size, where] = mass.astype(BF)
            ref[h, size:, where] = lo[part]

    def put_key(ref, a, b, bias, where):
        lo_lane = iota(a.shape, 1) < width
        bias_lane = iota(a.shape, 1) == width
        a_hi, b_hi = a.astype(BF).astype(F32), b.astype(BF).astype(F32)
        rest = jnp.where(bias_lane, bias, 0.0)
        ref[0, where, 0:rows] = jnp.where(lo_lane, a_hi, b - b_hi).astype(BF)
        ref[0, where, rows:] = jnp.where(lo_lane, a_hi, rest).astype(BF)
        ref[1, where, 0:rows] = jnp.where(lo_lane, b_hi, a - a_hi).astype(BF)
        ref[1, where, rows:] = jnp.where(lo_lane, b_hi, rest).astype(BF)

    def clip_mass(count, at, g):
        return jnp.clip(count - at, 0, g).astype(F32)

    base_of, first = {}, 0
    for level in near_levels:
        base_of[level] = first
        first += leaves >> level

    def pool_far(m):
        if not pieced:
            return
        start = m * 2 * LEAF
        kk = []
        for p in range(2):
            at = start + p * LEAF
            kk.append(dot(uf[...], kv[pl.ds(at, LEAF), rows:]))
        for level in pieced:
            count = LEAF >> level
            x = jnp.concatenate([k[uf_at[level] : uf_at[level] + count] for k in kk], axis=0)
            mass = [
                clip_mass(count_of(2 * m + p), iota((count, LANES), 0) << level, 1 << level)
                for p in range(2)
            ]
            mean = x[:, :rows] / jnp.maximum(jnp.concatenate(mass, axis=0), 1.0)
            fp[level][m, :, 0:rows] = fixed(mean, BOUND)
            fp[level][m, :, rows:] = fixed(x[:, rows:], BOUND * 2**level)

    def pool_near(m):
        start = m * 2 * LEAF
        t1, kk = [], []
        for p in range(2):
            at = start + p * LEAF
            t1.append(dot(xp[0 : 2 * rows, pl.ds(at, LEAF)], w1[p]))
            kk.append(dot(ua[...], kv[pl.ds(at, LEAF), 0 : 2 * rows]))
        if far_levels:
            pf[m] = dot(xp[0:rows, pl.ds(start, 2 * LEAF)], w3[m])
        n = [count_of(2 * m), count_of(2 * m + 1)]
        b1 = base_of[1] + m
        lane = iota((PAD, LANES), 1)
        for p in range(2):
            where = slice(p * LANES, (p + 1) * LANES)
            put_query(qf.at[b1], t1[p][:rows, :LANES], scale / 2, where)
            put_value(vvf.at[b1], t1[p][rows:, :LANES], clip_mass(n[p], lane << 1, 2), where)
        if 2 in near_levels:
            b2 = base_of[2] + m // 2
            x2 = t1[0][:, LANES:] + t1[1][:, LANES:]
            where = pl.ds((m % 2) * LANES, LANES)
            mass = jnp.where(
                lane < 64, clip_mass(n[0], lane << 2, 4), clip_mass(n[1], (lane - 64) << 2, 4)
            )
            put_query(qf.at[b2], x2[:rows], scale / 4, where)
            put_value(vvf.at[b2], x2[rows:], mass, where)
        for p in range(2):
            for level in near_levels:
                count = LEAF >> level
                x = kk[p][ua_at[level] : ua_at[level] + count]
                mass = clip_mass(n[p], iota((count, LANES), 0) << level, 1 << level)
                inverse = 1.0 / jnp.maximum(mass, 1.0)
                b, a = x[:, :rows] * inverse, x[:, rows:] * inverse
                bias = jnp.where(mass > 0, 0.0, NEG)
                if level == 1:
                    put_key(kmf.at[b1], a, b, bias, slice(p * count, (p + 1) * count))
                else:
                    spot = (m % 2) * LANES + p * count
                    put_key(kmf.at[b2], a, b, bias, pl.ds(spot, count))

    def remote(src, dst, send, recv, target):
        return pltpu.make_async_remote_copy(
            src_ref=src,
            dst_ref=dst,
            send_sem=send,
            recv_sem=recv,
            device_id={"seq": target},
            device_id_type=pl.DeviceIdType.MESH,
        )

    def halo(side):
        start, end = (LEAF, tokens + LEAF) if side == 0 else (tokens, 0)
        target = jnp.maximum(seq - 1, 0) if side == 0 else jnp.minimum(seq + 1, seq_count - 1)
        return (
            remote(
                ka.at[pl.ds(start, LEAF)],
                ka.at[pl.ds(end, LEAF)],
                halo_send.at[2 * side],
                halo_recv.at[2 * side],
                target,
            ),
            remote(
                vx.at[:, pl.ds(start, LEAF)],
                vx.at[:, pl.ds(end, LEAF)],
                halo_send.at[2 * side + 1],
                halo_recv.at[2 * side + 1],
                target,
            ),
        )

    def far_copies(level, piece):
        bit = level - depth_local
        nb = 1 << bit
        pieces = fp[level].shape[0]
        slot = lax.rem(seq, nb)
        base = ((seq >> bit) ^ 1) << bit
        return [
            remote(
                fp[level].at[piece],
                fr[level].at[slot, piece],
                far_send[level].at[j * pieces + piece],
                far_recv[level].at[slot * pieces + piece],
                base + j,
            )
            for j in range(nb)
        ]

    def send_far(m):
        for level in reversed(pieced):
            for copy in far_copies(level, m):
                copy.start()

    groups = [(0, leaves - 1), (1, leaves - 2)] + [(2 * m, 2 * m + 1) for m in range(1, pairs - 1)]
    ready = [[], []] + [[0, pairs - 1]] + [[m] for m in range(1, pairs - 1)]
    for step, group in enumerate(groups):
        for m in ready[step]:
            pool_far(m)
        if step:
            permute(group)
        else:
            permute(group, start=1)
            pl.semaphore_wait(barrier, seq_count - 1)

            @pl.when(has_left)
            def _():
                for copy in halo(0):
                    copy.start()

            @pl.when(has_right)
            def _():
                for copy in halo(1):
                    copy.start()

            loads[0].wait()

        for m in ready[step]:
            send_far(m)
    for m in ready[len(groups)]:
        pool_far(m)
    for m in ready[len(groups)]:
        send_far(m)
    if pairs > 2:
        pool_near(1)
    for level in us:
        sums = dot(us[level][...], kv[:, rows:])
        valid = jnp.broadcast_to(xp[2 * rows : 2 * rows + 1, :], (LANES, tokens))
        mass = dot(us[level][...], valid, ((1,), (1,)))
        fp[level][0, :, 0:rows] = fixed(sums[:, :rows] / jnp.maximum(mass, 1.0), BOUND)
        fp[level][0, :, rows:] = fixed(sums[:, rows:], BOUND * 2**level)
        for copy in far_copies(level, 0):
            copy.start()

    for m in range(2, pairs - 1):
        pool_near(m)
    permute(groups[0], stop=1)
    for m in (0, pairs - 1):
        pool_near(m)

    for i, level in enumerate(far_levels):
        pieces = max((tokens >> level) // LANES, 1)
        per = pairs // pieces
        cols = slice(i * LANES, (i + 1) * LANES)
        for j in range(pieces):
            x = sum(pf[j * per + e, :, cols] for e in range(per))
            put_query(qr[level], x, scale / 2**level, slice(j * LANES, (j + 1) * LANES))

    def far_score(km, q, slot, h, best_ref):
        s = dot(km, q)
        keys, cols = s.shape
        ss[slot, h, 0:keys, 0:cols] = s
        best = jnp.max(s.reshape(keys // 8, 8, cols), axis=0)
        best = jnp.max(best, axis=0, keepdims=True).astype(BF).astype(F32)
        best_ref[h] = jnp.broadcast_to(best, (8, cols))

    def far_soft(vvs, slot, h, best_ref, out_ref):
        cols = best_ref.shape[2]
        best = best_ref[h]
        step, acc = 0, None
        for vv in vvs:
            keys = vv.shape[1]
            x = ss[slot, h, step : step + keys, 0:cols].reshape(keys // 8, 8, cols)
            w = jnp.exp2(x - best[None]).reshape(keys, cols)
            w_hi, w_lo = split(w)
            both = dot(vv, w_hi)
            low = jnp.concatenate([both[size:], jnp.zeros((PAD, cols), F32)], axis=0)
            term = both[:size] + low + dot(vv[:size], w_lo)
            acc = term if acc is None else acc + term
            step += keys
        out_ref[h] = acc

    def local_score(i, slot, h):
        far_score(kmf[i ^ 1, h], qf[i, h], slot, h, fb.at[i])

    def local_soft(i, slot, h):
        far_soft([vvf[i ^ 1, h]], slot, h, fb.at[i], fo.at[i])

    def near_score(n, slot, h):
        at = pl.multiple_of(n * LEAF, LEAF)
        best = None
        for j in range(3):
            key_rows = pl.ds(pl.multiple_of(at + j * LEAF, LEAF), LEAF)
            left = jnp.concatenate([ka[key_rows, :], kb[h, key_rows, :]], axis=1)
            s = dot(left, qx[h, :, pl.ds(at, LEAF)])
            ss[slot, h, j * LEAF : (j + 1) * LEAF, :] = s
            top = jnp.max(s.reshape(LEAF // 8, 8, LEAF), axis=0)
            best = top if best is None else jnp.maximum(best, top)
        sb[slot, h] = jnp.broadcast_to(jnp.max(best, axis=0, keepdims=True), (8, LEAF))

    def near_soft(n, slot, h):
        at = pl.multiple_of(n * LEAF, LEAF)
        best = sb[slot, h]
        total, acc = None, None
        part = slice(h * width, (h + 1) * width)
        for j in range(3):
            x = ss[slot, h, j * LEAF : (j + 1) * LEAF, :].reshape(LEAF // 8, 8, LEAF)
            w = jnp.exp2(x - best[None])
            term = jnp.sum(w, axis=0)
            total = term if total is None else total + term
            keys = pl.ds(pl.multiple_of(at + j * LEAF, LEAF), LEAF)
            term = dot(vx[part, keys], w.reshape(LEAF, LEAF).astype(BF))
            acc = term if acc is None else acc + term
        num[part, pl.ds(at, LEAF)] = acc
        stat[2 * h : 2 * h + 1, pl.ds(at, LEAF)] = best[0:1]
        stat[2 * h + 1 : 2 * h + 2, pl.ds(at, LEAF)] = jnp.sum(total, axis=0, keepdims=True)

    def leaf_at(k):
        return jnp.where(k < leaves - 2, k + 1, jnp.where(k == leaves - 2, 0, leaves - 1))

    for h in range(heads):
        local_score(0, 0, h)
    for i in range(first):
        for h in range(heads):
            local_soft(i, i % 2, h)
            if i + 1 < first:
                local_score(i + 1, 1 - i % 2, h)
            else:
                near_score(leaf_at(0), 1 - i % 2, h)
    turn = first % 2

    @pl.loop(0, leaves // 4)
    def _(i):
        @pl.when(jnp.logical_and(i == 1, has_right))
        def _():
            for copy in halo(0):
                copy.wait_recv()

        @pl.when(jnp.logical_and(i == 1, has_left))
        def _():
            for copy in halo(1):
                copy.wait_recv()

        @pl.when(i == 1)
        def _():
            for n, at in ((-1, 0), (leaves, tokens + LEAF)):
                tail0, tail1, _ = key_tail(ka[at : at + LEAF, :].astype(F32), leaf_bias(count_of(n)))
                kb[0, at : at + LEAF, :] = tail0.astype(BF)
                kb[1, at : at + LEAF, :] = tail1.astype(BF)

        for j in range(4):
            k = 4 * i + j
            slot = (turn + j) % 2
            for h in range(heads):
                near_soft(leaf_at(k), slot, h)
                near_score(leaf_at(jnp.minimum(k + 1, leaves - 1)), 1 - slot, h)

    for level in reversed(far_levels):
        pieces = fp[level].shape[0]
        for i in range(1 << (level - depth_local)):
            for piece in range(pieces):
                remote(
                    fp[level].at[piece], fr[level].at[i, piece],
                    far_send[level].at[i * pieces + piece], far_recv[level].at[i * pieces + piece], seq,
                ).wait_recv()

    def unpack(level):
        bit = level - depth_local
        nb = 1 << bit
        base = ((seq >> bit) ^ 1) << bit
        lane = iota((PAD, LEAF), 1)
        count = jnp.zeros((PAD, LEAF), I32)
        for leaf in range(leaves * nb):
            count = jnp.where((lane << level) >> 8 == leaf, counts[base * leaves + leaf], count)
        mass = clip_mass(count, (lane << level) & (LEAF - 1), 1 << level)
        mass_col = dot(mass.astype(BF), jnp.ones((PAD, LANES), BF), ((0,), (0,)))
        bias = jnp.where(mass_col > 0, 0.0, NEG)
        got = jnp.concatenate(
            [
                fr[level][i, piece].astype(I32).astype(F32)
                for i in range(nb)
                for piece in range(fp[level].shape[0])
            ],
            axis=0,
        )
        mean = got[:, :rows] * (BOUND / STEPS)
        put_key(kmr2[level], mean, pltpu.roll(mean, width, 1), bias, slice(0, LEAF))
        put_value(vvr2[level], got[:, rows:].T * (BOUND * 2**level / STEPS), mass, slice(0, LEAF))

    for first_level in range(0, len(far_levels), 2):
        group = list(reversed(far_levels))[first_level : first_level + 2]
        for level in group:
            unpack(level)
        for slot, level in enumerate(group):
            for h in range(heads):
                far_score(kmr2[level][h], qr[level][h], slot, h, fbr[level])
        for slot, level in enumerate(group):
            for h in range(heads):
                far_soft([vvr2[level][h]], slot, h, fbr[level], for_[level])

    def up(z):
        return dot(jnp.concatenate(split(z), axis=1), uu[...])

    def with_best(acc, best):
        return jnp.concatenate([acc[: size - 8], jnp.broadcast_to(best, (8, acc.shape[1]))], axis=0)

    def merge(acc, best, z):
        old = z[size - 8 : size - 7]
        new = jnp.maximum(best, old)
        both = acc * jnp.exp2(best - new) + z * jnp.exp2(old - new)
        return with_best(both, new)

    def tiles(z):
        return [z[:, j * LANES : (j + 1) * LANES] for j in range(z.shape[1] // LANES)]

    zs = [None] * heads
    for level in reversed(far_levels):
        for h in range(heads):
            acc, best = for_[level][h], fbr[level][h, 0:1]
            if zs[h] is None:
                zs[h] = with_best(acc, best)
            else:
                z = jnp.concatenate([up(x) for x in tiles(zs[h])], axis=1)
                zs[h] = merge(acc, best, z[:, : acc.shape[1]])
    zs = [None if z is None else tiles(z) for z in zs]
    for level in reversed(near_levels):
        new = [[] for _ in range(heads)]
        for i in range(leaves >> level):
            for h in range(heads):
                block = base_of[level] + i
                acc, best = fo[block, h], fb[block, h, 0:1]
                x = with_best(acc, best) if zs[h] is None else merge(acc, best, up(zs[h][i]))
                for j, part in enumerate(tiles(x)):
                    zb[level % 2, h, 2 * i + j] = part
                    new[h].append(zb.at[level % 2, h, 2 * i + j])
        zs = [[ref[...] for ref in refs_h] for refs_h in new]
    for n in range(leaves):
        for h in range(heads):
            cols = slice(n * LEAF, (n + 1) * LEAF)
            part = slice(h * width, (h + 1) * width)
            near_best, near_total = stat[2 * h : 2 * h + 1, cols], stat[2 * h + 1 : 2 * h + 2, cols]
            z = up(zs[h][n])
            old = z[size - 8 : size - 7]
            new_best = jnp.maximum(near_best, old)
            mine, other = jnp.exp2(near_best - new_best), jnp.exp2(old - new_best)
            inverse = 1.0 / (near_total * mine + z[width : width + 1] * other)
            out[part, cols] = (num[part, cols] * (mine * inverse) + z[:width] * (other * inverse)).astype(BF)

    @pl.when(has_left)
    def _():
        for copy in halo(0):
            copy.wait_send()

    @pl.when(has_right)
    def _():
        for copy in halo(1):
            copy.wait_send()

    for level in far_levels:
        for piece in range(fp[level].shape[0]):
            for copy in far_copies(level, piece):
                copy.wait_send()


def shards(q_heads, k_heads, v_heads, morton_order, leaf_counts):
    heads_real, width, tokens = q_heads.shape
    heads = heads_real + heads_real % 2
    seq_count = lax.axis_size("seq")
    rows = heads * width
    flat = []
    for x in (q_heads, k_heads, v_heads):
        if heads != heads_real:
            x = jnp.concatenate([x, jnp.zeros_like(x[:1])], axis=0)
        flat.append(x.reshape(rows, tokens))
    leaves, depth_local, near_levels, far_levels = plan(tokens, seq_count)
    size = width + PAD
    near_blocks = sum(leaves >> l for l in near_levels)
    pieced = [l for l in far_levels if (LEAF >> l) >= 8]
    unit_rows = lambda which: max(sum(max(LEAF >> l, 16) for l in which), 16)
    pieces = lambda l: leaves // 2 if l in pieced else 1
    vm = pltpu.VMEM
    scratch = [
        vm(morton_order.shape, I32),
        pltpu.SMEM(leaf_counts.shape, I32),
        vm((3 * rows, tokens), BF),
        vm((tokens + 2 * LEAF, rows), BF),
        vm((heads, tokens + 2 * LEAF, LANES), BF),
        vm((rows, tokens + 2 * LEAF), BF),
        vm((heads, 4 * width, tokens), BF),
        vm((2 * rows + PAD, tokens), BF),
        vm((tokens, 3 * rows), BF),
        vm((2, LEAF, LEAF), BF),
        vm((leaves // 2, 2 * LEAF, LANES * len(far_levels)), BF),
        vm((unit_rows(near_levels), LEAF), BF),
        vm((unit_rows(pieced), LEAF), BF),
        vm((LEAF, LEAF), BF),
        vm((near_blocks, heads, 4 * width, LEAF), BF),
        vm((near_blocks, heads, LEAF, 2 * rows), BF),
        vm((near_blocks, heads, size + width, LEAF), BF),
        vm((near_blocks, heads, size, LEAF), F32),
        vm((near_blocks, heads, 8, LEAF), F32),
        vm((leaves // 2, rows, LANES * len(far_levels)), F32),
        vm((2, heads, 3 * LEAF, LEAF), F32),
        vm((2, heads, 8, LEAF), F32),
        vm((rows, tokens), F32),
        vm((2 * heads + (-2 * heads) % 8, tokens), F32),
        vm((2, heads, leaves, size, LANES), F32),
    ]
    scratch += [vm((heads, 4 * width, padded(tokens, l)), BF) for l in far_levels]
    scratch += [vm((heads, LEAF, 2 * rows), BF) for l in far_levels]
    scratch += [vm((heads, size + width, LEAF), BF) for l in far_levels]
    scratch += [vm((heads, size, padded(tokens, l)), F32) for l in far_levels]
    scratch += [vm((heads, 8, padded(tokens, l)), F32) for l in far_levels]
    sent = lambda l: (pieces(l), (tokens >> l) // pieces(l), 2 * rows)
    scratch += [vm(sent(l), I16) for l in far_levels]
    scratch += [vm((1 << (l - depth_local), *sent(l)), I16) for l in far_levels]
    sem = pltpu.SemaphoreType.DMA
    scratch += [sem((5,)), sem((4,)), sem((4,))]
    scratch += [sem((pieces(l) << (l - depth_local),)) for l in far_levels] * 2
    scratch += [vm((tokens >> l, tokens), BF) for l in far_levels if (LEAF >> l) < 8]
    out = pl.pallas_call(
        functools.partial(kernel, (heads, width, tokens, seq_count)),
        out_shape=pltpu.VMEM((rows, tokens), BF),
        in_specs=[pl.BlockSpec(memory_space=pltpu.HBM)] * 5,
        out_specs=pl.BlockSpec(memory_space=pltpu.VMEM),
        scratch_shapes=scratch,
        compiler_params=pltpu.CompilerParams(
            collective_id=0, has_side_effects=True, vmem_limit_bytes=VMEM_LIMIT
        ),
    )(*flat, morton_order, leaf_counts)
    return out.reshape(heads, width, tokens)[:heads_real]


def solution(mesh):
    placed = (
        P("head", None, ("grp", "seq")),
        P("head", None, ("grp", "seq")),
        P("head", None, ("grp", "seq")),
        P(("grp", "seq"), None),
        P("grp"),
    )
    return jax.shard_map(
        shards,
        mesh=mesh,
        in_specs=placed,
        out_specs=P("head", None, ("grp", "seq")),
        check_vma=False,
    )
```
